128 devices in a mesh: gx: 16 (over y, x), gy: 8 (over z, core).
Axes of the slice: x: 4, y: 4, z: 4, core: 2. Of those that a mesh axis runs over, the one named last changes fastest.
Arguments:
- state: float32 [128, 256, 2048], P('gx', 'gy'), may hold values from -6 to 6
- wind_x: float32 [128, 256, 64], P('gx', 'gy'), may hold values from -4 to 4
- wind_y: float32 [128, 256, 64], P('gx', 'gy'), may hold values from -4 to 4
- mass: float32 [128, 256], P('gx', 'gy'), may hold values from 0.3 to 1
- inv_mass: float32 [128, 256], P('gx', 'gy'), may hold values from 0.4 to 1.5
- span_of: int32 [18432, 1], P(('gx', 'gy')), may hold values from 0 to 127; in each aligned block of 144 rows (0 to 143, 144 to 287, ...) at most 2 rows name the same one
- block_inverse: float32 [32768, 1024], P(('gx', 'gy')), may hold values from -1 to 1, as said below
- coupling: float32 [32768, 3], P(('gx', 'gy')), may hold values from 0.15 to 0.45
Outputs:
- new_columns: float32 [18432, 2048], P(('gx', 'gy'))
The draws below stay inside these ranges and needn't reach their ends.
Inputs may be any that keep to these rules, and one draw needn't show every extreme that they name: `span_of`: from the columns of one device at most 2 go to one span, and some span receives exactly 2 of them. `block_inverse`: each block is a matrix with a diagonal between 0.6 and 1.0 and independent off-diagonal entries.
All inputs are finite; a program needn't handle non-finite values.
Results may differ from the reference program's by a relative error of at most 0.0001.
Values sent between devices are 32-bit elements; how exact they have to be, the bound alone decides.
A program may use at most 128 MiB of HBM per device.

```python
import math
import jax
import jax.numpy as jnp
import numpy as np
from jax import lax

EX = 2
EY = 8
NP = 4
L = 64
TR = 32
NB = 4
SWEEPS = 3
B = 16
C_DEV = 144
COLUMNS = 18432
CAP = 2
SLOTS = 32768
NXN = 128
NYN = 256
N_GX = 16
N_GY = 8
DEVICES = 128


def draw_block_inverse(key, part):
    key = jax.random.fold_in(key, 7)
    first, second = jax.random.split(key)
    diagonal = jax.random.uniform(first, (SLOTS, NB, B), jnp.float32, 0.6, 1.0)
    spread = 0.125 * jnp.clip(jax.random.normal(second, (SLOTS, NB, B, B), jnp.float32), -1.7, 1.7)
    rowpos = lax.broadcasted_iota(jnp.int32, (B, B), 0)
    colpos = lax.broadcasted_iota(jnp.int32, (B, B), 1)
    identity = (rowpos == colpos).astype(jnp.float32)
    blocks = spread * (1.0 - identity) + identity * diagonal[..., None]
    return blocks.reshape(SLOTS, NB * B * B)


def block_scale(key, dims, pieces, low, largest):
    def one(axis_at, blocks):
        heights = jax.random.uniform(jax.random.fold_in(jax.random.fold_in(key, 6), axis_at), (blocks,), jnp.float32, low / len(pieces), largest / len(pieces))
        return jnp.repeat(jnp.exp(heights), dims[axis_at] // blocks).reshape((-1,) + (1,) * (len(dims) - axis_at - 1))

    level = one(*pieces[0])
    for cut in pieces[1:]:
        level = level * one(*cut)
    return level


def assign_block(key, own, number, rows, amount, top, limit, skew):
    ranking = jax.random.permutation(key, amount)
    heavy_load, common = shares(amount, rows * top, limit, skew, True), shares(amount, rows * top, limit, skew, False)
    places = jnp.arange(amount)

    def named(lengths, rotation):
        used = int((lengths > 0).sum())
        fixed = max(1, used // 4)
        passed = fixed + (places - fixed + rotation * (used - fixed)) % max(1, amount - fixed)
        return jnp.zeros((amount,), jnp.int32).at[ranking[jnp.where(places < fixed, places, passed)]].set(jnp.asarray(lengths, jnp.int32))

    lengths = jnp.where(number % 4 == 0, named(heavy_load, number // 4), named(common, number - number // 4 - 1))
    mixed = jax.random.permutation(jax.random.fold_in(own, 3), amount)
    giver, sink = mixed[0:amount // 2 * 2:2], mixed[1:amount // 2 * 2:2]
    room = jnp.minimum(lengths[giver] - 1, limit - lengths[sink]) // 2
    room = jnp.where((giver == ranking[0]) | (sink == ranking[0]) | (lengths[sink] == 0), 0, jnp.maximum(room, 0))
    passed = jax.random.randint(jax.random.fold_in(own, 4), (amount // 2,), 0, 1 << 20) % (room + 1)
    lengths = lengths.at[giver].add(-passed).at[sink].add(passed)
    members = jnp.searchsorted(jnp.cumsum(lengths), jnp.arange(rows * top), side="right").astype(jnp.int32)
    table = members.reshape(top, rows).T
    table = table[jax.random.permutation(jax.random.fold_in(own, 1), rows)]
    rotation = jax.random.randint(jax.random.fold_in(own, 2), (rows, 1), 0, top)
    return jnp.take_along_axis(table, (jnp.arange(top)[None, :] + rotation) % top, axis=1)


def shares(number_of, total, bound, lean, full):
    loads = [(1 << 20) // math.isqrt(standing ** lean) + 1 for standing in range(1, number_of + 1)]
    largest = bound if full else min(bound, max(-(-total // number_of), total * loads[0] // sum(loads)))
    least = 1 if total - largest >= number_of - 1 else 0
    counts, surplus = [largest] + [least] * (number_of - 1), total - largest - least * (number_of - 1)
    while surplus > 0:
        candidates = [i for i in range(1, number_of) if counts[i] < largest] or [i for i in range(1, number_of) if counts[i] < bound]
        pool, budget = sum([loads[i] for i in candidates]), surplus
        for i in candidates:
            more = min(bound - counts[i], max(1, budget * loads[i] // pool), surplus)
            counts[i] = counts[i] + more
            surplus = surplus - more
    return np.array(counts)


def bell_draw(own_key, shape, scale, bound, cuts=(), held_as=jnp.bfloat16):
    drawn = jax.random.normal(own_key, shape, jnp.float32) * scale
    if len(cuts) > 0:
        drawn = block_scale(own_key, shape, cuts, -0.22, 0.18) * drawn
    return jnp.clip(drawn, min=-bound, max=bound).astype(held_as)


def setup_inputs(seed: int = 0) -> dict:
    keys = jax.random.split(jax.random.key(seed), 9)
    state = bell_draw(keys[0], (NXN, NYN, L * TR), 1.0, 6.0, ((0, 16), (1, 8)), jnp.float32)
    wind_x = bell_draw(keys[1], (NXN, NYN, L), 1.0, 4.0, ((0, 16), (1, 8)), jnp.float32)
    wind_y = bell_draw(keys[2], (NXN, NYN, L), 1.0, 4.0, ((0, 16), (1, 8)), jnp.float32)
    mass = jnp.clip(jnp.exp(math.log(1.0) - 1.2039728 * jax.random.uniform(keys[3], (NXN, NYN), jnp.float32) ** block_scale(keys[3], (NXN, NYN), ((0, 16), (1, 8)), -0.2, 0.2)), 0.3, 1.0)
    inv_mass = jnp.clip(jnp.exp(math.log(1.5) - 1.3217558 * jax.random.uniform(keys[4], (NXN, NYN), jnp.float32) ** block_scale(keys[4], (NXN, NYN), ((0, 16), (1, 8)), -0.2, 0.2)), 0.4, 1.5)
    span_of_keys = jax.random.split(jax.random.fold_in(keys[5], 1), COLUMNS // C_DEV)
    span_of_turns = jax.random.permutation(jax.random.fold_in(keys[5], 3), COLUMNS // C_DEV)
    span_of = jax.vmap(lambda own, number: assign_block(jax.random.fold_in(keys[5], 2), own, number, C_DEV, DEVICES, 1, CAP, 0))(span_of_keys, span_of_turns).reshape((COLUMNS, 1))
    block_inverse = draw_block_inverse(jax.random.fold_in(keys[8], 71), 0)
    coupling = jnp.clip(0.15 + 0.29999998 * jax.random.uniform(keys[7], (SLOTS, NB - 1), jnp.float32) ** block_scale(keys[7], (SLOTS, NB - 1), ((0, 128),), -0.2, 0.2), 0.15, 0.45)
    return {"state": state, "wind_x": wind_x, "wind_y": wind_y, "mass": mass, "inv_mass": inv_mass, "span_of": span_of, "block_inverse": block_inverse, "coupling": coupling}


HIGH = lax.Precision.HIGHEST
STEP = 0.05

def derivative_table():
    points = np.array([-1.0, -1.0 / np.sqrt(5.0), 1.0 / np.sqrt(5.0), 1.0])
    count = points.shape[0]
    weights = np.ones(count)
    for i in range(count):
        for m in range(count):
            if m != i:
                weights[i] = weights[i] * (points[i] - points[m])
    table = np.zeros((count, count))
    for i in range(count):
        for j in range(count):
            if i != j:
                table[i, j] = weights[i] / weights[j] / (points[i] - points[j])
                table[i, i] = table[i, i] + 1.0 / (points[i] - points[j])
    return table

def tendency(field, wind_x, wind_y, table):
    rows, cols, width = field.shape
    levels = wind_x.shape[2]
    first = field.reshape(rows // NP, NP, cols, width)
    along_x = jnp.einsum('ik,ekyc->eiyc', table, first, precision=HIGH).reshape(rows, cols, levels, width // levels)
    second = field.reshape(rows, cols // NP, NP, width)
    along_y = jnp.einsum('jk,xekc->xejc', table, second, precision=HIGH).reshape(rows, cols, levels, width // levels)
    flow = wind_x[..., None] * along_x + wind_y[..., None] * along_y
    return -flow.reshape(rows, cols, width)

def edge_sum(weighted):
    place = (jnp.arange(weighted.shape[0]) % NP)[:, None, None]
    along = weighted + jnp.where(place == NP - 1, jnp.roll(weighted, -1, 0), jnp.where(place == 0, jnp.roll(weighted, 1, 0), 0.0))
    place = (jnp.arange(weighted.shape[1]) % NP)[None, :, None]
    return along + jnp.where(place == NP - 1, jnp.roll(along, -1, 1), jnp.where(place == 0, jnp.roll(along, 1, 1), 0.0))

def diffuse(values, inverse, coupling, levels):
    count, width = values.shape
    tracers = width // levels
    depth = levels // NB
    source = values.reshape(count, NB, depth, tracers)
    blocks = inverse.reshape(count, NB, depth, depth)
    result = jnp.einsum('snab,snbt->snat', blocks, source, precision=HIGH)
    for sweep in range(SWEEPS):
        upper = jnp.pad(coupling[:, :, None] * result[:, 1:, 0, :], ((0, 0), (0, 1), (0, 0)))
        lower = jnp.pad(coupling[:, :, None] * result[:, :-1, depth - 1, :], ((0, 0), (1, 0), (0, 0)))
        forced = source.at[:, :, depth - 1, :].add(upper).at[:, :, 0, :].add(lower)
        result = jnp.einsum('snab,snbt->snat', blocks, forced, precision=HIGH)
    return (result - source).reshape(count, width)

def reference(state, wind_x, wind_y, mass, inv_mass, span_of, block_inverse, coupling):
    table = jnp.asarray(derivative_table(), jnp.float32)

    def operator(field):
        weighted = mass[..., None] * tendency(field, wind_x, wind_y, table)
        return inv_mass[..., None] * edge_sum(weighted)
    first = state + STEP * operator(state)
    second = 0.75 * state + 0.25 * (first + STEP * operator(first))
    final = state / 3.0 + 2.0 / 3.0 * (second + STEP * operator(second))
    width = state.shape[2]
    devices = N_GX * N_GY
    grid = final.reshape(N_GX, EX, NP, N_GY, EY, NP, width)[:, :, :NP - 1, :, :, :NP - 1]
    columns = grid.transpose(0, 3, 1, 2, 4, 5, 6).reshape(COLUMNS, width)
    target = span_of[:, 0].astype(jnp.int32)
    grouped = target.reshape(devices, C_DEV)
    onehot = (grouped[:, :, None] == jnp.arange(devices, dtype=jnp.int32)[None, None, :]).astype(jnp.int32)
    rank = lax.optimization_barrier(jnp.sum((jnp.cumsum(onehot, 1) - 1) * onehot, 2)).reshape(COLUMNS)
    owner = (jnp.arange(COLUMNS, dtype=jnp.int32) // C_DEV).astype(jnp.int32)
    slot = (target * (devices * CAP) + owner * CAP + rank).astype(jnp.int32)
    change = diffuse(columns, block_inverse[slot], coupling[slot], wind_x.shape[2])
    return columns + change
```

```python
import functools

import jax
import jax.numpy as jnp
import numpy as np
from jax import lax
from jax.experimental import pallas as pl
from jax.experimental.pallas import tpu as pltpu
from jax.sharding import PartitionSpec as P

NP = 4
NB = 4
SWEEPS = 3
STEP = 0.05
EX = 2
EY = 8
NX = EX * NP
NY = EY * NP
UX = EX * 3 + 1
UY = EY * 3 + 1
COLS = EX * 3 * EY * 3
MESH = pl.DeviceIdType.MESH
F32 = jnp.float32
BF16 = jnp.bfloat16


def derivative_table():
    points = np.array([-1.0, -1.0 / np.sqrt(5.0), 1.0 / np.sqrt(5.0), 1.0])
    count = points.shape[0]
    weights = np.ones(count)
    for i in range(count):
        for m in range(count):
            if m != i:
                weights[i] = weights[i] * (points[i] - points[m])
    table = np.zeros((count, count))
    for i in range(count):
        for j in range(count):
            if i != j:
                table[i, j] = weights[i] / weights[j] / (points[i] - points[j])
                table[i, i] = table[i, i] + 1.0 / (points[i] - points[j])
    return table


TABLE = derivative_table()
ODD = [float((TABLE[i, 0] + TABLE[i, 3]) / 2) for i in range(2)]
EVEN = [[float((TABLE[i, k] - TABLE[i, 3 - k]) / 2) for k in range(2)] for i in range(2)]


def derivative(q):
    outer, inner = q[0] - q[3], q[1] - q[2]
    bend = (q[0] + q[3]) - (q[1] + q[2])
    odd = [ODD[i] * bend for i in range(2)]
    even = [EVEN[i][0] * outer + EVEN[i][1] * inner for i in range(2)]
    return [even[0] + odd[0], even[1] + odd[1], even[1] - odd[1], even[0] - odd[0]]


def lane_group(shape):
    return lax.broadcasted_iota(jnp.int32, shape, 1) // 32


def spread(v):
    group = lane_group(v.shape)
    low, even = group < 2, group % 2 == 0
    turned = pltpu.roll(v, 64, 1)
    result = []
    for pair in (jnp.where(low, v, turned), jnp.where(low, turned, v)):
        swapped = pltpu.roll(pair, 32, 1)
        result += [jnp.where(even, pair, swapped), jnp.where(even, swapped, pair)]
    return result


def collect(tiles, source):
    group = lane_group(tiles[0].shape)
    result = None
    for b, tile in enumerate(tiles):
        shift = (b - source) % 4 * 32
        moved = pltpu.roll(tile, shift, 1) if shift else tile
        result = moved if result is None else jnp.where(group == b, moved, result)
    return result


def two_parts(x):
    high = x.astype(BF16)
    return high, (x - high.astype(F32)).astype(BF16)


def kernel(ngx, ngy, state, wind_x, wind_y, mass, inv_mass, span_of, inverse, coupling, out,
           raw, raw_wx, raw_wy, raw_span, raw_inv, raw_coup, st, fld, wxe, wye, grid, sx, sy, rx, ry, rc, fin,
           p0, p1, p2s, p2r, picks, pairs, hot, wide, edges, kup, klo, result,
           load_sem, out_sem, hs, hr, p1s_sem, p1r_sem, p2s_sem, p2r_sem):
    gx, gy = lax.axis_index("gx"), lax.axis_index("gy")
    devices = ngx * ngy

    loads = [
        pltpu.make_async_copy(src, dst, load_sem.at[n])
        for n, (src, dst) in enumerate((
            (wind_x, raw_wx), (wind_y, raw_wy), (state, raw), (inverse, raw_inv), (coupling, raw_coup), (span_of, raw_span)))
    ]
    for load in loads:
        load.start()

    barrier = pltpu.get_barrier_semaphore()

    def at(dx, dy):
        return (lax.rem(gx + (dx + ngx), ngx), lax.rem(gy + (dy + ngy), ngy))

    for d in range(1, ngy):
        pl.semaphore_signal(barrier, inc=1, device_id=at(0, d), device_id_type=MESH)
    for d in range(1, ngx):
        pl.semaphore_signal(barrier, inc=1, device_id=at(d, 0), device_id_type=MESH)
    for dx in (-1, 1):
        for dy in (-1, 1):
            pl.semaphore_signal(barrier, inc=1, device_id=at(dx, dy), device_id_type=MESH)

    per_gy = ngx * 16
    loads[3].wait()
    loads[4].wait()

    def pack(sx_, carry):
        for four in range(ngy // 4):
            rows = pl.ds(pl.multiple_of(sx_ * (2 * ngy) + four * 8, 8), 8)
            block = raw_inv[rows, :].reshape(8, 8, 128)
            for r in range(8):
                p0[four * 4 + r // 2, pl.ds(pl.multiple_of(sx_ * 16 + r % 2 * 8, 8), 8), :] = block[r]
        return carry

    lax.fori_loop(0, ngx, pack, 0)
    place = lax.broadcasted_iota(jnp.int32, (3, 128), 0)
    lane = lax.broadcasted_iota(jnp.int32, (3, 128), 1)
    both = sum(
        jnp.dot(raw_coup[pl.ds(r, devices, stride=2), :], (lane == place + 3 * r).astype(F32),
                preferred_element_type=F32, precision=lax.Precision.HIGHEST)
        for r in range(2)
    )
    both3 = both.reshape(ngx, ngy, 128)
    for s in range(ngy):
        p0[s, per_gy:, :] = both3[:, s, :]

    pl.semaphore_wait(barrier, ngy - 1 + ngx - 1 + 4)

    def phase1(d):
        return pltpu.make_async_remote_copy(
            src_ref=p0.at[lax.rem(gy + d, ngy)], dst_ref=p1.at[gy],
            send_sem=p1s_sem.at[d], recv_sem=p1r_sem.at[d],
            device_id=at(0, d), device_id_type=MESH)

    def phase2(d):
        return pltpu.make_async_remote_copy(
            src_ref=p2s.at[lax.rem(gx + d, ngx)], dst_ref=p2r.at[gx],
            send_sem=p2s_sem.at[d], recv_sem=p2r_sem.at[d],
            device_id=at(d, 0), device_id_type=MESH)

    for d in range(1, ngy):
        phase1(d).start()
    p1[gy] = p0[gy]

    loads[0].wait()
    loads[1].wait()
    level = lax.rem(lax.broadcasted_iota(jnp.int32, (128, 128), 0), 64)
    target = lax.broadcasted_iota(jnp.int32, (128, 128), 1) // 32
    for raw_w, wide_w in ((raw_wx, wxe), (raw_wy, wye)):
        w = raw_w[...].reshape(NX * NY, 64)
        high = w.astype(BF16).astype(F32)
        parts = jnp.concatenate([high, w - high], axis=1).astype(BF16)
        for i in range(16):
            spreader = (level == target + 4 * i).astype(BF16)
            value = jnp.dot(parts, spreader, preferred_element_type=F32)
            wide_w[i // 8, pl.ds(i % 8, NX * NY, stride=8), :] = value

    loads[2].wait()

    def turn(n, carry):
        x, y8 = n // (NY // 8), lax.rem(n, NY // 8)
        for h in range(2):
            block = raw[x, pl.ds(pl.multiple_of(y8 * 8, 8), 8), 1024 * h:1024 * (h + 1)]
            st[h, x, pl.ds(y8 * 8, 8)] = block.reshape(8, 8, 128)
        return carry

    lax.fori_loop(0, NX * NY // 8, turn, 0)

    def weighted(h, k, field):
        def body(ey, carry):
            lines = []
            for ex in range(EX):
                f = [[field(h, ex * NP + i, ey, j) for j in range(NP)] for i in range(NP)]
                along_x = [derivative([f[i][j] for i in range(NP)]) for j in range(NP)]
                along_y = [derivative(f[i]) for i in range(NP)]
                w = []
                for i in range(NP):
                    row = []
                    for j in range(NP):
                        x, y = ex * NP + i, ey * NP + j
                        node = pl.ds(pl.multiple_of((x * NY + y) * 8, 8), 8)
                        flow = wxe[h, node, :] * along_x[j][i] + wye[h, node, :] * along_y[i][j]
                        row.append(mass[x, y] * flow)
                    w.append(row)
                if lines:
                    lines[-1] = [a + b for a, b in zip(lines[-1], w[0])]
                    lines += w[1:]
                else:
                    lines = w
            for X in range(UX):
                values = [carry[X] + lines[X][0], lines[X][1], lines[X][2]]
                for j in range(3):
                    grid[k % 2, h, X, ey * 3 + j] = values[j]
                    if X == 0:
                        sx[k, h, 0, ey * 3 + j] = values[j]
                    if X == UX - 1:
                        sx[k, h, 1, ey * 3 + j] = values[j]
            return tuple(lines[X][3] for X in range(UX))

        carry = lax.fori_loop(0, EY, body, (jnp.zeros((8, 128), F32),) * UX)
        for X in range(UX):
            grid[k % 2, h, X, UY - 1] = carry[X]
            sy[k, h, 1, X] = carry[X]
            sy[k, h, 0, X] = grid[k % 2, h, X, 0]
        sx[k, h, 0, UY - 1] = carry[0]
        sx[k, h, 1, UY - 1] = carry[UX - 1]

    def halo(h, k):
        if k < 2:
            moves = [
                (sx.at[k, h, 1], rx.at[k, h, 0], (1, 0)),
                (sx.at[k, h, 0], rx.at[k, h, 1], (-1, 0)),
                (sy.at[k, h, 1], ry.at[k, h, 0], (0, 1)),
                (sy.at[k, h, 0], ry.at[k, h, 1], (0, -1)),
                (sx.at[k, h, 1, UY - 1], rc.at[k, h, 0], (1, 1)),
                (sx.at[k, h, 1, 0], rc.at[k, h, 1], (1, -1)),
                (sx.at[k, h, 0, UY - 1], rc.at[k, h, 2], (-1, 1)),
                (sx.at[k, h, 0, 0], rc.at[k, h, 3], (-1, -1)),
            ]
        else:
            moves = [
                (sx.at[k, h, 1, pl.ds(0, UY - 1)], rx.at[k, h, 0, pl.ds(0, UY - 1)], (1, 0)),
                (sy.at[k, h, 1, pl.ds(0, UX - 1)], ry.at[k, h, 0, pl.ds(0, UX - 1)], (0, 1)),
                (sx.at[k, h, 1, UY - 1], rc.at[k, h, 0], (1, 1)),
            ]
        return [
            pltpu.make_async_remote_copy(
                src_ref=src, dst_ref=dst, send_sem=hs.at[k, h, n], recv_sem=hr.at[k, h, n],
                device_id=at(*offset), device_id_type=MESH)
            for n, (src, dst, offset) in enumerate(moves)
        ]

    def arrive(h, k):
        for move in halo(h, k):
            move.wait_recv()
        g = grid.at[k % 2, h]
        if k < 2:
            g[0] += rx[k, h, 0]
            g[UX - 1] += rx[k, h, 1]
            g[:, 0] += ry[k, h, 0]
            g[:, UY - 1] += ry[k, h, 1]
            g[0, 0] += rc[k, h, 0]
            g[0, UY - 1] += rc[k, h, 1]
            g[UX - 1, 0] += rc[k, h, 2]
            g[UX - 1, UY - 1] += rc[k, h, 3]
        else:
            g[0, 0:UY - 1] += rx[k, h, 0, 0:UY - 1]
            g[0:UX - 1, 0] += ry[k, h, 0, 0:UX - 1]
            g[0, 0] += rc[k, h, 0]

    def edge(h, k, x, ey, j):
        return grid[k % 2, h, x - x // NP, ey * 3 + j]

    def initial(h, x, ey, j):
        return st[h, x, ey * NP + j]

    def first(h, x, ey, j):
        y = ey * NP + j
        value = st[h, x, y] - (STEP * inv_mass[x, y]) * edge(h, 0, x, ey, j)
        fld[h, x, y] = value
        return value

    def second(h, x, ey, j):
        y = ey * NP + j
        value = 0.75 * st[h, x, y] + 0.25 * fld[h, x, y] - (0.25 * STEP * inv_mass[x, y]) * edge(h, 1, x, ey, j)
        fld[h, x, y] = value
        return value

    def final(h):
        def body(ey, carry):
            for ex in range(EX):
                for i in range(3):
                    for j in range(3):
                        x, y = ex * NP + i, ey * NP + j
                        value = (1.0 / 3.0) * st[h, x, y] + (2.0 / 3.0) * fld[h, x, y]
                        value = value - (2.0 / 3.0 * STEP * inv_mass[x, y]) * edge(h, 2, x, ey, j)
                        row = ((ex * 3 + i) * EY + ey) * 3 + j
                        fin[h, pl.ds(pl.multiple_of(row * 8, 8), 8), :] = value
            return carry

        lax.fori_loop(0, EY, body, 0)

    for h in range(2):
        weighted(h, 0, initial)
        for move in halo(h, 0):
            move.start()

    for d in range(1, ngy):
        phase1(d).wait_recv()

    def repack(s, carry):
        for g in range(ngy):
            p2s[s, g * 16:(g + 1) * 16, :] = p1[g, pl.ds(pl.multiple_of(s * 16, 8), 16), :]
            p2s[s, ngy * 16 + g:ngy * 16 + g + 1, :] = p1[g, pl.ds(per_gy + s, 1), :]
        return carry

    lax.fori_loop(0, ngx, repack, 0)
    for d in range(1, ngx):
        phase2(d).start()
    p2r[gx] = p2s[gx]

    loads[5].wait()
    named = (raw_span[...] == lax.broadcasted_iota(jnp.int32, (COLS, devices), 1)).astype(F32)
    earlier = (lax.broadcasted_iota(jnp.int32, (COLS, COLS), 1) < lax.broadcasted_iota(jnp.int32, (COLS, COLS), 0)).astype(BF16)
    count = jnp.dot(earlier, named.astype(BF16), preferred_element_type=F32)
    picks[:, :devices] = jnp.where(count < 0.5, named, 0.0).astype(BF16)
    picks[:, devices:] = jnp.where(count < 0.5, 0.0, named).astype(BF16)

    entry = lax.rem(lax.broadcasted_iota(jnp.int32, (256, 128), 0), 128)
    group = lax.broadcasted_iota(jnp.int32, (256, 128), 1) // 32

    def build(b, carry):
        for e in range(2):
            hot[e, :, pl.ds(pl.multiple_of(b * 128, 128), 128)] = (entry == e * 64 + group * 16 + b).astype(F32).astype(BF16)
        return carry

    lax.fori_loop(0, 16, build, 0)

    for h in range(2):
        arrive(h, 0)
        weighted(h, 1, first)
        for move in halo(h, 1):
            move.start()
    for h in range(2):
        arrive(h, 1)
        weighted(h, 2, second)
        for move in halo(h, 2):
            move.start()

    for d in range(1, ngx):
        phase2(d).wait_recv()

    def gather(j, carry):
        slots = jnp.concatenate([
            p2r[g, pl.ds(r * 8 + j, ngy, stride=16), :] for r in range(2) for g in range(ngx)], axis=0)
        chosen = [jnp.dot(picks[...], part, preferred_element_type=F32).astype(BF16) for part in two_parts(slots)]
        pairs[j] = jnp.concatenate(chosen, axis=1)
        return carry

    lax.fori_loop(0, 8, gather, 0)

    def widen(n, carry):
        j, part = n // 8, lax.rem(n, 8)
        lanes = pl.ds(pl.multiple_of(part * 256, 256), 256)
        for e in range(2):
            wide[e, j, :, lanes] = jnp.dot(pairs[j], hot[e, :, lanes], preferred_element_type=F32)
        return carry

    lax.fori_loop(0, 64, widen, 0)

    links = jnp.concatenate([p2r[g, ngy * 16:ngy * 16 + ngy, :] for g in range(ngx)], axis=0)
    row = lax.broadcasted_iota(jnp.int32, (128, 128), 0)
    col = lax.broadcasted_iota(jnp.int32, (128, 128), 1) // 32
    hi = functools.partial(jnp.dot, preferred_element_type=F32, precision=lax.Precision.HIGHEST)
    up, down = 0.0, 0.0
    for r in range(2):
        mine = hi(picks[:, r * devices:(r + 1) * devices].astype(F32), links)
        up = up + hi(mine, ((row == col + 3 * r) & (col < 3)).astype(F32))
        down = down + hi(mine, ((row == col - 1 + 3 * r) & (col > 0)).astype(F32))
    kup[...] = up
    klo[...] = down

    def corners(cg, carry):
        rows = pl.ds(pl.multiple_of(cg * 8, 8), 8)
        for n, (e, more, b, source) in enumerate(((0, 0, 0, 0), (0, 0, 15, 0), (1, 1, 0, 3), (1, 1, 15, 3))):
            edges[n, rows, :] = collect(
                [wide[e, 2 * blk + more, rows, b * 128:(b + 1) * 128] for blk in range(NB)], source)
        return carry

    lax.fori_loop(0, COLS // 8, corners, 0)

    for h in range(2):
        arrive(h, 2)
        final(h)

        def base(cg, carry):
            rows = pl.ds(pl.multiple_of(cg * 8, 8), 8)
            for blk in (2 * h, 2 * h + 1):
                total = [None] * 4
                for tile in range(4):
                    s = blk % 2 * 4 + tile
                    values = spread(fin[h, pl.ds(cg * 64 + s, 8, stride=8), :])
                    for g in range(4):
                        b = tile * 4 + g
                        for i in range(4):
                            term = wide[i % 2, 2 * blk + i // 2, rows, b * 128:(b + 1) * 128] * values[g]
                            total[i] = term if total[i] is None else total[i] + term
                for i in range(4):
                    result[rows, (4 * blk + i) * 128:(4 * blk + i + 1) * 128] = total[i]
            return carry

        lax.fori_loop(0, COLS // 8, base, 0)

    def sweep(cg, carry):
        rows = pl.ds(pl.multiple_of(cg * 8, 8), 8)
        head = collect([result[rows, 4 * b * 128:(4 * b + 1) * 128] for b in range(NB)], 0)
        tail = collect([result[rows, (4 * b + 3) * 128:(4 * b + 4) * 128] for b in range(NB)], 3)
        now_head, now_tail = head, tail
        for n in range(SWEEPS):
            upper = kup[rows, :] * pltpu.roll(now_head, 96, 1)
            lower = klo[rows, :] * pltpu.roll(now_tail, 32, 1)
            if n < SWEEPS - 1:
                now_head = head + edges[1, rows, :] * upper + edges[0, rows, :] * lower
                now_tail = tail + edges[3, rows, :] * upper + edges[2, rows, :] * lower
        uppers, lowers = spread(upper), spread(lower)
        for blk in range(NB):
            for i in range(4):
                lanes = slice((4 * blk + i) * 128, (4 * blk + i + 1) * 128)
                e, j = i % 2, 2 * blk + i // 2
                result[rows, lanes] += (
                    wide[e, j, rows, 15 * 128:] * uppers[blk] + wide[e, j, rows, :128] * lowers[blk])
        return carry

    third = COLS // 8 // 3
    stores = []
    for n in range(3):
        lax.fori_loop(n * third, (n + 1) * third, sweep, 0)
        rows = pl.ds(n * third * 8, third * 8)
        stores.append(pltpu.make_async_copy(result.at[rows], out.at[rows], out_sem.at[n]))
        stores[-1].start()

    for d in range(1, ngy):
        phase1(d).wait_send()
    for d in range(1, ngx):
        phase2(d).wait_send()
    for k in range(3):
        for h in range(2):
            for move in halo(h, k):
                move.wait_send()
    for store in stores:
        store.wait()


def on_device(ngx, ngy, state, wind_x, wind_y, mass, inv_mass, span_of, block_inverse, coupling):
    devices = ngx * ngy
    width = state.shape[2]
    per_gy = ngx * 16 + ngx
    per_gx = ngy * 16 + ngy
    any_ = pl.BlockSpec(memory_space=pl.ANY)
    smem = pl.BlockSpec(memory_space=pltpu.SMEM)
    nodes = (2, NX, NY, 8, 128)
    vmem = pltpu.VMEM
    dma = pltpu.SemaphoreType.DMA
    return pl.pallas_call(
        functools.partial(kernel, ngx, ngy),
        out_shape=jax.ShapeDtypeStruct((COLS, width), F32),
        in_specs=[any_, any_, any_, smem, smem, any_, any_, any_],
        out_specs=any_,
        scratch_shapes=[
            vmem(state.shape, F32), vmem(wind_x.shape, F32), vmem(wind_y.shape, F32), vmem(span_of.shape, jnp.int32),
            vmem(block_inverse.shape, F32), vmem(coupling.shape, F32),
            vmem(nodes, F32), vmem(nodes, F32),
            vmem((2, NX * NY * 8, 128), F32), vmem((2, NX * NY * 8, 128), F32),
            vmem((2, 2, UX, UY, 8, 128), F32),
            vmem((3, 2, 2, UY, 8, 128), F32), vmem((3, 2, 2, UX, 8, 128), F32),
            vmem((3, 2, 2, UY, 8, 128), F32), vmem((3, 2, 2, UX, 8, 128), F32), vmem((3, 2, 4, 8, 128), F32),
            vmem((2, COLS * 8, 128), F32),
            vmem((ngy, per_gy, 128), F32), vmem((ngy, per_gy, 128), F32),
            vmem((ngx, per_gx, 128), F32), vmem((ngx, per_gx, 128), F32),
            vmem((COLS, 2 * devices), BF16), vmem((8, COLS, 256), BF16), vmem((2, 256, 2048), BF16),
            vmem((2, 8, COLS, 2048), F32),
            vmem((4, COLS, 128), F32), vmem((COLS, 128), F32), vmem((COLS, 128), F32),
            vmem((COLS, width), F32),
            dma((6,)), dma((3,)), dma((3, 2, 8)), dma((3, 2, 8)),
            dma((ngy,)), dma((ngy,)), dma((ngx,)), dma((ngx,)),
        ],
        compiler_params=pltpu.CompilerParams(
            collective_id=0, has_side_effects=True, vmem_limit_bytes=60 * 2**20),
    )(state, wind_x, wind_y, mass, inv_mass, span_of, block_inverse, coupling)


def solution(mesh):
    placed = (
        P("gx", "gy", None),
        P("gx", "gy", None),
        P("gx", "gy", None),
        P("gx", "gy"),
        P("gx", "gy"),
        P(("gx", "gy"), None),
        P(("gx", "gy"), None),
        P(("gx", "gy"), None),
    )
    return jax.shard_map(
        functools.partial(on_device, mesh.shape["gx"], mesh.shape["gy"]),
        mesh=mesh, in_specs=placed, out_specs=P(("gx", "gy"), None), check_vma=False,
    )
```

```python
import functools

import jax
import jax.numpy as jnp
import numpy as np
from jax import lax
from jax.experimental import pallas as pl
from jax.experimental.pallas import tpu as pltpu
from jax.sharding import PartitionSpec as P

NP = 4
NB = 4
SWEEPS = 3
STEP = 0.05
EX = 2
EY = 8
NX = EX * NP
NY = EY * NP
UX = EX * 3 + 1
UY = EY * 3 + 1
COLS = EX * 3 * EY * 3
MESH = pl.DeviceIdType.MESH
F32 = jnp.float32
BF16 = jnp.bfloat16


def derivative_table():
    points = np.array([-1.0, -1.0 / np.sqrt(5.0), 1.0 / np.sqrt(5.0), 1.0])
    count = points.shape[0]
    weights = np.ones(count)
    for i in range(count):
        for m in range(count):
            if m != i:
                weights[i] = weights[i] * (points[i] - points[m])
    table = np.zeros((count, count))
    for i in range(count):
        for j in range(count):
            if i != j:
                table[i, j] = weights[i] / weights[j] / (points[i] - points[j])
                table[i, i] = table[i, i] + 1.0 / (points[i] - points[j])
    return table


TABLE = derivative_table()
ODD = [float((TABLE[i, 0] + TABLE[i, 3]) / 2) for i in range(2)]
EVEN = [[float((TABLE[i, k] - TABLE[i, 3 - k]) / 2) for k in range(2)] for i in range(2)]


def derivative(q):
    outer, inner = q[0] - q[3], q[1] - q[2]
    bend = (q[0] + q[3]) - (q[1] + q[2])
    odd = [ODD[i] * bend for i in range(2)]
    even = [EVEN[i][0] * outer + EVEN[i][1] * inner for i in range(2)]
    return [even[0] + odd[0], even[1] + odd[1], even[1] - odd[1], even[0] - odd[0]]


def lane_group(shape):
    return lax.broadcasted_iota(jnp.int32, shape, 1) // 32


def spread(v):
    group = lane_group(v.shape)
    low, even = group < 2, group % 2 == 0
    turned = pltpu.roll(v, 64, 1)
    result = []
    for pair in (jnp.where(low, v, turned), jnp.where(low, turned, v)):
        swapped = pltpu.roll(pair, 32, 1)
        result += [jnp.where(even, pair, swapped), jnp.where(even, swapped, pair)]
    return result


def collect(tiles, source):
    group = lane_group(tiles[0].shape)
    result = None
    for b, tile in enumerate(tiles):
        shift = (b - source) % 4 * 32
        moved = pltpu.roll(tile, shift, 1) if shift else tile
        result = moved if result is None else jnp.where(group == b, moved, result)
    return result


def two_parts(x):
    high = x.astype(BF16)
    return high, (x - high.astype(F32)).astype(BF16)


def kernel(ngx, ngy, state, wind_x, wind_y, mass, inv_mass, span_of, inverse, coupling, out,
           raw, raw_wx, raw_wy, raw_span, raw_inv, raw_coup, st, fld, wxe, wye, grid, sx, sy, rx, ry, rc, fin,
           a0, a1, a2s, a2r, b0, b1, b2r, pairs, hot, wide, edges, kup, klo, result,
           load_sem, out_sem, hs, hr, a1s_sem, a1r_sem, a2s_sem, a2r_sem, b1s_sem, b1r_sem, b2s_sem, b2r_sem):
    gx, gy = lax.axis_index("gx"), lax.axis_index("gy")
    devices = ngx * ngy

    loads = [
        pltpu.make_async_copy(src, dst, load_sem.at[n])
        for n, (src, dst) in enumerate((
            (wind_x, raw_wx), (wind_y, raw_wy), (state, raw), (inverse, raw_inv), (coupling, raw_coup), (span_of, raw_span)))
    ]
    for load in loads:
        load.start()

    barrier = pltpu.get_barrier_semaphore()

    def at(dx, dy):
        return (lax.rem(gx + (dx + ngx), ngx), lax.rem(gy + (dy + ngy), ngy))

    for d in range(1, ngy):
        pl.semaphore_signal(barrier, inc=1, device_id=at(0, d), device_id_type=MESH)
    for d in range(1, ngx):
        pl.semaphore_signal(barrier, inc=1, device_id=at(d, 0), device_id_type=MESH)
    for dx in (-1, 1):
        for dy in (-1, 1):
            pl.semaphore_signal(barrier, inc=1, device_id=at(dx, dy), device_id_type=MESH)

    level = lax.rem(lax.broadcasted_iota(jnp.int32, (128, 128), 0), 64)
    target = lax.broadcasted_iota(jnp.int32, (128, 128), 1) // 32
    for n, (raw_w, wide_w) in enumerate(((raw_wx, wxe), (raw_wy, wye))):
        loads[n].wait()
        w = raw_w[...].reshape(NX * NY, 64)
        high = w.astype(BF16).astype(F32)
        parts = jnp.concatenate([high, w - high], axis=1).astype(BF16)
        for i in range(16):
            spreader = (level == target + 4 * i).astype(BF16)
            value = jnp.dot(parts, spreader, preferred_element_type=F32)
            wide_w[i // 8, pl.ds(i % 8, NX * NY, stride=8), :] = value

    loads[2].wait()

    def turn(n, carry):
        x, y8 = n // (NY // 8), lax.rem(n, NY // 8)
        for h in range(2):
            block = raw[x, pl.ds(pl.multiple_of(y8 * 8, 8), 8), 1024 * h:1024 * (h + 1)]
            st[h, x, pl.ds(y8 * 8, 8)] = block.reshape(8, 8, 128)
        return carry

    lax.fori_loop(0, NX * NY // 8, turn, 0)

    def weighted(h, k, field):
        def body(ey, carry):
            lines = []
            for ex in range(EX):
                f = [[field(h, ex * NP + i, ey, j) for j in range(NP)] for i in range(NP)]
                along_x = [derivative([f[i][j] for i in range(NP)]) for j in range(NP)]
                along_y = [derivative(f[i]) for i in range(NP)]
                w = []
                for i in range(NP):
                    row = []
                    for j in range(NP):
                        x, y = ex * NP + i, ey * NP + j
                        node = pl.ds(pl.multiple_of((x * NY + y) * 8, 8), 8)
                        flow = wxe[h, node, :] * along_x[j][i] + wye[h, node, :] * along_y[i][j]
                        row.append(mass[x, y] * flow)
                    w.append(row)
                if lines:
                    lines[-1] = [a + b for a, b in zip(lines[-1], w[0])]
                    lines += w[1:]
                else:
                    lines = w
            for X in range(UX):
                values = [carry[X] + lines[X][0], lines[X][1], lines[X][2]]
                for j in range(3):
                    grid[k % 2, h, X, ey * 3 + j] = values[j]
                    if X == 0:
                        sx[k, h, 0, ey * 3 + j] = values[j]
                    if X == UX - 1:
                        sx[k, h, 1, ey * 3 + j] = values[j]
            return tuple(lines[X][3] for X in range(UX))

        carry = lax.fori_loop(0, EY, body, (jnp.zeros((8, 128), F32),) * UX)
        for X in range(UX):
            grid[k % 2, h, X, UY - 1] = carry[X]
            sy[k, h, 1, X] = carry[X]
            sy[k, h, 0, X] = grid[k % 2, h, X, 0]
        sx[k, h, 0, UY - 1] = carry[0]
        sx[k, h, 1, UY - 1] = carry[UX - 1]

    def halo(h, k):
        if k < 2:
            moves = [
                (sx.at[k, h, 1], rx.at[k, h, 0], (1, 0)),
                (sx.at[k, h, 0], rx.at[k, h, 1], (-1, 0)),
                (sy.at[k, h, 1], ry.at[k, h, 0], (0, 1)),
                (sy.at[k, h, 0], ry.at[k, h, 1], (0, -1)),
                (sx.at[k, h, 1, UY - 1], rc.at[k, h, 0], (1, 1)),
                (sx.at[k, h, 1, 0], rc.at[k, h, 1], (1, -1)),
                (sx.at[k, h, 0, UY - 1], rc.at[k, h, 2], (-1, 1)),
                (sx.at[k, h, 0, 0], rc.at[k, h, 3], (-1, -1)),
            ]
        else:
            moves = [
                (sx.at[k, h, 1, pl.ds(0, UY - 1)], rx.at[k, h, 0, pl.ds(0, UY - 1)], (1, 0)),
                (sy.at[k, h, 1, pl.ds(0, UX - 1)], ry.at[k, h, 0, pl.ds(0, UX - 1)], (0, 1)),
                (sx.at[k, h, 1, UY - 1], rc.at[k, h, 0], (1, 1)),
            ]
        return [
            pltpu.make_async_remote_copy(
                src_ref=src, dst_ref=dst, send_sem=hs.at[k, h, n], recv_sem=hr.at[k, h, n],
                device_id=at(*offset), device_id_type=MESH)
            for n, (src, dst, offset) in enumerate(moves)
        ]

    def arrive(h, k):
        for move in halo(h, k):
            move.wait_recv()
        g = grid.at[k % 2, h]
        g[0] += rx[k, h, 0]
        g[UX - 1] += rx[k, h, 1]
        g[:, 0] += ry[k, h, 0]
        g[:, UY - 1] += ry[k, h, 1]
        g[0, 0] += rc[k, h, 0]
        g[0, UY - 1] += rc[k, h, 1]
        g[UX - 1, 0] += rc[k, h, 2]
        g[UX - 1, UY - 1] += rc[k, h, 3]

    def edge(h, k, x, ey, j):
        return grid[k % 2, h, x - x // NP, ey * 3 + j]

    def initial(h, x, ey, j):
        return st[h, x, ey * NP + j]

    def first(h, x, ey, j):
        y = ey * NP + j
        value = st[h, x, y] - (STEP * inv_mass[x, y]) * edge(h, 0, x, ey, j)
        fld[h, x, y] = value
        return value

    def second(h, x, ey, j):
        y = ey * NP + j
        value = 0.75 * st[h, x, y] + 0.25 * fld[h, x, y] - (0.25 * STEP * inv_mass[x, y]) * edge(h, 1, x, ey, j)
        fld[h, x, y] = value
        return value

    def final(h, lines):
        def body(ey, carry):
            for X in lines:
                for j in range(3):
                    x, y = X + X // 3, ey * NP + j
                    value = (1.0 / 3.0) * st[h, x, y] + (2.0 / 3.0) * fld[h, x, y]
                    value = value - (2.0 / 3.0 * STEP * inv_mass[x, y]) * edge(h, 2, x, ey, j)
                    row = (X * EY + ey) * 3 + j
                    fin[h, pl.ds(pl.multiple_of(row * 8, 8), 8), :] = value
            return carry

        lax.fori_loop(0, EY, body, 0)

    weighted(0, 0, initial)
    pl.semaphore_wait(barrier, ngy - 1 + ngx - 1 + 4)
    for move in halo(0, 0):
        move.start()
    weighted(1, 0, initial)
    for move in halo(1, 0):
        move.start()

    loads[3].wait()
    loads[4].wait()

    def pack(s, carry):
        upper_half = lax.broadcasted_iota(jnp.int32, (8, 128), 0) < 4
        for four in range(ngy // 4):
            rows = pl.ds(pl.multiple_of(s * (2 * ngy) + four * 8, 8), 8)
            block = raw_inv[rows, :].reshape(8, 8, 128)
            for q in range(4):
                one, two = block[2 * q], block[2 * q + 1]
                a0[four * 4 + q, pl.ds(pl.multiple_of(s * 8, 8), 8), :] = jnp.where(upper_half, one, pltpu.roll(two, 4, 0))
                b0[s, four * 4 + q] = jnp.where(upper_half, pltpu.roll(one, 4, 0), two)
        return carry

    lax.fori_loop(0, ngx, pack, 0)
    exact = functools.partial(lax.dot_general, preferred_element_type=F32, precision=lax.Precision.HIGHEST)
    across = (((1,), (1,)), ((), ()))
    plain = (((1,), (0,)), ((), ()))
    owner = lax.broadcasted_iota(jnp.int32, (devices, 2 * devices), 0)
    slot = lax.broadcasted_iota(jnp.int32, (devices, 2 * devices), 1)
    place = lax.broadcasted_iota(jnp.int32, (3, 128), 0)
    lane = lax.broadcasted_iota(jnp.int32, (3, 128), 1)
    both = sum(
        exact(exact((slot == 2 * owner + r).astype(F32), raw_coup[...], across), (lane == place + 3 * r).astype(F32), plain)
        for r in range(2)
    )
    both = both.reshape(ngx, ngy, 128)
    for s in range(ngy):
        a0[s, ngx * 8:, :] = both[:, s, :]

    def a_first(d):
        return pltpu.make_async_remote_copy(
            src_ref=a0.at[lax.rem(gy + d, ngy)], dst_ref=a1.at[gy],
            send_sem=a1s_sem.at[d], recv_sem=a1r_sem.at[d],
            device_id=at(0, d), device_id_type=MESH)

    def a_second(d):
        return pltpu.make_async_remote_copy(
            src_ref=a2s.at[lax.rem(gx + d, ngx)], dst_ref=a2r.at[gx],
            send_sem=a2s_sem.at[d], recv_sem=a2r_sem.at[d],
            device_id=at(d, 0), device_id_type=MESH)

    def b_first(d):
        return pltpu.make_async_remote_copy(
            src_ref=b0.at[lax.rem(gx + d, ngx)], dst_ref=b1.at[gx],
            send_sem=b1s_sem.at[d], recv_sem=b1r_sem.at[d],
            device_id=at(d, 0), device_id_type=MESH)

    def b_second(d):
        return pltpu.make_async_remote_copy(
            src_ref=b1.at[:, lax.rem(gy + d, ngy)], dst_ref=b2r.at[gy],
            send_sem=b2s_sem.at[d], recv_sem=b2r_sem.at[d],
            device_id=at(0, d), device_id_type=MESH)

    for d in range(1, ngx):
        b_first(d).start()
    for d in range(1, ngy):
        a_first(d).start()
    b1[gx] = b0[gx]
    a1[gy] = a0[gy]

    loads[5].wait()
    earlier = (lax.broadcasted_iota(jnp.int32, (COLS, COLS), 1) < lax.broadcasted_iota(jnp.int32, (COLS, COLS), 0)).astype(BF16)
    itself = (lax.broadcasted_iota(jnp.int32, (COLS, COLS), 1) == lax.broadcasted_iota(jnp.int32, (COLS, COLS), 0)).astype(BF16)
    span = lax.broadcasted_iota(jnp.int32, (devices, COLS), 0)
    picks = []
    for order in (span, lax.rem(span, ngx) * ngy + span // ngx):
        named = (raw_span[...] == order).astype(BF16)
        chosen = lax.dot_general(itself, named, across, preferred_element_type=F32)
        count = lax.dot_general(earlier, named, across, preferred_element_type=F32)
        picks.append(jnp.concatenate(
            [jnp.where(count < 0.5, chosen, 0.0), jnp.where(count < 0.5, 0.0, chosen)], axis=1).astype(BF16))

    entry = lax.rem(lax.broadcasted_iota(jnp.int32, (256, 128), 0), 128)
    group = lax.broadcasted_iota(jnp.int32, (256, 128), 1) // 32

    def build(b, carry):
        for e in range(2):
            hot[e, :, pl.ds(pl.multiple_of(b * 128, 128), 128)] = (entry == e * 64 + group * 16 + b).astype(F32).astype(BF16)
        return carry

    lax.fori_loop(0, 16, build, 0)

    for h in range(2):
        arrive(h, 0)
        weighted(h, 1, first)
        for move in halo(h, 1):
            move.start()

    for d in range(1, ngx):
        b_first(d).wait_recv()
    for d in range(1, ngy):
        b_second(d).start()
    for d in range(1, ngy):
        a_first(d).wait_recv()

    def repack(s, carry):
        for g in range(ngy):
            a2s[s, g * 8:(g + 1) * 8, :] = a1[g, pl.ds(pl.multiple_of(s * 8, 8), 8), :]
            a2s[s, ngy * 8 + g:ngy * 8 + g + 1, :] = a1[g, pl.ds(ngx * 8 + s, 1), :]
        return carry

    lax.fori_loop(0, ngx, repack, 0)
    for d in range(1, ngx):
        a_second(d).start()
    a2r[gx] = a2s[gx]
    b2r[gy] = b1[:, gy]

    for h in range(2):
        arrive(h, 1)
        weighted(h, 2, second)
        for move in halo(h, 2):
            move.start()

    def gather(h, j, slots):
        rows = slice((4 * h + j) * COLS, (4 * h + j + 1) * COLS)
        chosen = [jnp.dot(picks[h], part, preferred_element_type=F32).astype(BF16) for part in two_parts(slots)]
        pairs[rows, :] = jnp.concatenate(chosen, axis=1)

    def widen(h):
        rows = slice(4 * h * COLS, 4 * (h + 1) * COLS)

        def body(n, carry):
            lanes = pl.ds(pl.multiple_of(n * 256, 256), 256)
            for e in range(2):
                wide[e, n, rows, :] = jnp.dot(pairs[rows, :], hot[e, :, lanes], preferred_element_type=F32)
            return carry

        lax.fori_loop(0, 8, body, 0)

    def repeated(blk, i, b, rows):
        first_row = (2 * blk + i // 2) * COLS
        if not isinstance(rows, slice):
            start, size = rows
            rows = pl.ds(pl.multiple_of(first_row + start, 8), size)
        return wide[i % 2, b // 2, rows, b % 2 * 128:(b % 2 + 1) * 128]

    for d in range(1, ngy):
        b_second(d).wait_recv()
    for j in range(4):
        gather(1, j, jnp.concatenate([
            b2r[g, pl.ds(0, ngx), r * 4 + j, :] for r in range(2) for g in range(ngy)], axis=0))
    widen(1)
    for d in range(1, ngx):
        a_second(d).wait_recv()
    for j in range(4):
        gather(0, j, jnp.concatenate([
            a2r[g, pl.ds(r * 4 + j, ngy, stride=8), :] for r in range(2) for g in range(ngx)], axis=0))
    widen(0)

    links = jnp.concatenate([a2r[g, ngy * 8:ngy * 8 + ngy, :] for g in range(ngx)], axis=0)
    row = lax.broadcasted_iota(jnp.int32, (128, 128), 0)
    col = lax.broadcasted_iota(jnp.int32, (128, 128), 1) // 32
    up, down = 0.0, 0.0
    for r in range(2):
        mine = exact(picks[0][:, r * devices:(r + 1) * devices].astype(F32), links, plain)
        up = up + exact(mine, ((row == col + 3 * r) & (col < 3)).astype(F32), plain)
        down = down + exact(mine, ((row == col - 1 + 3 * r) & (col > 0)).astype(F32), plain)
    kup[...] = up
    klo[...] = down

    def corners(part, carry):
        start = part * 48
        rows = pl.ds(pl.multiple_of(start, 8), 48)
        for n, (i, b, source) in enumerate(((0, 0, 0), (0, 15, 0), (3, 0, 3), (3, 15, 3))):
            edges[n, rows, :] = collect([repeated(blk, i, b, (start, 48)) for blk in range(NB)], source)
        return carry

    lax.fori_loop(0, 3, corners, 0)

    def base(start, count, unroll):
        def body(n, carry):
            at_row = start + n * 8
            rows = pl.ds(pl.multiple_of(at_row, 8), 8)
            for blk in range(NB):
                total = [None] * 4
                for tile in range(4):
                    s = blk % 2 * 4 + tile
                    values = spread(fin[blk // 2, pl.ds(at_row * 8 + s, 8, stride=8), :])
                    for g in range(4):
                        for i in range(4):
                            term = repeated(blk, i, tile * 4 + g, (at_row, 8)) * values[g]
                            total[i] = term if total[i] is None else total[i] + term
                for i in range(4):
                    result[rows, (4 * blk + i) * 128:(4 * blk + i + 1) * 128] = total[i]
            return carry

        lax.fori_loop(0, count, body, 0, unroll=unroll)

    def sweep(start, size):
        rows = pl.ds(start if isinstance(start, int) else pl.multiple_of(start, 8), size)
        head = collect([result[rows, 4 * b * 128:(4 * b + 1) * 128] for b in range(NB)], 0)
        tail = collect([result[rows, (4 * b + 3) * 128:(4 * b + 4) * 128] for b in range(NB)], 3)
        now_head, now_tail = head, tail
        for n in range(SWEEPS):
            upper = kup[rows, :] * pltpu.roll(now_head, 96, 1)
            lower = klo[rows, :] * pltpu.roll(now_tail, 32, 1)
            if n < SWEEPS - 1:
                now_head = head + edges[1, rows, :] * upper + edges[0, rows, :] * lower
                now_tail = tail + edges[3, rows, :] * upper + edges[2, rows, :] * lower
        uppers, lowers = spread(upper), spread(lower)
        for blk in range(NB):
            for i in range(4):
                lanes = slice((4 * blk + i) * 128, (4 * blk + i + 1) * 128)
                result[rows, lanes] += (
                    repeated(blk, i, 15, (start, size)) * uppers[blk] + repeated(blk, i, 0, (start, size)) * lowers[blk])

    stores = []

    def store(start, size):
        rows = pl.ds(start, size)
        stores.append(pltpu.make_async_copy(result.at[rows], out.at[rows], out_sem.at[len(stores)]))
        stores[-1].start()

    line = EY * 3
    for h in range(2):
        for move in halo(h, 2)[1:]:
            move.wait_recv()
        g = grid.at[0, h]
        g[0:UX - 1, 0] += ry[2, h, 0, 0:UX - 1]
        g[0, 0] += rc[2, h, 0]
        final(h, range(1, UX - 1))
    base(line, (COLS - line) // 8, 3)
    for n in range(3):
        sweep(line + n * 40, 40)
        store(line + n * 40, 40)
    for h in range(2):
        halo(h, 2)[0].wait_recv()
        grid[0, h, 0, 0:UY - 1] += rx[2, h, 0, 0:UY - 1]
        final(h, range(1))
    base(0, line // 8, 3)
    sweep(0, line)
    store(0, line)

    for d in range(1, ngy):
        a_first(d).wait_send()
        b_second(d).wait_send()
    for d in range(1, ngx):
        a_second(d).wait_send()
        b_first(d).wait_send()
    for k in range(3):
        for h in range(2):
            for move in halo(h, k):
                move.wait_send()
    for each in stores:
        each.wait()


def on_device(ngx, ngy, state, wind_x, wind_y, mass, inv_mass, span_of, block_inverse, coupling):
    width = state.shape[2]
    any_ = pl.BlockSpec(memory_space=pl.ANY)
    smem = pl.BlockSpec(memory_space=pltpu.SMEM)
    nodes = (2, NX, NY, 8, 128)
    vmem = pltpu.VMEM
    dma = pltpu.SemaphoreType.DMA
    span_of, coupling = span_of.T, coupling.T
    return pl.pallas_call(
        functools.partial(kernel, ngx, ngy),
        out_shape=jax.ShapeDtypeStruct((COLS, width), F32),
        in_specs=[any_, any_, any_, smem, smem, any_, any_, any_],
        out_specs=any_,
        scratch_shapes=[
            vmem(state.shape, F32), vmem(wind_x.shape, F32), vmem(wind_y.shape, F32), vmem(span_of.shape, jnp.int32),
            vmem(block_inverse.shape, F32), vmem(coupling.shape, F32),
            vmem(nodes, F32), vmem(nodes, F32),
            vmem((2, NX * NY * 8, 128), F32), vmem((2, NX * NY * 8, 128), F32),
            vmem((2, 2, UX, UY, 8, 128), F32),
            vmem((3, 2, 2, UY, 8, 128), F32), vmem((3, 2, 2, UX, 8, 128), F32),
            vmem((3, 2, 2, UY, 8, 128), F32), vmem((3, 2, 2, UX, 8, 128), F32), vmem((3, 2, 4, 8, 128), F32),
            vmem((2, COLS * 8, 128), F32),
            vmem((ngy, ngx * 9, 128), F32), vmem((ngy, ngx * 9, 128), F32),
            vmem((ngx, ngy * 9, 128), F32), vmem((ngx, ngy * 9, 128), F32),
            vmem((ngx, ngy, 8, 128), F32), vmem((ngx, ngy, 8, 128), F32), vmem((ngy, ngx, 8, 128), F32),
            vmem((8 * COLS, 256), BF16), vmem((2, 256, 2048), BF16),
            vmem((2, 8, 8 * COLS, 256), F32),
            vmem((4, COLS, 128), F32), vmem((COLS, 128), F32), vmem((COLS, 128), F32),
            vmem((COLS, width), F32),
            dma((6,)), dma((4,)), dma((3, 2, 8)), dma((3, 2, 8)),
            dma((ngy,)), dma((ngy,)), dma((ngx,)), dma((ngx,)),
            dma((ngx,)), dma((ngx,)), dma((ngy,)), dma((ngy,)),
        ],
        compiler_params=pltpu.CompilerParams(
            collective_id=0, has_side_effects=True, vmem_limit_bytes=60 * 2**20),
    )(state, wind_x, wind_y, mass, inv_mass, span_of, block_inverse, coupling)


def solution(mesh):
    placed = (
        P("gx", "gy", None),
        P("gx", "gy", None),
        P("gx", "gy", None),
        P("gx", "gy"),
        P("gx", "gy"),
        P(("gx", "gy"), None),
        P(("gx", "gy"), None),
        P(("gx", "gy"), None),
    )
    return jax.shard_map(
        functools.partial(on_device, mesh.shape["gx"], mesh.shape["gy"]),
        mesh=mesh, in_specs=placed, out_specs=P(("gx", "gy"), None), check_vma=False,
    )
```

```python
import functools

import jax
import jax.numpy as jnp
import numpy as np
from jax import lax
from jax.experimental import pallas as pl
from jax.experimental.pallas import tpu as pltpu
from jax.sharding import PartitionSpec as P

NP = 4
NB = 4
SWEEPS = 3
STEP = 0.05
EX = 2
EY = 8
NX = EX * NP
NY = EY * NP
UX = EX * 3 + 1
UY = EY * 3 + 1
COLS = EX * 3 * EY * 3
LINE = EY * 3
SKIP = COLS - 128
MESH = pl.DeviceIdType.MESH
F32 = jnp.float32
BF16 = jnp.bfloat16


def derivative_table():
    points = np.array([-1.0, -1.0 / np.sqrt(5.0), 1.0 / np.sqrt(5.0), 1.0])
    count = points.shape[0]
    weights = np.ones(count)
    for i in range(count):
        for m in range(count):
            if m != i:
                weights[i] = weights[i] * (points[i] - points[m])
    table = np.zeros((count, count))
    for i in range(count):
        for j in range(count):
            if i != j:
                table[i, j] = weights[i] / weights[j] / (points[i] - points[j])
                table[i, i] = table[i, i] + 1.0 / (points[i] - points[j])
    return table


TABLE = derivative_table()
ODD = [float((TABLE[i, 0] + TABLE[i, 3]) / 2) for i in range(2)]
EVEN = [[float((TABLE[i, k] - TABLE[i, 3 - k]) / 2) for k in range(2)] for i in range(2)]


def derivative(q):
    outer, inner = q[0] - q[3], q[1] - q[2]
    bend = (q[0] + q[3]) - (q[1] + q[2])
    odd = [ODD[i] * bend for i in range(2)]
    even = [EVEN[i][0] * outer + EVEN[i][1] * inner for i in range(2)]
    return [even[0] + odd[0], even[1] + odd[1], even[1] - odd[1], even[0] - odd[0]]


def two_parts(x):
    high = x.astype(BF16)
    return high, (x - high.astype(F32)).astype(BF16)


def kernel(ngx, ngy, state, wind_x, wind_y, mass, inv_mass, span_of, inverse, coupling, out,
           raw, raw_wx, raw_wy, raw_span, raw_inv, raw_coup, st, fld, wxe, wye, grid, sx, sy, rx, ry, rc, fin,
           a0, a1, a2s, a2r, b0, b1, b2r, kt, bt, vt, xt, kp, bp, vp, xp, result,
           load_sem, out_sem, hs, hr, a1s_sem, a1r_sem, a2s_sem, a2r_sem, b1s_sem, b1r_sem, b2s_sem, b2r_sem):
    gx, gy = lax.axis_index("gx"), lax.axis_index("gy")
    devices = ngx * ngy

    loads = [
        pltpu.make_async_copy(src, dst, load_sem.at[n])
        for n, (src, dst) in enumerate((
            (inverse, raw_inv), (wind_x, raw_wx), (wind_y, raw_wy), (state, raw), (coupling, raw_coup), (span_of, raw_span)))
    ]
    for load in loads:
        load.start()

    barrier = pltpu.get_barrier_semaphore()

    def at(dx, dy):
        return (lax.rem(gx + (dx + ngx), ngx), lax.rem(gy + (dy + ngy), ngy))

    for d in range(1, ngy):
        pl.semaphore_signal(barrier, inc=1, device_id=at(0, d), device_id_type=MESH)
    for d in range(1, ngx):
        pl.semaphore_signal(barrier, inc=1, device_id=at(d, 0), device_id_type=MESH)
    for dx in (-1, 1):
        for dy in (-1, 1):
            pl.semaphore_signal(barrier, inc=1, device_id=at(dx, dy), device_id_type=MESH)

    def a_first(d):
        return pltpu.make_async_remote_copy(
            src_ref=a0.at[lax.rem(gy + d, ngy)], dst_ref=a1.at[gy],
            send_sem=a1s_sem.at[d], recv_sem=a1r_sem.at[d],
            device_id=at(0, d), device_id_type=MESH)

    def a_second(d):
        return pltpu.make_async_remote_copy(
            src_ref=a2s.at[lax.rem(gx + d, ngx)], dst_ref=a2r.at[gx],
            send_sem=a2s_sem.at[d], recv_sem=a2r_sem.at[d],
            device_id=at(d, 0), device_id_type=MESH)

    def b_first(d):
        return pltpu.make_async_remote_copy(
            src_ref=b0.at[lax.rem(gx + d, ngx)], dst_ref=b1.at[gx],
            send_sem=b1s_sem.at[d], recv_sem=b1r_sem.at[d],
            device_id=at(d, 0), device_id_type=MESH)

    def b_second(d):
        return pltpu.make_async_remote_copy(
            src_ref=b1.at[:, lax.rem(gy + d, ngy)], dst_ref=b2r.at[gy],
            send_sem=b2s_sem.at[d], recv_sem=b2r_sem.at[d],
            device_id=at(0, d), device_id_type=MESH)

    def weighted(h, k, field):
        def body(ey, carry):
            lines = []
            for ex in range(EX):
                f = [[field(h, ex * NP + i, ey, j) for j in range(NP)] for i in range(NP)]
                along_x = [derivative([f[i][j] for i in range(NP)]) for j in range(NP)]
                along_y = [derivative(f[i]) for i in range(NP)]
                w = []
                for i in range(NP):
                    row = []
                    for j in range(NP):
                        x, y = ex * NP + i, ey * NP + j
                        node = pl.ds(pl.multiple_of((x * NY + y) * 8, 8), 8)
                        flow = wxe[h, node, :] * along_x[j][i] + wye[h, node, :] * along_y[i][j]
                        row.append(mass[x, y] * flow)
                    w.append(row)
                if lines:
                    lines[-1] = [a + b for a, b in zip(lines[-1], w[0])]
                    lines += w[1:]
                else:
                    lines = w
            for X in range(UX):
                values = [carry[X] + lines[X][0], lines[X][1], lines[X][2]]
                for j in range(3):
                    grid[k % 2, h, X, ey * 3 + j] = values[j]
                    if X == 0:
                        sx[k, h, 0, ey * 3 + j] = values[j]
                    if X == UX - 1:
                        sx[k, h, 1, ey * 3 + j] = values[j]
            return tuple(lines[X][3] for X in range(UX))

        carry = lax.fori_loop(0, EY, body, (jnp.zeros((8, 128), F32),) * UX)
        for X in range(UX):
            grid[k % 2, h, X, UY - 1] = carry[X]
            sy[k, h, 1, X] = carry[X]
            sy[k, h, 0, X] = grid[k % 2, h, X, 0]
        sx[k, h, 0, UY - 1] = carry[0]
        sx[k, h, 1, UY - 1] = carry[UX - 1]

    def halo(h, k):
        if k < 2:
            moves = [
                (sx.at[k, h, 1, UY - 1], rc.at[k, h, 0], (1, 1)),
                (sx.at[k, h, 1, 0], rc.at[k, h, 1], (1, -1)),
                (sx.at[k, h, 0, UY - 1], rc.at[k, h, 2], (-1, 1)),
                (sx.at[k, h, 0, 0], rc.at[k, h, 3], (-1, -1)),
                (sy.at[k, h, 1], ry.at[k, h, 0], (0, 1)),
                (sy.at[k, h, 0], ry.at[k, h, 1], (0, -1)),
                (sx.at[k, h, 1], rx.at[k, h, 0], (1, 0)),
                (sx.at[k, h, 0], rx.at[k, h, 1], (-1, 0)),
            ]
        else:
            moves = [
                (sx.at[k, h, 1, UY - 1], rc.at[k, h, 0], (1, 1)),
                (sy.at[k, h, 1, pl.ds(0, UX - 1)], ry.at[k, h, 0, pl.ds(0, UX - 1)], (0, 1)),
                (sx.at[k, h, 1, pl.ds(0, UY - 1)], rx.at[k, h, 0, pl.ds(0, UY - 1)], (1, 0)),
            ]
        return [
            pltpu.make_async_remote_copy(
                src_ref=src, dst_ref=dst, send_sem=hs.at[k, h, n], recv_sem=hr.at[k, h, n],
                device_id=at(*offset), device_id_type=MESH)
            for n, (src, dst, offset) in enumerate(moves)
        ]

    def arrive(h, k):
        for move in halo(h, k):
            move.wait_recv()
        g = grid.at[k % 2, h]
        g[0] += rx[k, h, 0]
        g[UX - 1] += rx[k, h, 1]
        g[:, 0] += ry[k, h, 0]
        g[:, UY - 1] += ry[k, h, 1]
        g[0, 0] += rc[k, h, 0]
        g[0, UY - 1] += rc[k, h, 1]
        g[UX - 1, 0] += rc[k, h, 2]
        g[UX - 1, UY - 1] += rc[k, h, 3]

    def edge(h, k, x, ey, j):
        return grid[k % 2, h, x - x // NP, ey * 3 + j]

    def initial(h, x, ey, j):
        return st[h, x, ey * NP + j]

    def first(h, x, ey, j):
        y = ey * NP + j
        value = st[h, x, y] - (STEP * inv_mass[x, y]) * edge(h, 0, x, ey, j)
        fld[h, x, y] = value
        return value

    def second(h, x, ey, j):
        y = ey * NP + j
        value = 0.75 * st[h, x, y] + 0.25 * fld[h, x, y] - (0.25 * STEP * inv_mass[x, y]) * edge(h, 1, x, ey, j)
        fld[h, x, y] = value
        return value

    def final(h, lines):
        def body(ey, carry):
            for X in lines:
                for j in range(3):
                    x, y = X + X // 3, ey * NP + j
                    value = (1.0 / 3.0) * st[h, x, y] + (2.0 / 3.0) * fld[h, x, y]
                    value = value - (2.0 / 3.0 * STEP * inv_mass[x, y]) * edge(h, 2, x, ey, j)
                    row = (X * EY + ey) * 3 + j
                    fin[h, pl.ds(pl.multiple_of(row * 8, 8), 8), :] = value
            return carry

        lax.fori_loop(0, EY, body, 0)

    def go(h, k):
        moves = halo(h, k)
        for move in moves:
            move.start()
        return moves

    def sent(moves):
        for move in moves:
            move.wait_send()

    def repack(s, carry):
        for g in range(ngy):
            a2s[s, g * 8:(g + 1) * 8, :] = a1[g, pl.ds(pl.multiple_of(s * 8, 8), 8), :]
            a2s[s, ngy * 8 + g:ngy * 8 + g + 1, :] = a1[g, pl.ds(ngx * 8 + s, 1), :]
        return carry

    def gather(h, slots):
        chosen = sum(
            jnp.dot(picks[h], part, preferred_element_type=F32) for part in two_parts(jnp.concatenate(slots, axis=1)))
        for j in range(4):
            block = chosen[:, j * 128:(j + 1) * 128]
            rows = slice((4 * h + j) * 128, (4 * h + j + 1) * 128)
            bt[rows, :] = block[SKIP:].T
            bp[rows, :] = jnp.concatenate([block[:32]] * 4, axis=0).T

    level = lax.rem(lax.broadcasted_iota(jnp.int32, (128, 128), 0), 64)
    target = lax.broadcasted_iota(jnp.int32, (128, 128), 1) // 32
    for n, (raw_w, wide_w) in enumerate(((raw_wx, wxe), (raw_wy, wye))):
        loads[1 + n].wait()
        w = raw_w[...].reshape(NX * NY, 64)
        high = w.astype(BF16).astype(F32)
        parts = jnp.concatenate([high, w - high], axis=1).astype(BF16)
        for i in range(16):
            spreader = (level == target + 4 * i).astype(BF16)
            value = jnp.dot(parts, spreader, preferred_element_type=F32)
            wide_w[i // 8, pl.ds(i % 8, NX * NY, stride=8), :] = value

    loads[3].wait()

    def turn(n, carry):
        x, y8 = n // (NY // 8), lax.rem(n, NY // 8)
        for h in range(2):
            block = raw[x, pl.ds(pl.multiple_of(y8 * 8, 8), 8), 1024 * h:1024 * (h + 1)]
            st[h, x, pl.ds(y8 * 8, 8)] = block.reshape(8, 8, 128)
        return carry

    lax.fori_loop(0, NX * NY // 8, turn, 0)

    for h in range(2):
        fin[h, SKIP * 8:LINE * 8, :] = jnp.zeros(((LINE - SKIP) * 8, 128), F32)
    weighted(0, 0, initial)
    pl.semaphore_wait(barrier, ngy - 1 + ngx - 1 + 4)
    m00 = go(0, 0)
    loads[0].wait()

    def pack(s, carry):
        upper_half = lax.broadcasted_iota(jnp.int32, (8, 128), 0) < 4
        for four in range(ngy // 4):
            rows = pl.ds(pl.multiple_of(s * (2 * ngy) + four * 8, 8), 8)
            block = raw_inv[rows, :].reshape(8, 8, 128)
            for q in range(4):
                one, two = block[2 * q], block[2 * q + 1]
                a0[four * 4 + q, pl.ds(pl.multiple_of(s * 8, 8), 8), :] = jnp.where(upper_half, one, pltpu.roll(two, 4, 0))
                b0[s, four * 4 + q] = jnp.where(upper_half, pltpu.roll(one, 4, 0), two)
        return carry

    lax.fori_loop(0, ngx, pack, 0)
    for d in range(1, 8):
        b_first(d).start()
    b1[gx] = b0[gx]
    weighted(1, 0, initial)
    m10 = go(1, 0)
    for d in range(8, 16):
        b_first(d).start()
    across = (((1,), (1,)), ((), ()))
    loads[4].wait()
    slot = lax.broadcasted_iota(jnp.int32, (3, 2 * devices), 1)
    rows = jnp.concatenate(
        [jnp.where(lax.rem(slot, 2) == r, raw_coup[...], 0.0) for r in range(2)] + [jnp.zeros((122, 2 * devices), F32)], axis=0)
    owner = lax.broadcasted_iota(jnp.int32, (devices, 2 * devices), 0)
    slot = lax.broadcasted_iota(jnp.int32, (devices, 2 * devices), 1)
    chooser = (slot // 2 == owner).astype(BF16)
    both = sum(lax.dot_general(chooser, part, across, preferred_element_type=F32) for part in two_parts(rows))
    both = both.reshape(ngx, ngy, 128)
    for s in range(ngy):
        a0[s, ngx * 8:, :] = both[:, s, :]

    for d in range(1, 8):
        a_first(d).start()
    a1[gy] = a0[gy]
    loads[5].wait()
    earlier = (lax.broadcasted_iota(jnp.int32, (COLS, COLS), 1) < lax.broadcasted_iota(jnp.int32, (COLS, COLS), 0)).astype(BF16)
    itself = (lax.broadcasted_iota(jnp.int32, (COLS, COLS), 1) == lax.broadcasted_iota(jnp.int32, (COLS, COLS), 0)).astype(BF16)
    span = lax.broadcasted_iota(jnp.int32, (devices, COLS), 0)
    picks = []
    for order in (span, lax.rem(span, ngx) * ngy + span // ngx):
        named = (raw_span[...] == order).astype(BF16)
        chosen = lax.dot_general(itself, named, across, preferred_element_type=F32)
        count = lax.dot_general(earlier, named, across, preferred_element_type=F32)
        picks.append(jnp.concatenate(
            [jnp.where(count < 0.5, chosen, 0.0), jnp.where(count < 0.5, 0.0, chosen)], axis=1).astype(BF16))

    arrive(0, 0)
    weighted(0, 1, first)
    m01 = go(0, 1)
    arrive(1, 0)
    weighted(1, 1, first)
    m11 = go(1, 1)
    for d in range(1, ngx):
        b_first(d).wait_recv()
    for d in range(1, 8):
        b_second(d).start()
    b2r[gy] = b1[:, gy]
    for d in range(1, ngy):
        a_first(d).wait_recv()
    lax.fori_loop(0, ngx, repack, 0)
    a2r[gx] = a2s[gx]
    for d in range(1, 16):
        a_second(d).start()
    arrive(0, 1)
    weighted(0, 2, second)
    m02 = go(0, 2)
    arrive(1, 1)
    weighted(1, 2, second)
    m12 = go(1, 2)
    for d in range(1, ngy):
        b_second(d).wait_recv()
    gather(1, [
        jnp.concatenate([b2r[g, pl.ds(0, ngx), r * 4 + j, :] for r in range(2) for g in range(ngy)], axis=0)
        for j in range(4)])
    for d in range(1, ngx):
        a_second(d).wait_recv()
    gather(0, [
        jnp.concatenate([a2r[g, pl.ds(r * 4 + j, ngy, stride=8), :] for r in range(2) for g in range(ngx)], axis=0)
        for j in range(4)])

    links = jnp.concatenate([a2r[g, ngy * 8:ngy * 8 + ngy, :] for g in range(ngx)], axis=0)
    links = jnp.concatenate([links, pltpu.roll(links, 125, 1)], axis=0)
    strength = sum(jnp.dot(picks[0], part, preferred_element_type=F32) for part in two_parts(links))
    kt[...] = strength[SKIP:].T
    kp[...] = jnp.concatenate([strength[:32]] * 4, axis=0).T

    last = [m02, m12]
    def solve(h, count, blocks, values, solved):
        def body(n, carry):
            blk, four = 2 * h + n // 4, lax.rem(n, 4)
            rows = blocks[pl.ds(pl.multiple_of(blk * 256 + four * 64, 8), 64), :]
            for tt in range(count):
                v = [values[pl.ds(pl.multiple_of(((blk * 16 + b) * count + tt) * 8, 8), 8), :] for b in range(16)]
                for a in range(4):
                    total = None
                    for b in range(16):
                        term = rows[a * 16 + b:a * 16 + b + 1, :] * v[b]
                        total = term if total is None else total + term
                    solved[pl.ds(pl.multiple_of(((blk * 16 + four * 4 + a) * count + tt) * 8, 8), 8), :] = total
            return carry

        lax.fori_loop(0, 8, body, 0)

    def sweep(tt, count, blocks, strengths, solved):
        def level(blk, a):
            return pl.ds(pl.multiple_of(((blk * 16 + a) * count + tt) * 8, 8), 8)

        def entry(blk, a, b):
            return blocks[blk * 256 + a * 16 + b:blk * 256 + a * 16 + b + 1, :]

        head = [solved[level(b, 0), :] for b in range(NB)]
        tail = [solved[level(b, 15), :] for b in range(NB)]
        strength = [strengths[b:b + 1, :] for b in range(NB - 1)]
        now_head, now_tail = head, tail
        for n in range(SWEEPS):
            upper = [strength[b] * now_head[b + 1] for b in range(NB - 1)] + [None]
            lower = [None] + [strength[b] * now_tail[b] for b in range(NB - 1)]
            if n < SWEEPS - 1:
                now_head, now_tail = list(head), list(tail)
                for b in range(NB):
                    for a, now in ((0, now_head), (15, now_tail)):
                        if upper[b] is not None:
                            now[b] = now[b] + entry(b, a, 15) * upper[b]
                        if lower[b] is not None:
                            now[b] = now[b] + entry(b, a, 0) * lower[b]
        for b in range(NB):
            for a in range(16):
                value = solved[level(b, a), :]
                if upper[b] is not None:
                    value = value + entry(b, a, 15) * upper[b]
                if lower[b] is not None:
                    value = value + entry(b, a, 0) * lower[b]
                solved[level(b, a), :] = value

    quarter = lax.broadcasted_iota(jnp.int32, (8, 128), 1) // 32

    def lay_many(h):
        for s in range(8):
            vt[(8 * h + s) * 128:(8 * h + s + 1) * 128, :] = fin[h, pl.ds(SKIP * 8 + s, 128, stride=8), :].T

    def lay_few(h):
        for s in range(8):
            four = jnp.concatenate([fin[h, pl.ds(s, 32, stride=8), :]] * 4, axis=0).T
            for g in range(4):
                value = four[g * 32:g * 32 + 8]
                for q in range(1, 4):
                    value = jnp.where(quarter == q, four[g * 32 + q * 8:g * 32 + q * 8 + 8], value)
                vp[((8 * h + s) * 4 + g) * 8:((8 * h + s) * 4 + g + 1) * 8, :] = value

    def take_many(s):
        turned = xt[s * 128:(s + 1) * 128, :].T
        result[LINE:, s * 128:(s + 1) * 128] = turned[LINE - SKIP:]

    eighth = lax.rem(lax.broadcasted_iota(jnp.int32, (LINE, 128), 1) // 8, 4)

    def take_few(s):
        turned = jnp.concatenate([xp[(s * 4 + g) * 8:(s * 4 + g + 1) * 8, :] for g in range(4) for q in range(4)], axis=0).T
        value = turned[:LINE]
        for q in range(1, 4):
            value = jnp.where(eighth == q, turned[q * 32:q * 32 + LINE], value)
        result[:LINE, s * 128:(s + 1) * 128] = value

    stores = []

    def store(start, size):
        rows = pl.ds(start, size)
        stores.append(pltpu.make_async_copy(result.at[rows], out.at[rows], out_sem.at[len(stores)]))
        stores[-1].start()

    for h in range(2):
        for move in last[h][:2]:
            move.wait_recv()
        g = grid.at[0, h]
        g[0:UX - 1, 0] += ry[2, h, 0, 0:UX - 1]
        g[0, 0] += rc[2, h, 0]
        final(h, range(1, UX - 1))
        lay_many(h)
        solve(h, 4, bt, vt, xt)

    def sweep_many(tt, carry):
        sweep(tt, 4, bt, kt, xt)
        return carry

    lax.fori_loop(0, 4, sweep_many, 0)
    for s in range(16):
        take_many(s)
    store(LINE, COLS - LINE)
    for h in range(2):
        last[h][2].wait_recv()
        grid[0, h, 0, 0:UY - 1] += rx[2, h, 0, 0:UY - 1]
        final(h, range(1))
        lay_few(h)
        solve(h, 1, bp, vp, xp)
    sweep(0, 1, bp, kp, xp)
    for s in range(16):
        take_few(s)
    store(0, LINE)

    for d in range(1, ngy):
        a_first(d).wait_send()
        b_second(d).wait_send()
    for d in range(1, ngx):
        a_second(d).wait_send()
        b_first(d).wait_send()
    for k in range(3):
        for h in range(2):
            for move in halo(h, k):
                move.wait_send()
    for each in stores:
        each.wait()


def on_device(ngx, ngy, state, wind_x, wind_y, mass, inv_mass, span_of, block_inverse, coupling):
    width = state.shape[2]
    any_ = pl.BlockSpec(memory_space=pl.ANY)
    smem = pl.BlockSpec(memory_space=pltpu.SMEM)
    nodes = (2, NX, NY, 8, 128)
    vmem = pltpu.VMEM
    dma = pltpu.SemaphoreType.DMA
    span_of, coupling = span_of.T, coupling.T
    return pl.pallas_call(
        functools.partial(kernel, ngx, ngy),
        out_shape=jax.ShapeDtypeStruct((COLS, width), F32),
        in_specs=[any_, any_, any_, smem, smem, any_, any_, any_],
        out_specs=any_,
        scratch_shapes=[
            vmem(state.shape, F32), vmem(wind_x.shape, F32), vmem(wind_y.shape, F32), vmem(span_of.shape, jnp.int32),
            vmem(block_inverse.shape, F32), vmem(coupling.shape, F32),
            vmem(nodes, F32), vmem(nodes, F32),
            vmem((2, NX * NY * 8, 128), F32), vmem((2, NX * NY * 8, 128), F32),
            vmem((2, 2, UX, UY, 8, 128), F32),
            vmem((3, 2, 2, UY, 8, 128), F32), vmem((3, 2, 2, UX, 8, 128), F32),
            vmem((3, 2, 2, UY, 8, 128), F32), vmem((3, 2, 2, UX, 8, 128), F32), vmem((3, 2, 4, 8, 128), F32),
            vmem((2, COLS * 8, 128), F32),
            vmem((ngy, ngx * 9, 128), F32), vmem((ngy, ngx * 9, 128), F32),
            vmem((ngx, ngy * 9, 128), F32), vmem((ngx, ngy * 9, 128), F32),
            vmem((ngx, ngy, 8, 128), F32), vmem((ngx, ngy, 8, 128), F32), vmem((ngy, ngx, 8, 128), F32),
            vmem((128, 128), F32), vmem((1024, 128), F32), vmem((2048, 128), F32), vmem((2048, 128), F32),
            vmem((128, 128), F32), vmem((1024, 128), F32), vmem((512, 128), F32), vmem((512, 128), F32),
            vmem((COLS, width), F32),
            dma((6,)), dma((2,)), dma((3, 2, 8)), dma((3, 2, 8)),
            dma((ngy,)), dma((ngy,)), dma((ngx,)), dma((ngx,)),
            dma((ngx,)), dma((ngx,)), dma((ngy,)), dma((ngy,)),
        ],
        compiler_params=pltpu.CompilerParams(
            collective_id=0, has_side_effects=True, vmem_limit_bytes=60 * 2**20),
    )(state, wind_x, wind_y, mass, inv_mass, span_of, block_inverse, coupling)


def solution(mesh):
    placed = (
        P("gx", "gy", None),
        P("gx", "gy", None),
        P("gx", "gy", None),
        P("gx", "gy"),
        P("gx", "gy"),
        P(("gx", "gy"), None),
        P(("gx", "gy"), None),
        P(("gx", "gy"), None),
    )
    return jax.shard_map(
        functools.partial(on_device, mesh.shape["gx"], mesh.shape["gy"]),
        mesh=mesh, in_specs=placed, out_specs=P(("gx", "gy"), None), check_vma=False,
    )
```

```python
import functools

import jax
import jax.numpy as jnp
import numpy as np
from jax import lax
from jax.experimental import pallas as pl
from jax.experimental.pallas import tpu as pltpu
from jax.sharding import PartitionSpec as P

NP = 4
NB = 4
SWEEPS = 3
STEP = 0.05
EX = 2
EY = 8
NX = EX * NP
NY = EY * NP
UX = EX * 3 + 1
UY = EY * 3 + 1
COLS = EX * 3 * EY * 3
LINE = EY * 3
SKIP = COLS - 128
MESH = pl.DeviceIdType.MESH
F32 = jnp.float32
BF16 = jnp.bfloat16


def derivative_table():
    points = np.array([-1.0, -1.0 / np.sqrt(5.0), 1.0 / np.sqrt(5.0), 1.0])
    count = points.shape[0]
    weights = np.ones(count)
    for i in range(count):
        for m in range(count):
            if m != i:
                weights[i] = weights[i] * (points[i] - points[m])
    table = np.zeros((count, count))
    for i in range(count):
        for j in range(count):
            if i != j:
                table[i, j] = weights[i] / weights[j] / (points[i] - points[j])
                table[i, i] = table[i, i] + 1.0 / (points[i] - points[j])
    return table


TABLE = derivative_table()
ODD = [float((TABLE[i, 0] + TABLE[i, 3]) / 2) for i in range(2)]
EVEN = [[float((TABLE[i, k] - TABLE[i, 3 - k]) / 2) for k in range(2)] for i in range(2)]


def derivative(q):
    outer, inner = q[0] - q[3], q[1] - q[2]
    bend = (q[0] + q[3]) - (q[1] + q[2])
    odd = [ODD[i] * bend for i in range(2)]
    even = [EVEN[i][0] * outer + EVEN[i][1] * inner for i in range(2)]
    return [even[0] + odd[0], even[1] + odd[1], even[1] - odd[1], even[0] - odd[0]]


def two_parts(x):
    high = x.astype(BF16)
    return high, (x - high.astype(F32)).astype(BF16)


def kernel(ngx, ngy, state, wind_x, wind_y, mass, inv_mass, span_of, inverse, coupling, out,
           raw, raw_wx, raw_wy, raw_span, raw_inv, raw_coup, st, fld, wxe, wye, grid, sx, sy, rx, ry, rc, fin,
           a0, a1, a2s, a2r, b0, b1, b2r, kt, bt, vt, xt, kp, bp, vp, xp,
           load_sem, hs, hr, a1s_sem, a1r_sem, a2s_sem, a2r_sem, b1s_sem, b1r_sem, b2s_sem, b2r_sem):
    gx, gy = lax.axis_index("gx"), lax.axis_index("gy")
    devices = ngx * ngy

    loads = [
        pltpu.make_async_copy(src, dst, load_sem.at[n])
        for n, (src, dst) in enumerate((
            (inverse, raw_inv), (wind_x, raw_wx), (wind_y, raw_wy), (state, raw), (coupling, raw_coup), (span_of, raw_span)))
    ]
    for load in loads:
        load.start()

    barrier = pltpu.get_barrier_semaphore()

    def at(dx, dy):
        return (lax.rem(gx + (dx + ngx), ngx), lax.rem(gy + (dy + ngy), ngy))

    for d in range(1, ngy):
        pl.semaphore_signal(barrier, inc=1, device_id=at(0, d), device_id_type=MESH)
    for d in range(1, ngx):
        pl.semaphore_signal(barrier, inc=1, device_id=at(d, 0), device_id_type=MESH)
    for dx in (-1, 1):
        for dy in (-1, 1):
            pl.semaphore_signal(barrier, inc=1, device_id=at(dx, dy), device_id_type=MESH)

    def a_first(d):
        return pltpu.make_async_remote_copy(
            src_ref=a0.at[lax.rem(gy + d, ngy)], dst_ref=a1.at[gy],
            send_sem=a1s_sem.at[d], recv_sem=a1r_sem.at[d],
            device_id=at(0, d), device_id_type=MESH)

    def a_second(d):
        return pltpu.make_async_remote_copy(
            src_ref=a2s.at[lax.rem(gx + d, ngx)], dst_ref=a2r.at[gx],
            send_sem=a2s_sem.at[d], recv_sem=a2r_sem.at[d],
            device_id=at(d, 0), device_id_type=MESH)

    def b_first(d):
        return pltpu.make_async_remote_copy(
            src_ref=b0.at[lax.rem(gx + d, ngx)], dst_ref=b1.at[gx],
            send_sem=b1s_sem.at[d], recv_sem=b1r_sem.at[d],
            device_id=at(d, 0), device_id_type=MESH)

    def b_second(d):
        return pltpu.make_async_remote_copy(
            src_ref=b1.at[:, lax.rem(gy + d, ngy)], dst_ref=b2r.at[gy],
            send_sem=b2s_sem.at[d], recv_sem=b2r_sem.at[d],
            device_id=at(0, d), device_id_type=MESH)

    def weighted(h, k, field):
        def body(ey, carry):
            lines = []
            for ex in range(EX):
                f = [[field(h, ex * NP + i, ey, j) for j in range(NP)] for i in range(NP)]
                along_x = [derivative([f[i][j] for i in range(NP)]) for j in range(NP)]
                along_y = [derivative(f[i]) for i in range(NP)]
                w = []
                for i in range(NP):
                    row = []
                    for j in range(NP):
                        x, y = ex * NP + i, ey * NP + j
                        node = pl.ds(pl.multiple_of((x * NY + y) * 8, 8), 8)
                        flow = wxe[h, node, :] * along_x[j][i] + wye[h, node, :] * along_y[i][j]
                        row.append(mass[x, y] * flow)
                    w.append(row)
                if lines:
                    lines[-1] = [a + b for a, b in zip(lines[-1], w[0])]
                    lines += w[1:]
                else:
                    lines = w
            for X in range(UX):
                values = [carry[X] + lines[X][0], lines[X][1], lines[X][2]]
                for j in range(3):
                    grid[k % 2, h, X, ey * 3 + j] = values[j]
                    if X == 0:
                        sx[k, h, 0, ey * 3 + j] = values[j]
                    if X == UX - 1:
                        sx[k, h, 1, ey * 3 + j] = values[j]
            return tuple(lines[X][3] for X in range(UX))

        carry = lax.fori_loop(0, EY, body, (jnp.zeros((8, 128), F32),) * UX)
        for X in range(UX):
            grid[k % 2, h, X, UY - 1] = carry[X]
            sy[k, h, 1, X] = carry[X]
            sy[k, h, 0, X] = grid[k % 2, h, X, 0]
        sx[k, h, 0, UY - 1] = carry[0]
        sx[k, h, 1, UY - 1] = carry[UX - 1]

    def halo(h, k):
        if k < 2:
            moves = [
                (sx.at[k, h, 1, UY - 1], rc.at[k, h, 0], (1, 1)),
                (sx.at[k, h, 1, 0], rc.at[k, h, 1], (1, -1)),
                (sx.at[k, h, 0, UY - 1], rc.at[k, h, 2], (-1, 1)),
                (sx.at[k, h, 0, 0], rc.at[k, h, 3], (-1, -1)),
                (sy.at[k, h, 1], ry.at[k, h, 0], (0, 1)),
                (sy.at[k, h, 0], ry.at[k, h, 1], (0, -1)),
                (sx.at[k, h, 1], rx.at[k, h, 0], (1, 0)),
                (sx.at[k, h, 0], rx.at[k, h, 1], (-1, 0)),
            ]
        else:
            moves = [
                (sx.at[k, h, 1, UY - 1], rc.at[k, h, 0], (1, 1)),
                (sy.at[k, h, 1, pl.ds(0, UX - 1)], ry.at[k, h, 0, pl.ds(0, UX - 1)], (0, 1)),
                (sx.at[k, h, 1, pl.ds(0, UY - 1)], rx.at[k, h, 0, pl.ds(0, UY - 1)], (1, 0)),
            ]
        return [
            pltpu.make_async_remote_copy(
                src_ref=src, dst_ref=dst, send_sem=hs.at[k, h, n], recv_sem=hr.at[k, h, n],
                device_id=at(*offset), device_id_type=MESH)
            for n, (src, dst, offset) in enumerate(moves)
        ]

    def arrive(h, k):
        for move in halo(h, k):
            move.wait_recv()
        g = grid.at[k % 2, h]
        g[0] += rx[k, h, 0]
        g[UX - 1] += rx[k, h, 1]
        g[:, 0] += ry[k, h, 0]
        g[:, UY - 1] += ry[k, h, 1]
        g[0, 0] += rc[k, h, 0]
        g[0, UY - 1] += rc[k, h, 1]
        g[UX - 1, 0] += rc[k, h, 2]
        g[UX - 1, UY - 1] += rc[k, h, 3]

    def edge(h, k, x, ey, j):
        return grid[k % 2, h, x - x // NP, ey * 3 + j]

    def initial(h, x, ey, j):
        return st[h, x, ey * NP + j]

    def first(h, x, ey, j):
        y = ey * NP + j
        value = st[h, x, y] - (STEP * inv_mass[x, y]) * edge(h, 0, x, ey, j)
        fld[h, x, y] = value
        return value

    def second(h, x, ey, j):
        y = ey * NP + j
        value = 0.75 * st[h, x, y] + 0.25 * fld[h, x, y] - (0.25 * STEP * inv_mass[x, y]) * edge(h, 1, x, ey, j)
        fld[h, x, y] = value
        return value

    def final(h, lines):
        def body(ey, carry):
            for X in lines:
                for j in range(3):
                    x, y = X + X // 3, ey * NP + j
                    value = (1.0 / 3.0) * st[h, x, y] + (2.0 / 3.0) * fld[h, x, y]
                    value = value - (2.0 / 3.0 * STEP * inv_mass[x, y]) * edge(h, 2, x, ey, j)
                    row = (X * EY + ey) * 3 + j
                    fin[h, pl.ds(pl.multiple_of(row * 8, 8), 8), :] = value
            return carry

        lax.fori_loop(0, EY, body, 0)

    def go(h, k):
        moves = halo(h, k)
        for move in moves:
            move.start()
        return moves

    def sent(moves):
        for move in moves:
            move.wait_send()

    def repack(s, carry):
        for g in range(ngy):
            a2s[s, g * 8:(g + 1) * 8, :] = a1[g, pl.ds(pl.multiple_of(s * 8, 8), 8), :]
            a2s[s, ngy * 8 + g:ngy * 8 + g + 1, :] = a1[g, pl.ds(ngx * 8 + s, 1), :]
        return carry

    def gather(h, slots):
        chosen = sum(
            jnp.dot(picks[h], part, preferred_element_type=F32) for part in two_parts(jnp.concatenate(slots, axis=1)))
        for j in range(4):
            block = chosen[:, j * 128:(j + 1) * 128]
            rows = slice((4 * h + j) * 128, (4 * h + j + 1) * 128)
            bt[rows, :] = block[SKIP:].T
            bp[rows, :] = jnp.concatenate([block[:32]] * 4, axis=0).T

    level = lax.rem(lax.broadcasted_iota(jnp.int32, (128, 128), 0), 64)
    target = lax.broadcasted_iota(jnp.int32, (128, 128), 1) // 32
    for n, (raw_w, wide_w) in enumerate(((raw_wx, wxe), (raw_wy, wye))):
        loads[1 + n].wait()
        w = raw_w[...].reshape(NX * NY, 64)
        high = w.astype(BF16).astype(F32)
        parts = jnp.concatenate([high, w - high], axis=1).astype(BF16)
        for i in range(16):
            spreader = (level == target + 4 * i).astype(BF16)
            value = jnp.dot(parts, spreader, preferred_element_type=F32)
            wide_w[i // 8, pl.ds(i % 8, NX * NY, stride=8), :] = value

    loads[3].wait()

    def turn(n, carry):
        x, y8 = n // (NY // 8), lax.rem(n, NY // 8)
        for h in range(2):
            block = raw[x, pl.ds(pl.multiple_of(y8 * 8, 8), 8), 1024 * h:1024 * (h + 1)]
            st[h, x, pl.ds(y8 * 8, 8)] = block.reshape(8, 8, 128)
        return carry

    lax.fori_loop(0, NX * NY // 8, turn, 0)

    for h in range(2):
        fin[h, SKIP * 8:LINE * 8, :] = jnp.zeros(((LINE - SKIP) * 8, 128), F32)
    weighted(0, 0, initial)
    pl.semaphore_wait(barrier, ngy - 1 + ngx - 1 + 4)
    m00 = go(0, 0)
    loads[0].wait()

    def pack(s, carry):
        upper_half = lax.broadcasted_iota(jnp.int32, (8, 128), 0) < 4
        for four in range(ngy // 4):
            rows = pl.ds(pl.multiple_of(s * (2 * ngy) + four * 8, 8), 8)
            block = raw_inv[rows, :].reshape(8, 8, 128)
            for q in range(4):
                one, two = block[2 * q], block[2 * q + 1]
                a0[four * 4 + q, pl.ds(pl.multiple_of(s * 8, 8), 8), :] = jnp.where(upper_half, one, pltpu.roll(two, 4, 0))
                b0[s, four * 4 + q] = jnp.where(upper_half, pltpu.roll(one, 4, 0), two)
        return carry

    lax.fori_loop(0, ngx, pack, 0)
    for d in range(1, 8):
        b_first(d).start()
    b1[gx] = b0[gx]
    weighted(1, 0, initial)
    m10 = go(1, 0)
    for d in range(8, 16):
        b_first(d).start()
    across = (((1,), (1,)), ((), ()))
    loads[4].wait()
    slot = lax.broadcasted_iota(jnp.int32, (3, 2 * devices), 1)
    rows = jnp.concatenate(
        [jnp.where(lax.rem(slot, 2) == r, raw_coup[...], 0.0) for r in range(2)] + [jnp.zeros((122, 2 * devices), F32)], axis=0)
    owner = lax.broadcasted_iota(jnp.int32, (devices, 2 * devices), 0)
    slot = lax.broadcasted_iota(jnp.int32, (devices, 2 * devices), 1)
    chooser = (slot // 2 == owner).astype(BF16)
    both = sum(lax.dot_general(chooser, part, across, preferred_element_type=F32) for part in two_parts(rows))
    both = both.reshape(ngx, ngy, 128)
    for s in range(ngy):
        a0[s, ngx * 8:, :] = both[:, s, :]

    for d in range(1, 8):
        a_first(d).start()
    a1[gy] = a0[gy]
    loads[5].wait()
    earlier = (lax.broadcasted_iota(jnp.int32, (COLS, COLS), 1) < lax.broadcasted_iota(jnp.int32, (COLS, COLS), 0)).astype(BF16)
    itself = (lax.broadcasted_iota(jnp.int32, (COLS, COLS), 1) == lax.broadcasted_iota(jnp.int32, (COLS, COLS), 0)).astype(BF16)
    span = lax.broadcasted_iota(jnp.int32, (devices, COLS), 0)
    picks = []
    for order in (span, lax.rem(span, ngx) * ngy + span // ngx):
        named = (raw_span[...] == order).astype(BF16)
        chosen = lax.dot_general(itself, named, across, preferred_element_type=F32)
        count = lax.dot_general(earlier, named, across, preferred_element_type=F32)
        picks.append(jnp.concatenate(
            [jnp.where(count < 0.5, chosen, 0.0), jnp.where(count < 0.5, 0.0, chosen)], axis=1).astype(BF16))

    arrive(0, 0)
    weighted(0, 1, first)
    m01 = go(0, 1)
    arrive(1, 0)
    weighted(1, 1, first)
    m11 = go(1, 1)
    for d in range(1, ngx):
        b_first(d).wait_recv()
    for d in range(1, 8):
        b_second(d).start()
    b2r[gy] = b1[:, gy]
    for d in range(1, ngy):
        a_first(d).wait_recv()
    lax.fori_loop(0, ngx, repack, 0)
    a2r[gx] = a2s[gx]
    for d in range(1, 16):
        a_second(d).start()
    arrive(0, 1)
    weighted(0, 2, second)
    m02 = go(0, 2)
    arrive(1, 1)
    weighted(1, 2, second)
    m12 = go(1, 2)
    last = [m02, m12]
    def solve(h, count, blocks, values, solved):
        def body(n, carry):
            blk, four = 2 * h + n // 4, lax.rem(n, 4)
            rows = blocks[pl.ds(pl.multiple_of(blk * 256 + four * 64, 8), 64), :]
            for tt in range(count):
                v = [values[pl.ds(pl.multiple_of(((blk * 16 + b) * count + tt) * 8, 8), 8), :] for b in range(16)]
                for a in range(4):
                    total = None
                    for b in range(16):
                        term = rows[a * 16 + b:a * 16 + b + 1, :] * v[b]
                        total = term if total is None else total + term
                    solved[pl.ds(pl.multiple_of(((blk * 16 + four * 4 + a) * count + tt) * 8, 8), 8), :] = total
            return carry

        lax.fori_loop(0, 8, body, 0)

    def sweep(tt, count, blocks, strengths, solved):
        def level(blk, a):
            return pl.ds(pl.multiple_of(((blk * 16 + a) * count + tt) * 8, 8), 8)

        def entry(blk, a, b):
            return blocks[blk * 256 + a * 16 + b:blk * 256 + a * 16 + b + 1, :]

        head = [solved[level(b, 0), :] for b in range(NB)]
        tail = [solved[level(b, 15), :] for b in range(NB)]
        strength = [strengths[b:b + 1, :] for b in range(NB - 1)]
        now_head, now_tail = head, tail
        for n in range(SWEEPS):
            upper = [strength[b] * now_head[b + 1] for b in range(NB - 1)] + [None]
            lower = [None] + [strength[b] * now_tail[b] for b in range(NB - 1)]
            if n < SWEEPS - 1:
                now_head, now_tail = list(head), list(tail)
                for b in range(NB):
                    for a, now in ((0, now_head), (15, now_tail)):
                        if upper[b] is not None:
                            now[b] = now[b] + entry(b, a, 15) * upper[b]
                        if lower[b] is not None:
                            now[b] = now[b] + entry(b, a, 0) * lower[b]
        for b in range(NB):
            for a in range(16):
                value = solved[level(b, a), :]
                if upper[b] is not None:
                    value = value + entry(b, a, 15) * upper[b]
                if lower[b] is not None:
                    value = value + entry(b, a, 0) * lower[b]
                solved[level(b, a), :] = value

    quarter = lax.broadcasted_iota(jnp.int32, (8, 128), 1) // 32

    def lay_many(h):
        for s in range(8):
            vt[(8 * h + s) * 128:(8 * h + s + 1) * 128, :] = fin[h, pl.ds(SKIP * 8 + s, 128, stride=8), :].T

    def lay_few(h):
        for s in range(8):
            four = jnp.concatenate([fin[h, pl.ds(s, 32, stride=8), :]] * 4, axis=0).T
            for g in range(4):
                value = four[g * 32:g * 32 + 8]
                for q in range(1, 4):
                    value = jnp.where(quarter == q, four[g * 32 + q * 8:g * 32 + q * 8 + 8], value)
                vp[((8 * h + s) * 4 + g) * 8:((8 * h + s) * 4 + g + 1) * 8, :] = value

    def take_many(s):
        turned = xt[s * 128:(s + 1) * 128, :].T
        out[LINE:, s * 128:(s + 1) * 128] = turned[LINE - SKIP:]

    eighth = lax.rem(lax.broadcasted_iota(jnp.int32, (LINE, 128), 1) // 8, 4)

    def take_few(s):
        turned = jnp.concatenate([xp[(s * 4 + g) * 8:(s * 4 + g + 1) * 8, :] for g in range(4) for q in range(4)], axis=0).T
        value = turned[:LINE]
        for q in range(1, 4):
            value = jnp.where(eighth == q, turned[q * 32:q * 32 + LINE], value)
        out[:LINE, s * 128:(s + 1) * 128] = value

    def sweep_many(tt, carry):
        sweep(tt, 4, bt, kt, xt)
        return carry

    for d in range(1, ngy):
        b_second(d).wait_recv()
    gather(1, [
        jnp.concatenate([b2r[g, pl.ds(0, ngx), r * 4 + j, :] for r in range(2) for g in range(ngy)], axis=0)
        for j in range(4)])
    for d in range(1, ngx):
        a_second(d).wait_recv()
    gather(0, [
        jnp.concatenate([a2r[g, pl.ds(r * 4 + j, ngy, stride=8), :] for r in range(2) for g in range(ngx)], axis=0)
        for j in range(4)])

    links = jnp.concatenate([a2r[g, ngy * 8:ngy * 8 + ngy, :] for g in range(ngx)], axis=0)
    links = jnp.concatenate([links, pltpu.roll(links, 125, 1)], axis=0)
    strength = sum(jnp.dot(picks[0], part, preferred_element_type=F32) for part in two_parts(links))
    kt[...] = strength[SKIP:].T
    kp[...] = jnp.concatenate([strength[:32]] * 4, axis=0).T

    for h in range(2):
        last[h][1].wait_recv()
        grid[0, h, 0:UX - 1, 0] += ry[2, h, 0, 0:UX - 1]
        final(h, range(1, UX - 1))
        lay_many(h)
    solve(0, 4, bt, vt, xt)
    solve(1, 4, bt, vt, xt)
    lax.fori_loop(0, 4, sweep_many, 0)
    for s in range(16):
        take_many(s)
    for h in range(2):
        last[h][0].wait_recv()
        last[h][2].wait_recv()
        grid[0, h, 0, 0] += rc[2, h, 0]
        grid[0, h, 0, 0:UY - 1] += rx[2, h, 0, 0:UY - 1]
        final(h, range(1))
        lay_few(h)
        solve(h, 1, bp, vp, xp)
    sweep(0, 1, bp, kp, xp)
    for s in range(16):
        take_few(s)

    for d in range(1, ngy):
        a_first(d).wait_send()
        b_second(d).wait_send()
    for d in range(1, ngx):
        a_second(d).wait_send()
        b_first(d).wait_send()
    for k in range(3):
        for h in range(2):
            for move in halo(h, k):
                move.wait_send()


def on_device(ngx, ngy, state, wind_x, wind_y, mass, inv_mass, span_of, block_inverse, coupling):
    width = state.shape[2]
    any_ = pl.BlockSpec(memory_space=pl.ANY)
    smem = pl.BlockSpec(memory_space=pltpu.SMEM)
    nodes = (2, NX, NY, 8, 128)
    vmem = pltpu.VMEM
    dma = pltpu.SemaphoreType.DMA
    span_of, coupling = span_of.T, coupling.T
    return pl.pallas_call(
        functools.partial(kernel, ngx, ngy),
        out_shape=pltpu.VMEM((COLS, width), F32),
        in_specs=[any_, any_, any_, smem, smem, any_, any_, any_],
        out_specs=pl.BlockSpec(memory_space=pltpu.VMEM),
        scratch_shapes=[
            vmem(state.shape, F32), vmem(wind_x.shape, F32), vmem(wind_y.shape, F32), vmem(span_of.shape, jnp.int32),
            vmem(block_inverse.shape, F32), vmem(coupling.shape, F32),
            vmem(nodes, F32), vmem(nodes, F32),
            vmem((2, NX * NY * 8, 128), F32), vmem((2, NX * NY * 8, 128), F32),
            vmem((2, 2, UX, UY, 8, 128), F32),
            vmem((3, 2, 2, UY, 8, 128), F32), vmem((3, 2, 2, UX, 8, 128), F32),
            vmem((3, 2, 2, UY, 8, 128), F32), vmem((3, 2, 2, UX, 8, 128), F32), vmem((3, 2, 4, 8, 128), F32),
            vmem((2, COLS * 8, 128), F32),
            vmem((ngy, ngx * 9, 128), F32), vmem((ngy, ngx * 9, 128), F32),
            vmem((ngx, ngy * 9, 128), F32), vmem((ngx, ngy * 9, 128), F32),
            vmem((ngx, ngy, 8, 128), F32), vmem((ngx, ngy, 8, 128), F32), vmem((ngy, ngx, 8, 128), F32),
            vmem((128, 128), F32), vmem((1024, 128), F32), vmem((2048, 128), F32), vmem((2048, 128), F32),
            vmem((128, 128), F32), vmem((1024, 128), F32), vmem((512, 128), F32), vmem((512, 128), F32),
            dma((6,)), dma((3, 2, 8)), dma((3, 2, 8)),
            dma((ngy,)), dma((ngy,)), dma((ngx,)), dma((ngx,)),
            dma((ngx,)), dma((ngx,)), dma((ngy,)), dma((ngy,)),
        ],
        compiler_params=pltpu.CompilerParams(
            collective_id=0, has_side_effects=True, vmem_limit_bytes=60 * 2**20),
    )(state, wind_x, wind_y, mass, inv_mass, span_of, block_inverse, coupling)


def solution(mesh):
    placed = (
        P("gx", "gy", None),
        P("gx", "gy", None),
        P("gx", "gy", None),
        P("gx", "gy"),
        P("gx", "gy"),
        P(("gx", "gy"), None),
        P(("gx", "gy"), None),
        P(("gx", "gy"), None),
    )
    return jax.shard_map(
        functools.partial(on_device, mesh.shape["gx"], mesh.shape["gy"]),
        mesh=mesh, in_specs=placed, out_specs=P(("gx", "gy"), None), check_vma=False,
    )
```

```python
import functools

import jax
import jax.numpy as jnp
import numpy as np
from jax import lax
from jax.experimental import pallas as pl
from jax.experimental.pallas import tpu as pltpu
from jax.sharding import PartitionSpec as P

NP = 4
NB = 4
SWEEPS = 3
STEP = 0.05
EX = 2
EY = 8
NX = EX * NP
NY = EY * NP
UX = EX * 3 + 1
UY = EY * 3 + 1
COLS = EX * 3 * EY * 3
LINE = EY * 3
SKIP = COLS - 128
MESH = pl.DeviceIdType.MESH
F32 = jnp.float32
BF16 = jnp.bfloat16


def derivative_table():
    points = np.array([-1.0, -1.0 / np.sqrt(5.0), 1.0 / np.sqrt(5.0), 1.0])
    count = points.shape[0]
    weights = np.ones(count)
    for i in range(count):
        for m in range(count):
            if m != i:
                weights[i] = weights[i] * (points[i] - points[m])
    table = np.zeros((count, count))
    for i in range(count):
        for j in range(count):
            if i != j:
                table[i, j] = weights[i] / weights[j] / (points[i] - points[j])
                table[i, i] = table[i, i] + 1.0 / (points[i] - points[j])
    return table


TABLE = derivative_table()
ODD = [float((TABLE[i, 0] + TABLE[i, 3]) / 2) for i in range(2)]
EVEN = [[float((TABLE[i, k] - TABLE[i, 3 - k]) / 2) for k in range(2)] for i in range(2)]


def derivative(q):
    outer, inner = q[0] - q[3], q[1] - q[2]
    bend = (q[0] + q[3]) - (q[1] + q[2])
    odd = [ODD[i] * bend for i in range(2)]
    even = [EVEN[i][0] * outer + EVEN[i][1] * inner for i in range(2)]
    return [even[0] + odd[0], even[1] + odd[1], even[1] - odd[1], even[0] - odd[0]]


def two_parts(x):
    high = x.astype(BF16)
    return high, (x - high.astype(F32)).astype(BF16)


def kernel(ngx, ngy, state, wind_x, wind_y, mass, inv_mass, span_of, inverse, coupling, out,
           raw, raw_wx, raw_wy, raw_span, raw_inv, raw_coup, st, fld, wxe, wye, grid, sx, sy, rx, ry, rc, fin,
           a0, a1, a2s, a2r, b0, b1, b2r, kt, bt, vt, xt, kp, bp, vp, xp,
           load_sem, hs, hr, a1s_sem, a1r_sem, a2s_sem, a2r_sem, b1s_sem, b1r_sem, b2s_sem, b2r_sem):
    gx, gy = lax.axis_index("gx"), lax.axis_index("gy")
    devices = ngx * ngy

    loads = [
        pltpu.make_async_copy(src, dst, load_sem.at[n])
        for n, (src, dst) in enumerate((
            (wind_x, raw_wx), (wind_y, raw_wy), (state.at[:, :, :1024], raw.at[:, :, :1024]), (state.at[:, :, 1024:], raw.at[:, :, 1024:]),
            (inverse, raw_inv), (coupling, raw_coup), (span_of, raw_span)))
    ]
    for load in loads:
        load.start()

    barrier = pltpu.get_barrier_semaphore()

    def at(dx, dy):
        return (lax.rem(gx + (dx + ngx), ngx), lax.rem(gy + (dy + ngy), ngy))

    for d in range(1, ngy):
        pl.semaphore_signal(barrier, inc=1, device_id=at(0, d), device_id_type=MESH)
    for d in range(1, ngx):
        pl.semaphore_signal(barrier, inc=1, device_id=at(d, 0), device_id_type=MESH)
    for dx in (-1, 1):
        for dy in (-1, 1):
            pl.semaphore_signal(barrier, inc=1, device_id=at(dx, dy), device_id_type=MESH)

    def a_first(d):
        return pltpu.make_async_remote_copy(
            src_ref=a0.at[lax.rem(gy + d, ngy)], dst_ref=a1.at[gy],
            send_sem=a1s_sem.at[d], recv_sem=a1r_sem.at[d],
            device_id=at(0, d), device_id_type=MESH)

    def a_second(d):
        return pltpu.make_async_remote_copy(
            src_ref=a2s.at[lax.rem(gx + d, ngx)], dst_ref=a2r.at[gx],
            send_sem=a2s_sem.at[d], recv_sem=a2r_sem.at[d],
            device_id=at(d, 0), device_id_type=MESH)

    def b_first(d):
        return pltpu.make_async_remote_copy(
            src_ref=b0.at[lax.rem(gx + d, ngx)], dst_ref=b1.at[gx],
            send_sem=b1s_sem.at[d], recv_sem=b1r_sem.at[d],
            device_id=at(d, 0), device_id_type=MESH)

    def b_second(d):
        return pltpu.make_async_remote_copy(
            src_ref=b1.at[:, lax.rem(gy + d, ngy)], dst_ref=b2r.at[gy],
            send_sem=b2s_sem.at[d], recv_sem=b2r_sem.at[d],
            device_id=at(0, d), device_id_type=MESH)

    def weighted(h, k, field):
        def body(ey, carry):
            lines = []
            for ex in range(EX):
                f = [[field(h, ex * NP + i, ey, j) for j in range(NP)] for i in range(NP)]
                along_x = [derivative([f[i][j] for i in range(NP)]) for j in range(NP)]
                along_y = [derivative(f[i]) for i in range(NP)]
                w = []
                for i in range(NP):
                    row = []
                    for j in range(NP):
                        x, y = ex * NP + i, ey * NP + j
                        node = pl.ds(pl.multiple_of((x * NY + y) * 8, 8), 8)
                        flow = wxe[h, node, :] * along_x[j][i] + wye[h, node, :] * along_y[i][j]
                        row.append(mass[x, y] * flow)
                    w.append(row)
                if lines:
                    lines[-1] = [a + b for a, b in zip(lines[-1], w[0])]
                    lines += w[1:]
                else:
                    lines = w
            for X in range(UX):
                values = [carry[X] + lines[X][0], lines[X][1], lines[X][2]]
                for j in range(3):
                    grid[k % 2, h, X, ey * 3 + j] = values[j]
                    if X == 0:
                        sx[k, h, 0, ey * 3 + j] = values[j]
                    if X == UX - 1:
                        sx[k, h, 1, ey * 3 + j] = values[j]
            return tuple(lines[X][3] for X in range(UX))

        carry = lax.fori_loop(0, EY, body, (jnp.zeros((8, 128), F32),) * UX)
        for X in range(UX):
            grid[k % 2, h, X, UY - 1] = carry[X]
            sy[k, h, 1, X] = carry[X]
            sy[k, h, 0, X] = grid[k % 2, h, X, 0]
        sx[k, h, 0, UY - 1] = carry[0]
        sx[k, h, 1, UY - 1] = carry[UX - 1]

    def halo(h, k):
        if k < 2:
            moves = [
                (sx.at[k, h, 1, UY - 1], rc.at[k, h, 0], (1, 1)),
                (sx.at[k, h, 1, 0], rc.at[k, h, 1], (1, -1)),
                (sx.at[k, h, 0, UY - 1], rc.at[k, h, 2], (-1, 1)),
                (sx.at[k, h, 0, 0], rc.at[k, h, 3], (-1, -1)),
                (sy.at[k, h, 1], ry.at[k, h, 0], (0, 1)),
                (sy.at[k, h, 0], ry.at[k, h, 1], (0, -1)),
                (sx.at[k, h, 1], rx.at[k, h, 0], (1, 0)),
                (sx.at[k, h, 0], rx.at[k, h, 1], (-1, 0)),
            ]
        else:
            moves = [
                (sx.at[k, h, 1, UY - 1], rc.at[k, h, 0], (1, 1)),
                (sy.at[k, h, 1, pl.ds(0, UX - 1)], ry.at[k, h, 0, pl.ds(0, UX - 1)], (0, 1)),
                (sx.at[k, h, 1, pl.ds(0, UY - 1)], rx.at[k, h, 0, pl.ds(0, UY - 1)], (1, 0)),
            ]
        return [
            pltpu.make_async_remote_copy(
                src_ref=src, dst_ref=dst, send_sem=hs.at[k, h, n], recv_sem=hr.at[k, h, n],
                device_id=at(*offset), device_id_type=MESH)
            for n, (src, dst, offset) in enumerate(moves)
        ]

    def arrive(h, k):
        for move in halo(h, k):
            move.wait_recv()
        g = grid.at[k % 2, h]
        g[0] += rx[k, h, 0]
        g[UX - 1] += rx[k, h, 1]
        g[:, 0] += ry[k, h, 0]
        g[:, UY - 1] += ry[k, h, 1]
        g[0, 0] += rc[k, h, 0]
        g[0, UY - 1] += rc[k, h, 1]
        g[UX - 1, 0] += rc[k, h, 2]
        g[UX - 1, UY - 1] += rc[k, h, 3]

    def edge(h, k, x, ey, j):
        return grid[k % 2, h, x - x // NP, ey * 3 + j]

    def initial(h, x, ey, j):
        return st[h, x, ey * NP + j]

    def first(h, x, ey, j):
        y = ey * NP + j
        value = st[h, x, y] - (STEP * inv_mass[x, y]) * edge(h, 0, x, ey, j)
        fld[h, x, y] = value
        return value

    def second(h, x, ey, j):
        y = ey * NP + j
        value = 0.75 * st[h, x, y] + 0.25 * fld[h, x, y] - (0.25 * STEP * inv_mass[x, y]) * edge(h, 1, x, ey, j)
        fld[h, x, y] = value
        return value

    def third(h, x, ey, j):
        y = ey * NP + j
        value = (1.0 / 3.0) * st[h, x, y] + (2.0 / 3.0) * fld[h, x, y]
        return value - (2.0 / 3.0 * STEP * inv_mass[x, y]) * edge(h, 2, x, ey, j)

    def final(h, lines):
        def body(ey, carry):
            for X in lines:
                for j in range(3):
                    row = (X * EY + ey) * 3 + j
                    fin[h, pl.ds(pl.multiple_of(row * 8, 8), 8), :] = third(h, X + X // 3, ey, j)
            return carry

        lax.fori_loop(0, EY, body, 0)

    def go(h, k):
        moves = halo(h, k)
        for move in moves:
            move.start()
        return moves

    def repack(s, carry):
        for g in range(ngy):
            a2s[s, g * 8:(g + 1) * 8, :] = a1[g, pl.ds(pl.multiple_of(s * 8, 8), 8), :]
            a2s[s, ngy * 8 + g:ngy * 8 + g + 1, :] = a1[g, pl.ds(ngx * 8 + s, 1), :]
        return carry

    def gather(h, slots):
        source = two_parts(jnp.concatenate(slots, axis=1))
        many = sum(jnp.dot(picks[h][SKIP:], part, preferred_element_type=F32) for part in source)
        few = sum(jnp.dot(late_picks[h], part, preferred_element_type=F32) for part in source)
        for j in range(4):
            rows = slice((4 * h + j) * 128, (4 * h + j + 1) * 128)
            bt[rows, :] = many[:, j * 128:(j + 1) * 128].T
            bp[rows, :] = few[:, j * 128:(j + 1) * 128].T

    level = lax.rem(lax.broadcasted_iota(jnp.int32, (128, 128), 0), 64)
    target = lax.broadcasted_iota(jnp.int32, (128, 128), 1) // 32
    loads[0].wait()
    loads[1].wait()
    winds = []
    for raw_w in (raw_wx, raw_wy):
        w = raw_w[...].reshape(NX * NY, 64)
        high = w.astype(BF16).astype(F32)
        winds.append(jnp.concatenate([high, w - high], axis=1).astype(BF16))

    def spread_winds(h):
        for parts, wide_w in zip(winds, (wxe, wye)):
            for i in range(8):
                spreader = (level == target + 4 * (8 * h + i)).astype(BF16)
                value = jnp.dot(parts, spreader, preferred_element_type=F32)
                wide_w[h, pl.ds(i, NX * NY, stride=8), :] = value

    def turn(h):
        loads[2 + h].wait()

        def body(n, carry):
            x, y8 = n // (NY // 8), lax.rem(n, NY // 8)
            block = raw[x, pl.ds(pl.multiple_of(y8 * 8, 8), 8), 1024 * h:1024 * (h + 1)]
            st[h, x, pl.ds(y8 * 8, 8)] = block.reshape(8, 8, 128)
            return carry

        lax.fori_loop(0, NX * NY // 8, body, 0, unroll=2)

    for h in range(2):
        fin[h, SKIP * 8:LINE * 8, :] = jnp.zeros(((LINE - SKIP) * 8, 128), F32)
        fin[h, COLS * 8:, :] = jnp.zeros(((LINE * 9 + 1 - COLS) * 8, 128), F32)
    spread_winds(0)
    turn(0)
    weighted(0, 0, initial)
    pl.semaphore_wait(barrier, ngy - 1 + ngx - 1 + 4)
    go(0, 0)
    loads[4].wait()

    def pack(s, carry):
        upper_half = lax.broadcasted_iota(jnp.int32, (8, 128), 0) < 4
        for four in range(ngy // 4):
            rows = pl.ds(pl.multiple_of(s * (2 * ngy) + four * 8, 8), 8)
            block = raw_inv[rows, :].reshape(8, 8, 128)
            for q in range(4):
                one, two = block[2 * q], block[2 * q + 1]
                a0[four * 4 + q, pl.ds(pl.multiple_of(s * 8, 8), 8), :] = jnp.where(upper_half, one, pltpu.roll(two, 4, 0))
                b0[s, four * 4 + q] = jnp.where(upper_half, pltpu.roll(one, 4, 0), two)
        return carry

    lax.fori_loop(0, ngx, pack, 0)
    for d in range(1, ngx // 2):
        b_first(d).start()
    b1[gx] = b0[gx]
    spread_winds(1)
    turn(1)
    weighted(1, 0, initial)
    go(1, 0)
    for d in range(ngx // 2, ngx):
        b_first(d).start()
    across = (((1,), (1,)), ((), ()))
    loads[5].wait()
    slot = lax.broadcasted_iota(jnp.int32, (3, 2 * devices), 1)
    rows = jnp.concatenate(
        [jnp.where(lax.rem(slot, 2) == r, raw_coup[...], 0.0) for r in range(2)] + [jnp.zeros((122, 2 * devices), F32)], axis=0)
    owner = lax.broadcasted_iota(jnp.int32, (devices, 2 * devices), 0)
    slot = lax.broadcasted_iota(jnp.int32, (devices, 2 * devices), 1)
    chooser = (slot // 2 == owner).astype(BF16)
    both = sum(lax.dot_general(chooser, part, across, preferred_element_type=F32) for part in two_parts(rows))
    both = both.reshape(ngx, ngy, 128)
    for s in range(ngy):
        a0[s, ngx * 8:, :] = both[:, s, :]

    for d in range(1, ngy):
        a_first(d).start()
    a1[gy] = a0[gy]
    loads[6].wait()
    earlier = (lax.broadcasted_iota(jnp.int32, (COLS, COLS), 1) < lax.broadcasted_iota(jnp.int32, (COLS, COLS), 0)).astype(BF16)
    itself = (lax.broadcasted_iota(jnp.int32, (COLS, COLS), 1) == lax.broadcasted_iota(jnp.int32, (COLS, COLS), 0)).astype(BF16)
    span = lax.broadcasted_iota(jnp.int32, (devices, COLS), 0)
    late = lax.rem(lax.broadcasted_iota(jnp.int32, (128, COLS), 0), 32)
    late = jnp.where(late < LINE, late, (late - LINE + 1) * LINE)
    late = (late == lax.broadcasted_iota(jnp.int32, (128, COLS), 1)).astype(BF16)
    picks, late_picks = [], []
    for order in (span, lax.rem(span, ngx) * ngy + span // ngx):
        named = (raw_span[...] == order).astype(BF16)
        chosen = lax.dot_general(itself, named, across, preferred_element_type=F32)
        count = lax.dot_general(earlier, named, across, preferred_element_type=F32)
        picks.append(jnp.concatenate(
            [jnp.where(count < 0.5, chosen, 0.0), jnp.where(count < 0.5, 0.0, chosen)], axis=1).astype(BF16))
        late_picks.append(jnp.dot(late, picks[-1], preferred_element_type=F32).astype(BF16))

    arrive(0, 0)
    weighted(0, 1, first)
    go(0, 1)
    arrive(1, 0)
    weighted(1, 1, first)
    go(1, 1)
    for d in range(1, ngx):
        b_first(d).wait_recv()
    for d in range(1, ngy):
        b_second(d).start()
    b2r[gy] = b1[:, gy]
    for d in range(1, ngy):
        a_first(d).wait_recv()
    lax.fori_loop(0, ngx, repack, 0)
    a2r[gx] = a2s[gx]
    for d in range(1, ngx):
        a_second(d).start()
    arrive(0, 1)
    weighted(0, 2, second)
    last_low = go(0, 2)
    arrive(1, 1)
    weighted(1, 2, second)
    last_high = go(1, 2)
    last = [last_low, last_high]
    def solve(h, count, blocks, values, solved):
        def body(n, carry):
            blk, four = 2 * h + n // 4, lax.rem(n, 4)
            rows = blocks[pl.ds(pl.multiple_of(blk * 256 + four * 64, 8), 64), :]
            for tt in range(count):
                v = [values[pl.ds(pl.multiple_of(((blk * 16 + b) * count + tt) * 8, 8), 8), :] for b in range(16)]
                for a in range(4):
                    total = None
                    for b in range(16):
                        term = rows[a * 16 + b:a * 16 + b + 1, :] * v[b]
                        total = term if total is None else total + term
                    solved[pl.ds(pl.multiple_of(((blk * 16 + four * 4 + a) * count + tt) * 8, 8), 8), :] = total
            return carry

        lax.fori_loop(0, 8, body, 0)

    def sweep(tt, count, blocks, strengths, solved):
        def level(blk, a):
            return pl.ds(pl.multiple_of(((blk * 16 + a) * count + tt) * 8, 8), 8)

        def entry(blk, a, b):
            return blocks[blk * 256 + a * 16 + b:blk * 256 + a * 16 + b + 1, :]

        head = [solved[level(b, 0), :] for b in range(NB)]
        tail = [solved[level(b, 15), :] for b in range(NB)]
        strength = [strengths[b:b + 1, :] for b in range(NB - 1)]
        now_head, now_tail = head, tail
        for n in range(SWEEPS):
            upper = [strength[b] * now_head[b + 1] for b in range(NB - 1)] + [None]
            lower = [None] + [strength[b] * now_tail[b] for b in range(NB - 1)]
            if n < SWEEPS - 1:
                now_head, now_tail = list(head), list(tail)
                for b in range(NB):
                    for a, now in ((0, now_head), (15, now_tail)):
                        if upper[b] is not None:
                            now[b] = now[b] + entry(b, a, 15) * upper[b]
                        if lower[b] is not None:
                            now[b] = now[b] + entry(b, a, 0) * lower[b]
        for b in range(NB):
            for a in range(16):
                value = solved[level(b, a), :]
                if upper[b] is not None:
                    value = value + entry(b, a, 15) * upper[b]
                if lower[b] is not None:
                    value = value + entry(b, a, 0) * lower[b]
                solved[level(b, a), :] = value

    quarter = lax.broadcasted_iota(jnp.int32, (8, 128), 1) // 32

    def lay_many(h):
        for s in range(8):
            vt[(8 * h + s) * 128:(8 * h + s + 1) * 128, :] = fin[h, pl.ds(SKIP * 8 + s, 128, stride=8), :].T

    def lay_few(h):
        for s in range(8):
            four = jnp.concatenate([fin[h, pl.ds(s, LINE, stride=8), :], fin[h, pl.ds(LINE * 8 + s, 8, stride=LINE * 8), :]] * 4, axis=0).T
            for g in range(4):
                value = four[g * 32:g * 32 + 8]
                for q in range(1, 4):
                    value = jnp.where(quarter == q, four[g * 32 + q * 8:g * 32 + q * 8 + 8], value)
                vp[((8 * h + s) * 4 + g) * 8:((8 * h + s) * 4 + g + 1) * 8, :] = value

    def take_many(s):
        turned = xt[s * 128:(s + 1) * 128, :].T
        out[LINE:, s * 128:(s + 1) * 128] = turned[LINE - SKIP:]

    eighth = lax.rem(lax.broadcasted_iota(jnp.int32, (32, 128), 1) // 8, 4)

    def take_few(s):
        turned = jnp.concatenate([xp[(s * 4 + g) * 8:(s * 4 + g + 1) * 8, :] for g in range(4) for q in range(4)], axis=0).T
        value = turned[:32]
        for q in range(1, 4):
            value = jnp.where(eighth == q, turned[q * 32:q * 32 + 32], value)
        out[:LINE, s * 128:(s + 1) * 128] = value[:LINE]
        for n in range(1, UX - 1):
            out[n * LINE:n * LINE + 1, s * 128:(s + 1) * 128] = value[LINE + n - 1:LINE + n]

    def sweep_many(tt, carry):
        sweep(tt, 4, bt, kt, xt)
        return carry

    for d in range(1, ngy):
        b_second(d).wait_recv()
    gather(1, [
        jnp.concatenate([b2r[g, pl.ds(0, ngx), r * 4 + j, :] for r in range(2) for g in range(ngy)], axis=0)
        for j in range(4)])
    for h in range(2):
        final(h, range(1, UX - 1))
        lay_many(h)
    solve(1, 4, bt, vt, xt)
    for d in range(1, ngx):
        a_second(d).wait_recv()
    gather(0, [
        jnp.concatenate([a2r[g, pl.ds(r * 4 + j, ngy, stride=8), :] for r in range(2) for g in range(ngx)], axis=0)
        for j in range(4)])

    links = jnp.concatenate([a2r[g, ngy * 8:ngy * 8 + ngy, :] for g in range(ngx)], axis=0)
    links = two_parts(jnp.concatenate([links, pltpu.roll(links, 125, 1)], axis=0))
    kt[...] = sum(jnp.dot(picks[0][SKIP:], part, preferred_element_type=F32) for part in links).T
    kp[...] = sum(jnp.dot(late_picks[0], part, preferred_element_type=F32) for part in links).T

    solve(0, 4, bt, vt, xt)
    lax.fori_loop(0, 4, sweep_many, 0)
    for s in range(16):
        take_many(s)
    for h in range(2):
        for move in last[h]:
            move.wait_recv()
        grid[0, h, 0:UX - 1, 0] += ry[2, h, 0, 0:UX - 1]
        grid[0, h, 0, 0] += rc[2, h, 0]
        grid[0, h, 0, 0:UY - 1] += rx[2, h, 0, 0:UY - 1]
        final(h, range(1))
        for X in range(1, UX - 1):
            fin[h, X * LINE * 8:X * LINE * 8 + 8, :] = third(h, X + X // 3, 0, 0)
        lay_few(h)
        solve(h, 1, bp, vp, xp)
    sweep(0, 1, bp, kp, xp)
    for s in range(16):
        take_few(s)

    for d in range(1, ngy):
        a_first(d).wait_send()
        b_second(d).wait_send()
    for d in range(1, ngx):
        a_second(d).wait_send()
        b_first(d).wait_send()
    for k in range(3):
        for h in range(2):
            for move in halo(h, k):
                move.wait_send()


def on_device(ngx, ngy, state, wind_x, wind_y, mass, inv_mass, span_of, block_inverse, coupling):
    width = state.shape[2]
    any_ = pl.BlockSpec(memory_space=pl.ANY)
    smem = pl.BlockSpec(memory_space=pltpu.SMEM)
    nodes = (2, NX, NY, 8, 128)
    vmem = pltpu.VMEM
    dma = pltpu.SemaphoreType.DMA
    span_of, coupling = span_of.T, coupling.T
    return pl.pallas_call(
        functools.partial(kernel, ngx, ngy),
        out_shape=pltpu.VMEM((COLS, width), F32),
        in_specs=[any_, any_, any_, smem, smem, any_, any_, any_],
        out_specs=pl.BlockSpec(memory_space=pltpu.VMEM),
        scratch_shapes=[
            vmem(state.shape, F32), vmem(wind_x.shape, F32), vmem(wind_y.shape, F32), vmem(span_of.shape, jnp.int32),
            vmem(block_inverse.shape, F32), vmem(coupling.shape, F32),
            vmem(nodes, F32), vmem(nodes, F32),
            vmem((2, (NX * NY + 1) * 8, 128), F32), vmem((2, (NX * NY + 1) * 8, 128), F32),
            vmem((2, 2, UX, UY, 8, 128), F32),
            vmem((3, 2, 2, UY, 8, 128), F32), vmem((3, 2, 2, UX, 8, 128), F32),
            vmem((3, 2, 2, UY, 8, 128), F32), vmem((3, 2, 2, UX, 8, 128), F32), vmem((3, 2, 4, 8, 128), F32),
            vmem((2, (LINE * 9 + 1) * 8, 128), F32),
            vmem((ngy, ngx * 9, 128), F32), vmem((ngy, ngx * 9, 128), F32),
            vmem((ngx, ngy * 9, 128), F32), vmem((ngx, ngy * 9, 128), F32),
            vmem((ngx, ngy, 8, 128), F32), vmem((ngx, ngy, 8, 128), F32), vmem((ngy, ngx, 8, 128), F32),
            vmem((128, 128), F32), vmem((1024, 128), F32), vmem((2048, 128), F32), vmem((2048, 128), F32),
            vmem((128, 128), F32), vmem((1024, 128), F32), vmem((512, 128), F32), vmem((512, 128), F32),
            dma((7,)), dma((3, 2, 8)), dma((3, 2, 8)),
            dma((ngy,)), dma((ngy,)), dma((ngx,)), dma((ngx,)),
            dma((ngx,)), dma((ngx,)), dma((ngy,)), dma((ngy,)),
        ],
        compiler_params=pltpu.CompilerParams(
            collective_id=0, has_side_effects=True, vmem_limit_bytes=60 * 2**20),
    )(state, wind_x, wind_y, mass, inv_mass, span_of, block_inverse, coupling)


def solution(mesh):
    placed = (
        P("gx", "gy", None),
        P("gx", "gy", None),
        P("gx", "gy", None),
        P("gx", "gy"),
        P("gx", "gy"),
        P(("gx", "gy"), None),
        P(("gx", "gy"), None),
        P(("gx", "gy"), None),
    )
    return jax.shard_map(
        functools.partial(on_device, mesh.shape["gx"], mesh.shape["gy"]),
        mesh=mesh, in_specs=placed, out_specs=P(("gx", "gy"), None), check_vma=False,
    )
```

```python
import functools

import jax
import jax.numpy as jnp
import numpy as np
from jax import lax
from jax.experimental import pallas as pl
from jax.experimental.pallas import tpu as pltpu
from jax.sharding import PartitionSpec as P

NP = 4
NB = 4
SWEEPS = 3
STEP = 0.05
EX = 2
EY = 8
NX = EX * NP
NY = EY * NP
UX = EX * 3 + 1
UY = EY * 3 + 1
COLS = EX * 3 * EY * 3
LINE = EY * 3
SKIP = COLS - 128
MESH = pl.DeviceIdType.MESH
F32 = jnp.float32
BF16 = jnp.bfloat16


def derivative_table():
    points = np.array([-1.0, -1.0 / np.sqrt(5.0), 1.0 / np.sqrt(5.0), 1.0])
    count = points.shape[0]
    weights = np.ones(count)
    for i in range(count):
        for m in range(count):
            if m != i:
                weights[i] = weights[i] * (points[i] - points[m])
    table = np.zeros((count, count))
    for i in range(count):
        for j in range(count):
            if i != j:
                table[i, j] = weights[i] / weights[j] / (points[i] - points[j])
                table[i, i] = table[i, i] + 1.0 / (points[i] - points[j])
    return table


TABLE = derivative_table()
ODD = [float((TABLE[i, 0] + TABLE[i, 3]) / 2) for i in range(2)]
EVEN = [[float((TABLE[i, k] - TABLE[i, 3 - k]) / 2) for k in range(2)] for i in range(2)]


def derivative(q):
    outer, inner = q[0] - q[3], q[1] - q[2]
    bend = (q[0] + q[3]) - (q[1] + q[2])
    odd = [ODD[i] * bend for i in range(2)]
    even = [EVEN[i][0] * outer + EVEN[i][1] * inner for i in range(2)]
    return [even[0] + odd[0], even[1] + odd[1], even[1] - odd[1], even[0] - odd[0]]


def two_parts(x):
    high = x.astype(BF16)
    return high, (x - high.astype(F32)).astype(BF16)


def kernel(ngx, ngy, state, wind_x, wind_y, mass_in, inv_mass_in, span_of, inverse, coupling, out,
           mass, inv_mass, raw, raw_wx, raw_wy, raw_span, raw_inv, raw_coup, st, fld, wxe, wye, grid, sx, sy, rx, ry, rc, fin,
           a0, a1, a2s, a2r, b0, b1, b2r, kt, bt, vt, xt, kp, bp, vp, xp,
           load_sem, hs, hr, a1s_sem, a1r_sem, a2s_sem, a2r_sem, b1s_sem, b1r_sem, b2s_sem, b2r_sem):
    gx, gy = lax.axis_index("gx"), lax.axis_index("gy")
    devices = ngx * ngy

    loads = [
        pltpu.make_async_copy(src, dst, load_sem.at[n])
        for n, (src, dst) in enumerate((
            (wind_x, raw_wx), (wind_y, raw_wy), (state.at[:, :, :1024], raw.at[:, :, :1024]), (state.at[:, :, 1024:], raw.at[:, :, 1024:]),
            (inverse, raw_inv), (coupling, raw_coup), (span_of, raw_span),
            (mass_in, mass), (inv_mass_in, inv_mass)))
    ]

    barrier = pltpu.get_barrier_semaphore()

    def at(dx, dy):
        return (lax.rem(gx + (dx + ngx), ngx), lax.rem(gy + (dy + ngy), ngy))

    for d in range(1, ngy):
        pl.semaphore_signal(barrier, inc=1, device_id=at(0, d), device_id_type=MESH)
    for d in range(1, ngx):
        pl.semaphore_signal(barrier, inc=1, device_id=at(d, 0), device_id_type=MESH)
    for dx in (-1, 1):
        for dy in (-1, 1):
            pl.semaphore_signal(barrier, inc=1, device_id=at(dx, dy), device_id_type=MESH)
    for load in loads:
        load.start()

    def a_first(d):
        return pltpu.make_async_remote_copy(
            src_ref=a0.at[lax.rem(gy + d, ngy)], dst_ref=a1.at[gy],
            send_sem=a1s_sem.at[d], recv_sem=a1r_sem.at[d],
            device_id=at(0, d), device_id_type=MESH)

    def a_second(d):
        return pltpu.make_async_remote_copy(
            src_ref=a2s.at[lax.rem(gx + d, ngx)], dst_ref=a2r.at[gx],
            send_sem=a2s_sem.at[d], recv_sem=a2r_sem.at[d],
            device_id=at(d, 0), device_id_type=MESH)

    def b_first(d):
        return pltpu.make_async_remote_copy(
            src_ref=b0.at[lax.rem(gx + d, ngx)], dst_ref=b1.at[gx],
            send_sem=b1s_sem.at[d], recv_sem=b1r_sem.at[d],
            device_id=at(d, 0), device_id_type=MESH)

    def b_second(d):
        return pltpu.make_async_remote_copy(
            src_ref=b1.at[:, lax.rem(gy + d, ngy)], dst_ref=b2r.at[gy],
            send_sem=b2s_sem.at[d], recv_sem=b2r_sem.at[d],
            device_id=at(0, d), device_id_type=MESH)

    def weighted(h, k, field):
        def body(ey, carry):
            lines = []
            for ex in range(EX):
                f = [[field(h, ex * NP + i, ey, j) for j in range(NP)] for i in range(NP)]
                along_x = [derivative([f[i][j] for i in range(NP)]) for j in range(NP)]
                along_y = [derivative(f[i]) for i in range(NP)]
                w = []
                for i in range(NP):
                    row = []
                    for j in range(NP):
                        x, y = ex * NP + i, ey * NP + j
                        node = pl.ds(pl.multiple_of((x * NY + y) * 8, 8), 8)
                        flow = wxe[h, node, :] * along_x[j][i] + wye[h, node, :] * along_y[i][j]
                        row.append(mass[x, y] * flow)
                    w.append(row)
                if lines:
                    lines[-1] = [a + b for a, b in zip(lines[-1], w[0])]
                    lines += w[1:]
                else:
                    lines = w
            for X in range(UX):
                values = [carry[X] + lines[X][0], lines[X][1], lines[X][2]]
                for j in range(3):
                    grid[k % 2, h, X, ey * 3 + j] = values[j]
                    if X == 0:
                        sx[k, h, 0, ey * 3 + j] = values[j]
                    if X == UX - 1:
                        sx[k, h, 1, ey * 3 + j] = values[j]
            return tuple(lines[X][3] for X in range(UX))

        carry = lax.fori_loop(0, EY, body, (jnp.zeros((8, 128), F32),) * UX)
        for X in range(UX):
            grid[k % 2, h, X, UY - 1] = carry[X]
            sy[k, h, 1, X] = carry[X]
            sy[k, h, 0, X] = grid[k % 2, h, X, 0]
        sx[k, h, 0, UY - 1] = carry[0]
        sx[k, h, 1, UY - 1] = carry[UX - 1]

    def halo(h, k):
        if k < 2:
            moves = [
                (sx.at[k, h, 1, UY - 1], rc.at[k, h, 0], (1, 1)),
                (sx.at[k, h, 1, 0], rc.at[k, h, 1], (1, -1)),
                (sx.at[k, h, 0, UY - 1], rc.at[k, h, 2], (-1, 1)),
                (sx.at[k, h, 0, 0], rc.at[k, h, 3], (-1, -1)),
                (sy.at[k, h, 1], ry.at[k, h, 0], (0, 1)),
                (sy.at[k, h, 0], ry.at[k, h, 1], (0, -1)),
                (sx.at[k, h, 1], rx.at[k, h, 0], (1, 0)),
                (sx.at[k, h, 0], rx.at[k, h, 1], (-1, 0)),
            ]
        else:
            moves = [
                (sx.at[k, h, 1, UY - 1], rc.at[k, h, 0], (1, 1)),
                (sy.at[k, h, 1, pl.ds(0, UX - 1)], ry.at[k, h, 0, pl.ds(0, UX - 1)], (0, 1)),
                (sx.at[k, h, 1, pl.ds(0, UY - 1)], rx.at[k, h, 0, pl.ds(0, UY - 1)], (1, 0)),
            ]
        return [
            pltpu.make_async_remote_copy(
                src_ref=src, dst_ref=dst, send_sem=hs.at[k, h, n], recv_sem=hr.at[k, h, n],
                device_id=at(*offset), device_id_type=MESH)
            for n, (src, dst, offset) in enumerate(moves)
        ]

    def arrive(h, k):
        for move in halo(h, k):
            move.wait_recv()
        g = grid.at[k % 2, h]
        g[0] += rx[k, h, 0]
        g[UX - 1] += rx[k, h, 1]
        g[:, 0] += ry[k, h, 0]
        g[:, UY - 1] += ry[k, h, 1]
        g[0, 0] += rc[k, h, 0]
        g[0, UY - 1] += rc[k, h, 1]
        g[UX - 1, 0] += rc[k, h, 2]
        g[UX - 1, UY - 1] += rc[k, h, 3]

    def edge(h, k, x, ey, j):
        return grid[k % 2, h, x - x // NP, ey * 3 + j]

    def initial(h, x, ey, j):
        return st[h, x, ey * NP + j]

    def first(h, x, ey, j):
        y = ey * NP + j
        value = st[h, x, y] - (STEP * inv_mass[x, y]) * edge(h, 0, x, ey, j)
        fld[h, x, y] = value
        return value

    def second(h, x, ey, j):
        y = ey * NP + j
        value = 0.75 * st[h, x, y] + 0.25 * fld[h, x, y] - (0.25 * STEP * inv_mass[x, y]) * edge(h, 1, x, ey, j)
        fld[h, x, y] = value
        return value

    def third(h, x, ey, j):
        y = ey * NP + j
        value = (1.0 / 3.0) * st[h, x, y] + (2.0 / 3.0) * fld[h, x, y]
        return value - (2.0 / 3.0 * STEP * inv_mass[x, y]) * edge(h, 2, x, ey, j)

    def final(h, lines):
        def body(ey, carry):
            for X in lines:
                for j in range(3):
                    row = (X * EY + ey) * 3 + j
                    fin[h, pl.ds(pl.multiple_of(row * 8, 8), 8), :] = third(h, X + X // 3, ey, j)
            return carry

        lax.fori_loop(0, EY, body, 0, unroll=4 if len(lines) == 1 else 1)

    def go(h, k):
        moves = halo(h, k)
        for move in moves:
            move.start()
        return moves

    def repack(s, carry):
        for g in range(ngy):
            a2s[s, g * 8:(g + 1) * 8, :] = a1[g, pl.ds(pl.multiple_of(s * 8, 8), 8), :]
            a2s[s, ngy * 8 + g:ngy * 8 + g + 1, :] = a1[g, pl.ds(ngx * 8 + s, 1), :]
        return carry

    def gather(h, slots):
        source = two_parts(jnp.concatenate(slots, axis=1))
        many = sum(jnp.dot(picks[h][SKIP:], part, preferred_element_type=F32) for part in source)
        few = sum(jnp.dot(late_picks[h], part, preferred_element_type=F32) for part in source)
        for j in range(4):
            rows = slice((4 * h + j) * 128, (4 * h + j + 1) * 128)
            bt[rows, :] = many[:, j * 128:(j + 1) * 128].T
            bp[rows, :] = few[:, j * 128:(j + 1) * 128].T

    level = lax.rem(lax.broadcasted_iota(jnp.int32, (128, 128), 0), 64)
    target = lax.broadcasted_iota(jnp.int32, (128, 128), 1) // 32
    for load in loads[:2] + loads[7:]:
        load.wait()
    winds = []
    for raw_w in (raw_wx, raw_wy):
        w = raw_w[...].reshape(NX * NY, 64)
        high = w.astype(BF16).astype(F32)
        winds.append(jnp.concatenate([high, w - high], axis=1).astype(BF16))

    def spread_winds(h):
        for parts, wide_w in zip(winds, (wxe, wye)):
            for i in range(8):
                spreader = (level == target + 4 * (8 * h + i)).astype(BF16)
                value = jnp.dot(parts, spreader, preferred_element_type=F32)
                wide_w[h, pl.ds(i, NX * NY, stride=8), :] = value

    def turn(h):
        loads[2 + h].wait()

        def body(n, carry):
            x, y8 = n // (NY // 8), lax.rem(n, NY // 8)
            block = raw[x, pl.ds(pl.multiple_of(y8 * 8, 8), 8), 1024 * h:1024 * (h + 1)]
            st[h, x, pl.ds(y8 * 8, 8)] = block.reshape(8, 8, 128)
            return carry

        lax.fori_loop(0, NX * NY // 8, body, 0, unroll=2)

    for h in range(2):
        fin[h, SKIP * 8:LINE * 8, :] = jnp.zeros(((LINE - SKIP) * 8, 128), F32)
        fin[h, COLS * 8:, :] = jnp.zeros(((LINE * 9 + 1 - COLS) * 8, 128), F32)
    spread_winds(0)
    turn(0)
    weighted(0, 0, initial)
    pl.semaphore_wait(barrier, ngy - 1 + ngx - 1 + 4)
    go(0, 0)
    loads[4].wait()

    def pack(s, carry):
        upper_half = lax.broadcasted_iota(jnp.int32, (8, 128), 0) < 4
        for four in range(ngy // 4):
            rows = pl.ds(pl.multiple_of(s * (2 * ngy) + four * 8, 8), 8)
            block = raw_inv[rows, :].reshape(8, 8, 128)
            for q in range(4):
                one, two = block[2 * q], block[2 * q + 1]
                a0[four * 4 + q, pl.ds(pl.multiple_of(s * 8, 8), 8), :] = jnp.where(upper_half, one, pltpu.roll(two, 4, 0))
                b0[s, four * 4 + q] = jnp.where(upper_half, pltpu.roll(one, 4, 0), two)
        return carry

    lax.fori_loop(0, ngx, pack, 0)
    for d in range(1, ngx // 2):
        b_first(d).start()
    b1[gx] = b0[gx]
    spread_winds(1)
    turn(1)
    weighted(1, 0, initial)
    go(1, 0)
    for d in range(ngx // 2, ngx):
        b_first(d).start()
    across = (((1,), (1,)), ((), ()))
    loads[5].wait()
    slot = lax.broadcasted_iota(jnp.int32, (3, 2 * devices), 1)
    rows = jnp.concatenate(
        [jnp.where(lax.rem(slot, 2) == r, raw_coup[...], 0.0) for r in range(2)] + [jnp.zeros((122, 2 * devices), F32)], axis=0)
    owner = lax.broadcasted_iota(jnp.int32, (devices, 2 * devices), 0)
    slot = lax.broadcasted_iota(jnp.int32, (devices, 2 * devices), 1)
    chooser = (slot // 2 == owner).astype(BF16)
    both = sum(lax.dot_general(chooser, part, across, preferred_element_type=F32) for part in two_parts(rows))
    both = both.reshape(ngx, ngy, 128)
    for s in range(ngy):
        a0[s, ngx * 8:, :] = both[:, s, :]

    for d in range(1, ngy):
        a_first(d).start()
    a1[gy] = a0[gy]
    loads[6].wait()
    earlier = (lax.broadcasted_iota(jnp.int32, (COLS, COLS), 1) < lax.broadcasted_iota(jnp.int32, (COLS, COLS), 0)).astype(BF16)
    itself = (lax.broadcasted_iota(jnp.int32, (COLS, COLS), 1) == lax.broadcasted_iota(jnp.int32, (COLS, COLS), 0)).astype(BF16)
    span = lax.broadcasted_iota(jnp.int32, (devices, COLS), 0)
    late = lax.rem(lax.broadcasted_iota(jnp.int32, (128, COLS), 0), 32)
    late = jnp.where(late < LINE, late, (late - LINE + 1) * LINE)
    late = (late == lax.broadcasted_iota(jnp.int32, (128, COLS), 1)).astype(BF16)
    picks, late_picks = [], []
    for order in (span, lax.rem(span, ngx) * ngy + span // ngx):
        named = (raw_span[...] == order).astype(BF16)
        chosen = lax.dot_general(itself, named, across, preferred_element_type=F32)
        count = lax.dot_general(earlier, named, across, preferred_element_type=F32)
        picks.append(jnp.concatenate(
            [jnp.where(count < 0.5, chosen, 0.0), jnp.where(count < 0.5, 0.0, chosen)], axis=1).astype(BF16))
        late_picks.append(jnp.dot(late, picks[-1], preferred_element_type=F32).astype(BF16))

    arrive(0, 0)
    weighted(0, 1, first)
    go(0, 1)
    arrive(1, 0)
    weighted(1, 1, first)
    go(1, 1)
    for d in range(1, ngx):
        b_first(d).wait_recv()
    for d in range(1, ngy):
        b_second(d).start()
    b2r[gy] = b1[:, gy]
    for d in range(1, ngy):
        a_first(d).wait_recv()
    lax.fori_loop(0, ngx, repack, 0)
    a2r[gx] = a2s[gx]
    for d in range(1, ngx):
        a_second(d).start()
    arrive(0, 1)
    weighted(0, 2, second)
    last_low = go(0, 2)
    arrive(1, 1)
    weighted(1, 2, second)
    last_high = go(1, 2)
    last = [last_low, last_high]
    def solve(h, count, blocks, values, solved):
        def body(n, carry):
            blk, four = 2 * h + n // 4, lax.rem(n, 4)
            rows = blocks[pl.ds(pl.multiple_of(blk * 256 + four * 64, 8), 64), :]
            for tt in range(count):
                v = [values[pl.ds(pl.multiple_of(((blk * 16 + b) * count + tt) * 8, 8), 8), :] for b in range(16)]
                for a in range(4):
                    total = None
                    for b in range(16):
                        term = rows[a * 16 + b:a * 16 + b + 1, :] * v[b]
                        total = term if total is None else total + term
                    solved[pl.ds(pl.multiple_of(((blk * 16 + four * 4 + a) * count + tt) * 8, 8), 8), :] = total
            return carry

        lax.fori_loop(0, 8, body, 0, unroll=8 // count if count < 4 else 1)

    def sweep(tt, count, blocks, strengths, solved):
        def level(blk, a):
            return pl.ds(pl.multiple_of(((blk * 16 + a) * count + tt) * 8, 8), 8)

        def entry(blk, a, b):
            return blocks[blk * 256 + a * 16 + b:blk * 256 + a * 16 + b + 1, :]

        head = [solved[level(b, 0), :] for b in range(NB)]
        tail = [solved[level(b, 15), :] for b in range(NB)]
        strength = [strengths[b:b + 1, :] for b in range(NB - 1)]
        now_head, now_tail = head, tail
        for n in range(SWEEPS):
            upper = [strength[b] * now_head[b + 1] for b in range(NB - 1)] + [None]
            lower = [None] + [strength[b] * now_tail[b] for b in range(NB - 1)]
            if n < SWEEPS - 1:
                now_head, now_tail = list(head), list(tail)
                for b in range(NB):
                    for a, now in ((0, now_head), (15, now_tail)):
                        if upper[b] is not None:
                            now[b] = now[b] + entry(b, a, 15) * upper[b]
                        if lower[b] is not None:
                            now[b] = now[b] + entry(b, a, 0) * lower[b]
        for b in range(NB):
            for a in range(16):
                value = solved[level(b, a), :]
                if upper[b] is not None:
                    value = value + entry(b, a, 15) * upper[b]
                if lower[b] is not None:
                    value = value + entry(b, a, 0) * lower[b]
                solved[level(b, a), :] = value

    quarter = lax.broadcasted_iota(jnp.int32, (8, 128), 1) // 32

    def lay_many(h):
        for s in range(8):
            vt[(8 * h + s) * 128:(8 * h + s + 1) * 128, :] = fin[h, pl.ds(SKIP * 8 + s, 128, stride=8), :].T

    def lay_few(h):
        for s in range(8):
            four = jnp.concatenate([fin[h, pl.ds(s, LINE, stride=8), :], fin[h, pl.ds(LINE * 8 + s, 8, stride=LINE * 8), :]] * 4, axis=0).T
            for g in range(4):
                value = four[g * 32:g * 32 + 8]
                for q in range(1, 4):
                    value = jnp.where(quarter == q, four[g * 32 + q * 8:g * 32 + q * 8 + 8], value)
                vp[((8 * h + s) * 4 + g) * 8:((8 * h + s) * 4 + g + 1) * 8, :] = value

    def take_many(s):
        turned = xt[s * 128:(s + 1) * 128, :].T
        out[LINE:, s * 128:(s + 1) * 128] = turned[LINE - SKIP:]

    eighth = lax.rem(lax.broadcasted_iota(jnp.int32, (32, 128), 1) // 8, 4)

    def take_few(s):
        turned = jnp.concatenate([xp[(s * 4 + g) * 8:(s * 4 + g + 1) * 8, :] for g in range(4) for q in range(4)], axis=0).T
        value = turned[:32]
        for q in range(1, 4):
            value = jnp.where(eighth == q, turned[q * 32:q * 32 + 32], value)
        out[:LINE, s * 128:(s + 1) * 128] = value[:LINE]
        for n in range(1, UX - 1):
            out[n * LINE:n * LINE + 1, s * 128:(s + 1) * 128] = value[LINE + n - 1:LINE + n]

    def sweep_many(tt, carry):
        sweep(tt, 4, bt, kt, xt)
        return carry

    for d in range(1, ngy):
        b_second(d).wait_recv()
    gather(1, [
        jnp.concatenate([b2r[g, pl.ds(0, ngx), r * 4 + j, :] for r in range(2) for g in range(ngy)], axis=0)
        for j in range(4)])
    for h in range(2):
        final(h, range(1, UX - 1))
        lay_many(h)
    solve(1, 4, bt, vt, xt)
    for d in range(1, ngx):
        a_second(d).wait_recv()
    gather(0, [
        jnp.concatenate([a2r[g, pl.ds(r * 4 + j, ngy, stride=8), :] for r in range(2) for g in range(ngx)], axis=0)
        for j in range(4)])

    links = jnp.concatenate([a2r[g, ngy * 8:ngy * 8 + ngy, :] for g in range(ngx)], axis=0)
    links = two_parts(jnp.concatenate([links, pltpu.roll(links, 125, 1)], axis=0))
    kt[...] = sum(jnp.dot(picks[0][SKIP:], part, preferred_element_type=F32) for part in links).T
    kp[...] = sum(jnp.dot(late_picks[0], part, preferred_element_type=F32) for part in links).T

    solve(0, 4, bt, vt, xt)
    lax.fori_loop(0, 4, sweep_many, 0)
    for s in range(16):
        take_many(s)
    for d in range(1, ngy):
        a_first(d).wait_send()
        b_second(d).wait_send()
    for d in range(1, ngx):
        a_second(d).wait_send()
        b_first(d).wait_send()
    for k in range(2):
        for h in range(2):
            for move in halo(h, k):
                move.wait_send()
    for h in range(2):
        for move in last[h]:
            move.wait_recv()
        grid[0, h, 0:UX - 1, 0] += ry[2, h, 0, 0:UX - 1]
        grid[0, h, 0, 0] += rc[2, h, 0]
        grid[0, h, 0, 0:UY - 1] += rx[2, h, 0, 0:UY - 1]
        final(h, range(1))
        for X in range(1, UX - 1):
            fin[h, X * LINE * 8:X * LINE * 8 + 8, :] = third(h, X + X // 3, 0, 0)
        lay_few(h)
        solve(h, 1, bp, vp, xp)
    sweep(0, 1, bp, kp, xp)
    for s in range(16):
        take_few(s)

    for moves in last:
        for move in moves:
            move.wait_send()


def on_device(ngx, ngy, state, wind_x, wind_y, mass, inv_mass, span_of, block_inverse, coupling):
    width = state.shape[2]
    any_ = pl.BlockSpec(memory_space=pl.ANY)
    nodes = (2, NX, NY, 8, 128)
    vmem = pltpu.VMEM
    dma = pltpu.SemaphoreType.DMA
    span_of, coupling = span_of.T, coupling.T
    return pl.pallas_call(
        functools.partial(kernel, ngx, ngy),
        out_shape=pltpu.VMEM((COLS, width), F32),
        in_specs=[any_] * 8,
        out_specs=pl.BlockSpec(memory_space=pltpu.VMEM),
        scratch_shapes=[
            pltpu.SMEM(mass.shape, F32), pltpu.SMEM(inv_mass.shape, F32),
            vmem(state.shape, F32), vmem(wind_x.shape, F32), vmem(wind_y.shape, F32), vmem(span_of.shape, jnp.int32),
            vmem(block_inverse.shape, F32), vmem(coupling.shape, F32),
            vmem(nodes, F32), vmem(nodes, F32),
            vmem((2, (NX * NY + 1) * 8, 128), F32), vmem((2, (NX * NY + 1) * 8, 128), F32),
            vmem((2, 2, UX, UY, 8, 128), F32),
            vmem((3, 2, 2, UY, 8, 128), F32), vmem((3, 2, 2, UX, 8, 128), F32),
            vmem((3, 2, 2, UY, 8, 128), F32), vmem((3, 2, 2, UX, 8, 128), F32), vmem((3, 2, 4, 8, 128), F32),
            vmem((2, (LINE * 9 + 1) * 8, 128), F32),
            vmem((ngy, ngx * 9, 128), F32), vmem((ngy, ngx * 9, 128), F32),
            vmem((ngx, ngy * 9, 128), F32), vmem((ngx, ngy * 9, 128), F32),
            vmem((ngx, ngy, 8, 128), F32), vmem((ngx, ngy, 8, 128), F32), vmem((ngy, ngx, 8, 128), F32),
            vmem((128, 128), F32), vmem((1024, 128), F32), vmem((2048, 128), F32), vmem((2048, 128), F32),
            vmem((128, 128), F32), vmem((1024, 128), F32), vmem((512, 128), F32), vmem((512, 128), F32),
            dma((9,)), dma((3, 2, 8)), dma((3, 2, 8)),
            dma((ngy,)), dma((ngy,)), dma((ngx,)), dma((ngx,)),
            dma((ngx,)), dma((ngx,)), dma((ngy,)), dma((ngy,)),
        ],
        compiler_params=pltpu.CompilerParams(
            collective_id=0, has_side_effects=True, vmem_limit_bytes=60 * 2**20),
    )(state, wind_x, wind_y, mass, inv_mass, span_of, block_inverse, coupling)


def solution(mesh):
    placed = (
        P("gx", "gy", None),
        P("gx", "gy", None),
        P("gx", "gy", None),
        P("gx", "gy"),
        P("gx", "gy"),
        P(("gx", "gy"), None),
        P(("gx", "gy"), None),
        P(("gx", "gy"), None),
    )
    return jax.shard_map(
        functools.partial(on_device, mesh.shape["gx"], mesh.shape["gy"]),
        mesh=mesh, in_specs=placed, out_specs=P(("gx", "gy"), None), check_vma=False,
    )
```

```python
import functools

import jax
import jax.numpy as jnp
import numpy as np
from jax import lax
from jax.experimental import pallas as pl
from jax.experimental.pallas import tpu as pltpu
from jax.sharding import PartitionSpec as P

NP = 4
NB = 4
SWEEPS = 3
STEP = 0.05
EX = 2
EY = 8
NX = EX * NP
NY = EY * NP
UX = EX * 3 + 1
UY = EY * 3 + 1
COLS = EX * 3 * EY * 3
LINE = EY * 3
SKIP = COLS - 128
MESH = pl.DeviceIdType.MESH
F32 = jnp.float32
BF16 = jnp.bfloat16


def derivative_table():
    points = np.array([-1.0, -1.0 / np.sqrt(5.0), 1.0 / np.sqrt(5.0), 1.0])
    count = points.shape[0]
    weights = np.ones(count)
    for i in range(count):
        for m in range(count):
            if m != i:
                weights[i] = weights[i] * (points[i] - points[m])
    table = np.zeros((count, count))
    for i in range(count):
        for j in range(count):
            if i != j:
                table[i, j] = weights[i] / weights[j] / (points[i] - points[j])
                table[i, i] = table[i, i] + 1.0 / (points[i] - points[j])
    return table


TABLE = derivative_table()
ODD = [float((TABLE[i, 0] + TABLE[i, 3]) / 2) for i in range(2)]
EVEN = [[float((TABLE[i, k] - TABLE[i, 3 - k]) / 2) for k in range(2)] for i in range(2)]


def derivative(q):
    outer, inner = q[0] - q[3], q[1] - q[2]
    bend = (q[0] + q[3]) - (q[1] + q[2])
    odd = [ODD[i] * bend for i in range(2)]
    even = [EVEN[i][0] * outer + EVEN[i][1] * inner for i in range(2)]
    return [even[0] + odd[0], even[1] + odd[1], even[1] - odd[1], even[0] - odd[0]]


def two_parts(x):
    high = x.astype(BF16)
    return high, (x - high.astype(F32)).astype(BF16)


def kernel(ngx, ngy, state, wind_x, wind_y, mass_in, inv_mass_in, span_of, inverse, coupling, out,
           mass, inv_mass, raw, raw_wx, raw_wy, raw_span, raw_inv, raw_coup, st, fld, wxe, wye, grid, sx, sy, rx, ry, rc, fin,
           a0, a1, a2s, a2r, b0, b1, b2r, kt, bt, vt, xt, kp, bp, vp, xp,
           load_sem, hs, hr, a1s_sem, a1r_sem, a2s_sem, a2r_sem, b1s_sem, b1r_sem, b2s_sem, b2r_sem):
    gx, gy = lax.axis_index("gx"), lax.axis_index("gy")
    devices = ngx * ngy

    loads = [
        pltpu.make_async_copy(src, dst, load_sem.at[n])
        for n, (src, dst) in enumerate((
            (wind_x, raw_wx), (wind_y, raw_wy), (state.at[:, :, :1024], raw.at[:, :, :1024]), (state.at[:, :, 1024:], raw.at[:, :, 1024:]),
            (inverse, raw_inv), (coupling, raw_coup), (span_of, raw_span),
            (mass_in, mass), (inv_mass_in, inv_mass)))
    ]

    barrier = pltpu.get_barrier_semaphore()

    def at(dx, dy):
        return (lax.rem(gx + (dx + ngx), ngx), lax.rem(gy + (dy + ngy), ngy))

    for d in range(1, ngy):
        pl.semaphore_signal(barrier, inc=1, device_id=at(0, d), device_id_type=MESH)
    for d in range(1, ngx):
        pl.semaphore_signal(barrier, inc=1, device_id=at(d, 0), device_id_type=MESH)
    for dx in (-1, 1):
        for dy in (-1, 1):
            pl.semaphore_signal(barrier, inc=1, device_id=at(dx, dy), device_id_type=MESH)
    for load in loads:
        load.start()

    def a_first(d):
        return pltpu.make_async_remote_copy(
            src_ref=a0.at[lax.rem(gy + d, ngy)], dst_ref=a1.at[gy],
            send_sem=a1s_sem.at[d], recv_sem=a1r_sem.at[d],
            device_id=at(0, d), device_id_type=MESH)

    def a_second(d):
        return pltpu.make_async_remote_copy(
            src_ref=a2s.at[lax.rem(gx + d, ngx), pl.ds(0, ngy * 8 + 1)], dst_ref=a2r.at[gx, pl.ds(0, ngy * 8 + 1)],
            send_sem=a2s_sem.at[d], recv_sem=a2r_sem.at[d],
            device_id=at(d, 0), device_id_type=MESH)

    def b_first(d):
        return pltpu.make_async_remote_copy(
            src_ref=b0.at[lax.rem(gx + d, ngx)], dst_ref=b1.at[gx],
            send_sem=b1s_sem.at[d], recv_sem=b1r_sem.at[d],
            device_id=at(d, 0), device_id_type=MESH)

    def b_second(d):
        return pltpu.make_async_remote_copy(
            src_ref=b1.at[:, lax.rem(gy + d, ngy)], dst_ref=b2r.at[gy],
            send_sem=b2s_sem.at[d], recv_sem=b2r_sem.at[d],
            device_id=at(0, d), device_id_type=MESH)

    def weighted(h, k, field):
        def body(ey, carry):
            lines = []
            for ex in range(EX):
                f = [[field(h, ex * NP + i, ey, j) for j in range(NP)] for i in range(NP)]
                along_x = [derivative([f[i][j] for i in range(NP)]) for j in range(NP)]
                along_y = [derivative(f[i]) for i in range(NP)]
                w = []
                for i in range(NP):
                    row = []
                    for j in range(NP):
                        x, y = ex * NP + i, ey * NP + j
                        node = pl.ds(pl.multiple_of((x * NY + y) * 8, 8), 8)
                        flow = wxe[h, node, :] * along_x[j][i] + wye[h, node, :] * along_y[i][j]
                        row.append(mass[x, y] * flow)
                    w.append(row)
                if lines:
                    lines[-1] = [a + b for a, b in zip(lines[-1], w[0])]
                    lines += w[1:]
                else:
                    lines = w
            for X in range(UX):
                values = [carry[X] + lines[X][0], lines[X][1], lines[X][2]]
                for j in range(3):
                    grid[k % 2, h, X, ey * 3 + j] = values[j]
                    if X == 0:
                        sx[k, h, 0, ey * 3 + j] = values[j]
                    if X == UX - 1:
                        sx[k, h, 1, ey * 3 + j] = values[j]
            return tuple(lines[X][3] for X in range(UX))

        carry = lax.fori_loop(0, EY, body, (jnp.zeros((8, 128), F32),) * UX)
        for X in range(UX):
            grid[k % 2, h, X, UY - 1] = carry[X]
            sy[k, h, 1, X] = carry[X]
            sy[k, h, 0, X] = grid[k % 2, h, X, 0]
        sx[k, h, 0, UY - 1] = carry[0]
        sx[k, h, 1, UY - 1] = carry[UX - 1]

    def halo(h, k):
        if k < 2:
            moves = [
                (sx.at[k, h, 1, UY - 1], rc.at[k, h, 0], (1, 1)),
                (sx.at[k, h, 1, 0], rc.at[k, h, 1], (1, -1)),
                (sx.at[k, h, 0, UY - 1], rc.at[k, h, 2], (-1, 1)),
                (sx.at[k, h, 0, 0], rc.at[k, h, 3], (-1, -1)),
                (sy.at[k, h, 1], ry.at[k, h, 0], (0, 1)),
                (sy.at[k, h, 0], ry.at[k, h, 1], (0, -1)),
                (sx.at[k, h, 1], rx.at[k, h, 0], (1, 0)),
                (sx.at[k, h, 0], rx.at[k, h, 1], (-1, 0)),
            ]
        else:
            moves = [
                (sx.at[k, h, 1, UY - 1], rc.at[k, h, 0], (1, 1)),
                (sy.at[k, h, 1, pl.ds(0, UX - 1)], ry.at[k, h, 0, pl.ds(0, UX - 1)], (0, 1)),
                (sx.at[k, h, 1, pl.ds(0, UY - 1)], rx.at[k, h, 0, pl.ds(0, UY - 1)], (1, 0)),
            ]
        return [
            pltpu.make_async_remote_copy(
                src_ref=src, dst_ref=dst, send_sem=hs.at[k, h, n], recv_sem=hr.at[k, h, n],
                device_id=at(*offset), device_id_type=MESH)
            for n, (src, dst, offset) in enumerate(moves)
        ]

    def arrive(h, k):
        for move in halo(h, k):
            move.wait_recv()
        g = grid.at[k % 2, h]
        g[0] += rx[k, h, 0]
        g[UX - 1] += rx[k, h, 1]
        g[:, 0] += ry[k, h, 0]
        g[:, UY - 1] += ry[k, h, 1]
        g[0, 0] += rc[k, h, 0]
        g[0, UY - 1] += rc[k, h, 1]
        g[UX - 1, 0] += rc[k, h, 2]
        g[UX - 1, UY - 1] += rc[k, h, 3]

    def edge(h, k, x, ey, j):
        return grid[k % 2, h, x - x // NP, ey * 3 + j]

    def initial(h, x, ey, j):
        return st[h, x, ey * NP + j]

    def first(h, x, ey, j):
        y = ey * NP + j
        value = st[h, x, y] - (STEP * inv_mass[x, y]) * edge(h, 0, x, ey, j)
        fld[h, x, y] = value
        return value

    def second(h, x, ey, j):
        y = ey * NP + j
        value = 0.75 * st[h, x, y] + 0.25 * fld[h, x, y] - (0.25 * STEP * inv_mass[x, y]) * edge(h, 1, x, ey, j)
        fld[h, x, y] = value
        return value

    def third(h, x, ey, j):
        y = ey * NP + j
        value = (1.0 / 3.0) * st[h, x, y] + (2.0 / 3.0) * fld[h, x, y]
        return value - (2.0 / 3.0 * STEP * inv_mass[x, y]) * edge(h, 2, x, ey, j)

    def final(h, lines):
        def body(ey, carry):
            for X in lines:
                for j in range(3):
                    row = (X * EY + ey) * 3 + j
                    fin[h, pl.ds(pl.multiple_of(row * 8, 8), 8), :] = third(h, X + X // 3, ey, j)
            return carry

        lax.fori_loop(0, EY, body, 0, unroll=4 if len(lines) == 1 else 1)

    def go(h, k):
        moves = halo(h, k)
        for move in moves:
            move.start()
        return moves

    def repack(s, carry):
        for g in range(ngy):
            a2s[s, g * 8:(g + 1) * 8, :] = a1[g, pl.ds(pl.multiple_of(s * 8, 8), 8), :]
        return carry

    def gather(h, slots):
        source = two_parts(jnp.concatenate(slots, axis=1))
        many = sum(jnp.dot(picks[h][SKIP:], part, preferred_element_type=F32) for part in source)
        few = sum(jnp.dot(late_picks[h], part, preferred_element_type=F32) for part in source)
        for j in range(4):
            rows = slice((4 * h + j) * 128, (4 * h + j + 1) * 128)
            bt[rows, :] = many[:, j * 128:(j + 1) * 128].T
            bp[rows, :] = few[:, j * 128:(j + 1) * 128].T

    level = lax.rem(lax.broadcasted_iota(jnp.int32, (128, 128), 0), 64)
    target = lax.broadcasted_iota(jnp.int32, (128, 128), 1) // 32
    for load in loads[:2] + loads[7:]:
        load.wait()
    winds = []
    for raw_w in (raw_wx, raw_wy):
        w = raw_w[...].reshape(NX * NY, 64)
        high = w.astype(BF16).astype(F32)
        winds.append(jnp.concatenate([high, w - high], axis=1).astype(BF16))

    def spread_winds(h):
        for parts, wide_w in zip(winds, (wxe, wye)):
            for i in range(8):
                spreader = (level == target + 4 * (8 * h + i)).astype(BF16)
                value = jnp.dot(parts, spreader, preferred_element_type=F32)
                wide_w[h, pl.ds(i, NX * NY, stride=8), :] = value

    def turn(h):
        loads[2 + h].wait()

        def body(n, carry):
            x, y8 = n // (NY // 8), lax.rem(n, NY // 8)
            block = raw[x, pl.ds(pl.multiple_of(y8 * 8, 8), 8), 1024 * h:1024 * (h + 1)]
            st[h, x, pl.ds(y8 * 8, 8)] = block.reshape(8, 8, 128)
            return carry

        lax.fori_loop(0, NX * NY // 8, body, 0, unroll=2)

    for h in range(2):
        fin[h, SKIP * 8:LINE * 8, :] = jnp.zeros(((LINE - SKIP) * 8, 128), F32)
        fin[h, COLS * 8:, :] = jnp.zeros(((LINE * 9 + 1 - COLS) * 8, 128), F32)
    spread_winds(0)
    turn(0)
    weighted(0, 0, initial)
    pl.semaphore_wait(barrier, ngy - 1 + ngx - 1 + 4)
    go(0, 0)
    loads[4].wait()

    def pack(s, carry):
        upper_half = lax.broadcasted_iota(jnp.int32, (8, 128), 0) < 4
        for four in range(ngy // 4):
            rows = pl.ds(pl.multiple_of(s * (2 * ngy) + four * 8, 8), 8)
            block = raw_inv[rows, :].reshape(8, 8, 128)
            for q in range(4):
                one, two = block[2 * q], block[2 * q + 1]
                a0[four * 4 + q, pl.ds(pl.multiple_of(s * 8, 8), 8), :] = jnp.where(upper_half, one, pltpu.roll(two, 4, 0))
                b0[s, four * 4 + q] = jnp.where(upper_half, pltpu.roll(one, 4, 0), two)
        return carry

    lax.fori_loop(0, ngx, pack, 0)
    for d in range(1, ngx // 2):
        b_first(d).start()
    b1[gx] = b0[gx]
    spread_winds(1)
    turn(1)
    weighted(1, 0, initial)
    go(1, 0)
    for d in range(ngx // 2, ngx):
        b_first(d).start()
    across = (((1,), (1,)), ((), ()))
    loads[5].wait()
    slot = lax.broadcasted_iota(jnp.int32, (3, 2 * devices), 1)
    rows = jnp.concatenate(
        [jnp.where(lax.rem(slot, 2) == r, raw_coup[...], 0.0) for r in range(2)] + [jnp.zeros((122, 2 * devices), F32)], axis=0)
    owner = lax.broadcasted_iota(jnp.int32, (devices, 2 * devices), 0)
    slot = lax.broadcasted_iota(jnp.int32, (devices, 2 * devices), 1)
    chooser = (slot // 2 == owner).astype(BF16)
    both = sum(lax.dot_general(chooser, part, across, preferred_element_type=F32) for part in two_parts(rows))
    both = both.reshape(ngx, ngy, 128)
    for s in range(ngy):
        a0[s, ngx * 8:, :] = both[:, s, :]

    for d in range(1, ngy):
        a_first(d).start()
    a1[gy] = a0[gy]
    loads[6].wait()
    earlier = (lax.broadcasted_iota(jnp.int32, (COLS, COLS), 1) < lax.broadcasted_iota(jnp.int32, (COLS, COLS), 0)).astype(BF16)
    itself = (lax.broadcasted_iota(jnp.int32, (COLS, COLS), 1) == lax.broadcasted_iota(jnp.int32, (COLS, COLS), 0)).astype(BF16)
    span = lax.broadcasted_iota(jnp.int32, (devices, COLS), 0)
    late = lax.rem(lax.broadcasted_iota(jnp.int32, (128, COLS), 0), 32)
    late = jnp.where(late < LINE, late, (late - LINE + 1) * LINE)
    late = (late == lax.broadcasted_iota(jnp.int32, (128, COLS), 1)).astype(BF16)
    picks, late_picks = [], []
    for order in (span, lax.rem(span, ngx) * ngy + span // ngx):
        named = (raw_span[...] == order).astype(BF16)
        chosen = lax.dot_general(itself, named, across, preferred_element_type=F32)
        count = lax.dot_general(earlier, named, across, preferred_element_type=F32)
        picks.append(jnp.concatenate(
            [jnp.where(count < 0.5, chosen, 0.0), jnp.where(count < 0.5, 0.0, chosen)], axis=1).astype(BF16))
        late_picks.append(jnp.dot(late, picks[-1], preferred_element_type=F32).astype(BF16))

    arrive(0, 0)
    weighted(0, 1, first)
    go(0, 1)
    arrive(1, 0)
    weighted(1, 1, first)
    go(1, 1)
    for d in range(1, ngx):
        b_first(d).wait_recv()
    for d in range(1, ngy):
        b_second(d).start()
    b2r[gy] = b1[:, gy]
    for d in range(1, ngy):
        a_first(d).wait_recv()
    lax.fori_loop(0, ngx, repack, 0)
    row = a1[0, ngx * 8:, :]
    for g in range(1, ngy):
        row = row + pltpu.roll(a1[g, ngx * 8:, :], 16 * g, 1)
    for s in range(ngx):
        a2s[s, ngy * 8:ngy * 8 + 1, :] = row[s:s + 1]
    a2r[gx, :ngy * 8 + 1, :] = a2s[gx, :ngy * 8 + 1, :]
    for d in range(1, ngx):
        a_second(d).start()
    arrive(0, 1)
    weighted(0, 2, second)
    last_low = go(0, 2)
    arrive(1, 1)
    weighted(1, 2, second)
    last_high = go(1, 2)
    last = [last_low, last_high]
    def solve(h, count, blocks, values, solved):
        def body(n, carry):
            blk, four = 2 * h + n // 4, lax.rem(n, 4)
            rows = blocks[pl.ds(pl.multiple_of(blk * 256 + four * 64, 8), 64), :]
            for tt in range(count):
                v = [values[pl.ds(pl.multiple_of(((blk * 16 + b) * count + tt) * 8, 8), 8), :] for b in range(16)]
                for a in range(4):
                    total = None
                    for b in range(16):
                        term = rows[a * 16 + b:a * 16 + b + 1, :] * v[b]
                        total = term if total is None else total + term
                    solved[pl.ds(pl.multiple_of(((blk * 16 + four * 4 + a) * count + tt) * 8, 8), 8), :] = total
            return carry

        lax.fori_loop(0, 8, body, 0, unroll=8 // count if count < 4 else 1)

    def sweep(tt, count, blocks, strengths, solved):
        def level(blk, a):
            return pl.ds(pl.multiple_of(((blk * 16 + a) * count + tt) * 8, 8), 8)

        def entry(blk, a, b):
            return blocks[blk * 256 + a * 16 + b:blk * 256 + a * 16 + b + 1, :]

        head = [solved[level(b, 0), :] for b in range(NB)]
        tail = [solved[level(b, 15), :] for b in range(NB)]
        strength = [strengths[b:b + 1, :] for b in range(NB - 1)]
        now_head, now_tail = head, tail
        for n in range(SWEEPS):
            upper = [strength[b] * now_head[b + 1] for b in range(NB - 1)] + [None]
            lower = [None] + [strength[b] * now_tail[b] for b in range(NB - 1)]
            if n < SWEEPS - 1:
                now_head, now_tail = list(head), list(tail)
                for b in range(NB):
                    for a, now in ((0, now_head), (15, now_tail)):
                        if upper[b] is not None:
                            now[b] = now[b] + entry(b, a, 15) * upper[b]
                        if lower[b] is not None:
                            now[b] = now[b] + entry(b, a, 0) * lower[b]
        for b in range(NB):
            for a in range(16):
                value = solved[level(b, a), :]
                if upper[b] is not None:
                    value = value + entry(b, a, 15) * upper[b]
                if lower[b] is not None:
                    value = value + entry(b, a, 0) * lower[b]
                solved[level(b, a), :] = value

    quarter = lax.broadcasted_iota(jnp.int32, (8, 128), 1) // 32

    def lay_many(h):
        for s in range(8):
            vt[(8 * h + s) * 128:(8 * h + s + 1) * 128, :] = fin[h, pl.ds(SKIP * 8 + s, 128, stride=8), :].T

    def lay_few(h):
        for s in range(8):
            four = jnp.concatenate([fin[h, pl.ds(s, LINE, stride=8), :], fin[h, pl.ds(LINE * 8 + s, 8, stride=LINE * 8), :]] * 4, axis=0).T
            for g in range(4):
                value = four[g * 32:g * 32 + 8]
                for q in range(1, 4):
                    value = jnp.where(quarter == q, four[g * 32 + q * 8:g * 32 + q * 8 + 8], value)
                vp[((8 * h + s) * 4 + g) * 8:((8 * h + s) * 4 + g + 1) * 8, :] = value

    def take_many(s):
        turned = xt[s * 128:(s + 1) * 128, :].T
        out[LINE:, s * 128:(s + 1) * 128] = turned[LINE - SKIP:]

    eighth = lax.rem(lax.broadcasted_iota(jnp.int32, (32, 128), 1) // 8, 4)

    def take_few(s):
        turned = jnp.concatenate([xp[(s * 4 + g) * 8:(s * 4 + g + 1) * 8, :] for g in range(4) for q in range(4)], axis=0).T
        value = turned[:32]
        for q in range(1, 4):
            value = jnp.where(eighth == q, turned[q * 32:q * 32 + 32], value)
        out[:LINE, s * 128:(s + 1) * 128] = value[:LINE]
        for n in range(1, UX - 1):
            out[n * LINE:n * LINE + 1, s * 128:(s + 1) * 128] = value[LINE + n - 1:LINE + n]

    def sweep_many(tt, carry):
        sweep(tt, 4, bt, kt, xt)
        return carry

    for d in range(1, ngy):
        b_second(d).wait_recv()
    gather(1, [
        jnp.concatenate([b2r[g, pl.ds(0, ngx), r * 4 + j, :] for r in range(2) for g in range(ngy)], axis=0)
        for j in range(4)])
    for h in range(2):
        final(h, range(1, UX - 1))
        lay_many(h)
    solve(1, 4, bt, vt, xt)
    for d in range(1, ngx):
        a_second(d).wait_recv()
    gather(0, [
        jnp.concatenate([a2r[g, pl.ds(r * 4 + j, ngy, stride=8), :] for r in range(2) for g in range(ngx)], axis=0)
        for j in range(4)])

    row = a2r[:, ngy * 8, :]
    links = two_parts(jnp.concatenate(
        [pltpu.roll(row, (128 - 16 * g - 3 * r) % 128, 1) for r in range(2) for g in range(ngy)], axis=0))
    kt[...] = sum(jnp.dot(picks[1][SKIP:], part, preferred_element_type=F32) for part in links).T
    kp[...] = sum(jnp.dot(late_picks[1], part, preferred_element_type=F32) for part in links).T

    solve(0, 4, bt, vt, xt)
    lax.fori_loop(0, 4, sweep_many, 0)
    for s in range(16):
        take_many(s)
    for d in range(1, ngy):
        a_first(d).wait_send()
        b_second(d).wait_send()
    for d in range(1, ngx):
        a_second(d).wait_send()
        b_first(d).wait_send()
    for k in range(2):
        for h in range(2):
            for move in halo(h, k):
                move.wait_send()
    for h in range(2):
        for move in last[h]:
            move.wait_recv()
        grid[0, h, 0:UX - 1, 0] += ry[2, h, 0, 0:UX - 1]
        grid[0, h, 0, 0] += rc[2, h, 0]
        grid[0, h, 0, 0:UY - 1] += rx[2, h, 0, 0:UY - 1]
        final(h, range(1))
        for X in range(1, UX - 1):
            fin[h, X * LINE * 8:X * LINE * 8 + 8, :] = third(h, X + X // 3, 0, 0)
        lay_few(h)
        solve(h, 1, bp, vp, xp)
    sweep(0, 1, bp, kp, xp)
    for s in range(16):
        take_few(s)

    for moves in last:
        for move in moves:
            move.wait_send()


def on_device(ngx, ngy, state, wind_x, wind_y, mass, inv_mass, span_of, block_inverse, coupling):
    width = state.shape[2]
    any_ = pl.BlockSpec(memory_space=pl.ANY)
    nodes = (2, NX, NY, 8, 128)
    vmem = pltpu.VMEM
    dma = pltpu.SemaphoreType.DMA
    span_of, coupling = span_of.T, coupling.T
    return pl.pallas_call(
        functools.partial(kernel, ngx, ngy),
        out_shape=pltpu.VMEM((COLS, width), F32),
        in_specs=[any_] * 8,
        out_specs=pl.BlockSpec(memory_space=pltpu.VMEM),
        scratch_shapes=[
            pltpu.SMEM(mass.shape, F32), pltpu.SMEM(inv_mass.shape, F32),
            vmem(state.shape, F32), vmem(wind_x.shape, F32), vmem(wind_y.shape, F32), vmem(span_of.shape, jnp.int32),
            vmem(block_inverse.shape, F32), vmem(coupling.shape, F32),
            vmem(nodes, F32), vmem(nodes, F32),
            vmem((2, (NX * NY + 1) * 8, 128), F32), vmem((2, (NX * NY + 1) * 8, 128), F32),
            vmem((2, 2, UX, UY, 8, 128), F32),
            vmem((3, 2, 2, UY, 8, 128), F32), vmem((3, 2, 2, UX, 8, 128), F32),
            vmem((3, 2, 2, UY, 8, 128), F32), vmem((3, 2, 2, UX, 8, 128), F32), vmem((3, 2, 4, 8, 128), F32),
            vmem((2, (LINE * 9 + 1) * 8, 128), F32),
            vmem((ngy, ngx * 9, 128), F32), vmem((ngy, ngx * 9, 128), F32),
            vmem((ngx, ngy * 9, 128), F32), vmem((ngx, ngy * 9, 128), F32),
            vmem((ngx, ngy, 8, 128), F32), vmem((ngx, ngy, 8, 128), F32), vmem((ngy, ngx, 8, 128), F32),
            vmem((128, 128), F32), vmem((1024, 128), F32), vmem((2048, 128), F32), vmem((2048, 128), F32),
            vmem((128, 128), F32), vmem((1024, 128), F32), vmem((512, 128), F32), vmem((512, 128), F32),
            dma((9,)), dma((3, 2, 8)), dma((3, 2, 8)),
            dma((ngy,)), dma((ngy,)), dma((ngx,)), dma((ngx,)),
            dma((ngx,)), dma((ngx,)), dma((ngy,)), dma((ngy,)),
        ],
        compiler_params=pltpu.CompilerParams(
            collective_id=0, has_side_effects=True, vmem_limit_bytes=60 * 2**20),
    )(state, wind_x, wind_y, mass, inv_mass, span_of, block_inverse, coupling)


def solution(mesh):
    placed = (
        P("gx", "gy", None),
        P("gx", "gy", None),
        P("gx", "gy", None),
        P("gx", "gy"),
        P("gx", "gy"),
        P(("gx", "gy"), None),
        P(("gx", "gy"), None),
        P(("gx", "gy"), None),
    )
    return jax.shard_map(
        functools.partial(on_device, mesh.shape["gx"], mesh.shape["gy"]),
        mesh=mesh, in_specs=placed, out_specs=P(("gx", "gy"), None), check_vma=False,
    )
```

```python
import functools

import jax
import jax.numpy as jnp
import numpy as np
from jax import lax
from jax.experimental import pallas as pl
from jax.experimental.pallas import tpu as pltpu
from jax.sharding import PartitionSpec as P

NP = 4
NB = 4
SWEEPS = 3
STEP = 0.05
EX = 2
EY = 8
NX = EX * NP
NY = EY * NP
UX = EX * 3 + 1
UY = EY * 3 + 1
COLS = EX * 3 * EY * 3
LINE = EY * 3
SKIP = COLS - 128
MESH = pl.DeviceIdType.MESH
F32 = jnp.float32
BF16 = jnp.bfloat16


def derivative_table():
    points = np.array([-1.0, -1.0 / np.sqrt(5.0), 1.0 / np.sqrt(5.0), 1.0])
    count = points.shape[0]
    weights = np.ones(count)
    for i in range(count):
        for m in range(count):
            if m != i:
                weights[i] = weights[i] * (points[i] - points[m])
    table = np.zeros((count, count))
    for i in range(count):
        for j in range(count):
            if i != j:
                table[i, j] = weights[i] / weights[j] / (points[i] - points[j])
                table[i, i] = table[i, i] + 1.0 / (points[i] - points[j])
    return table


TABLE = derivative_table()
ODD = [float((TABLE[i, 0] + TABLE[i, 3]) / 2) for i in range(2)]
EVEN = [[float((TABLE[i, k] - TABLE[i, 3 - k]) / 2) for k in range(2)] for i in range(2)]


def derivative(q):
    outer, inner = q[0] - q[3], q[1] - q[2]
    bend = (q[0] + q[3]) - (q[1] + q[2])
    odd = [ODD[i] * bend for i in range(2)]
    even = [EVEN[i][0] * outer + EVEN[i][1] * inner for i in range(2)]
    return [even[0] + odd[0], even[1] + odd[1], even[1] - odd[1], even[0] - odd[0]]


def two_parts(x):
    high = x.astype(BF16)
    return high, (x - high.astype(F32)).astype(BF16)


def kernel(ngx, ngy, state, wind_x, wind_y, mass_in, inv_mass_in, span_of, inverse, coupling, out,
           mass, inv_mass, raw, raw_wx, raw_wy, raw_span, raw_inv, raw_coup, st, fld, wxe, wye, grid, sx, sy, rx, ry, rc, fin,
           a0, a1, a2s, a2r, b0, b1, b2r, kt, bt, vt, xt, kp, bp, vp, xp,
           load_sem, hs, hr, a1s_sem, a1r_sem, a2s_sem, a2r_sem, b1s_sem, b1r_sem, b2s_sem, b2r_sem):
    gx, gy = lax.axis_index("gx"), lax.axis_index("gy")
    devices = ngx * ngy

    loads = [
        pltpu.make_async_copy(src, dst, load_sem.at[n])
        for n, (src, dst) in enumerate((
            (wind_x, raw_wx), (wind_y, raw_wy), (state.at[:, :, :1024], raw.at[:, :, :1024]), (state.at[:, :, 1024:], raw.at[:, :, 1024:]),
            (inverse, raw_inv), (coupling, raw_coup), (span_of, raw_span),
            (mass_in, mass), (inv_mass_in, inv_mass)))
    ]

    barrier = pltpu.get_barrier_semaphore()

    def at(dx, dy):
        return (lax.rem(gx + (dx + ngx), ngx), lax.rem(gy + (dy + ngy), ngy))

    for d in range(1, ngy):
        pl.semaphore_signal(barrier, inc=1, device_id=at(0, d), device_id_type=MESH)
    for d in range(1, ngx):
        pl.semaphore_signal(barrier, inc=1, device_id=at(d, 0), device_id_type=MESH)
    for dx in (-1, 1):
        for dy in (-1, 1):
            pl.semaphore_signal(barrier, inc=1, device_id=at(dx, dy), device_id_type=MESH)
    for load in loads:
        load.start()

    def a_first(d):
        return pltpu.make_async_remote_copy(
            src_ref=a0.at[lax.rem(gy + d, ngy)], dst_ref=a1.at[gy],
            send_sem=a1s_sem.at[d], recv_sem=a1r_sem.at[d],
            device_id=at(0, d), device_id_type=MESH)

    def a_second(d):
        return pltpu.make_async_remote_copy(
            src_ref=a2s.at[lax.rem(gx + d, ngx), pl.ds(0, ngy * 8 + 1)], dst_ref=a2r.at[gx, pl.ds(0, ngy * 8 + 1)],
            send_sem=a2s_sem.at[d], recv_sem=a2r_sem.at[d],
            device_id=at(d, 0), device_id_type=MESH)

    def b_first(d):
        return pltpu.make_async_remote_copy(
            src_ref=b0.at[lax.rem(gx + d, ngx)], dst_ref=b1.at[gx],
            send_sem=b1s_sem.at[d], recv_sem=b1r_sem.at[d],
            device_id=at(d, 0), device_id_type=MESH)

    def b_second(d):
        return pltpu.make_async_remote_copy(
            src_ref=b1.at[:, lax.rem(gy + d, ngy)], dst_ref=b2r.at[gy],
            send_sem=b2s_sem.at[d], recv_sem=b2r_sem.at[d],
            device_id=at(0, d), device_id_type=MESH)

    def weighted(h, k, field):
        def body(ey, carry):
            lines = []
            for ex in range(EX):
                f = [[field(h, ex * NP + i, ey, j) for j in range(NP)] for i in range(NP)]
                along_x = [derivative([f[i][j] for i in range(NP)]) for j in range(NP)]
                along_y = [derivative(f[i]) for i in range(NP)]
                w = []
                for i in range(NP):
                    row = []
                    for j in range(NP):
                        x, y = ex * NP + i, ey * NP + j
                        node = pl.ds(pl.multiple_of((x * NY + y) * 8, 8), 8)
                        flow = wxe[h, node, :] * along_x[j][i] + wye[h, node, :] * along_y[i][j]
                        row.append(mass[x, y] * flow)
                    w.append(row)
                if lines:
                    lines[-1] = [a + b for a, b in zip(lines[-1], w[0])]
                    lines += w[1:]
                else:
                    lines = w
            for X in range(UX):
                values = [carry[X] + lines[X][0], lines[X][1], lines[X][2]]
                for j in range(3):
                    grid[k % 2, h, X, ey * 3 + j] = values[j]
                    if X == 0:
                        sx[k, h, 0, ey * 3 + j] = values[j]
                    if X == UX - 1:
                        sx[k, h, 1, ey * 3 + j] = values[j]
            return tuple(lines[X][3] for X in range(UX))

        carry = lax.fori_loop(0, EY, body, (jnp.zeros((8, 128), F32),) * UX)
        for X in range(UX):
            grid[k % 2, h, X, UY - 1] = carry[X]
            sy[k, h, 1, X] = carry[X]
            sy[k, h, 0, X] = grid[k % 2, h, X, 0]
        sx[k, h, 0, UY - 1] = carry[0]
        sx[k, h, 1, UY - 1] = carry[UX - 1]

    def halo(h, k):
        if k < 2:
            moves = [
                (sx.at[k, h, 1, UY - 1], rc.at[k, h, 0], (1, 1)),
                (sx.at[k, h, 1, 0], rc.at[k, h, 1], (1, -1)),
                (sx.at[k, h, 0, UY - 1], rc.at[k, h, 2], (-1, 1)),
                (sx.at[k, h, 0, 0], rc.at[k, h, 3], (-1, -1)),
                (sy.at[k, h, 1], ry.at[k, h, 0], (0, 1)),
                (sy.at[k, h, 0], ry.at[k, h, 1], (0, -1)),
                (sx.at[k, h, 1], rx.at[k, h, 0], (1, 0)),
                (sx.at[k, h, 0], rx.at[k, h, 1], (-1, 0)),
            ]
        else:
            moves = [
                (sx.at[k, h, 1, UY - 1], rc.at[k, h, 0], (1, 1)),
                (sy.at[k, h, 1, pl.ds(0, UX - 1)], ry.at[k, h, 0, pl.ds(0, UX - 1)], (0, 1)),
                (sx.at[k, h, 1, pl.ds(0, UY - 1)], rx.at[k, h, 0, pl.ds(0, UY - 1)], (1, 0)),
            ]
        return [
            pltpu.make_async_remote_copy(
                src_ref=src, dst_ref=dst, send_sem=hs.at[k, h, n], recv_sem=hr.at[k, h, n],
                device_id=at(*offset), device_id_type=MESH)
            for n, (src, dst, offset) in enumerate(moves)
        ]

    def arrive(h, k):
        for move in halo(h, k):
            move.wait_recv()
        g = grid.at[k % 2, h]
        g[0] += rx[k, h, 0]
        g[UX - 1] += rx[k, h, 1]
        g[:, 0] += ry[k, h, 0]
        g[:, UY - 1] += ry[k, h, 1]
        g[0, 0] += rc[k, h, 0]
        g[0, UY - 1] += rc[k, h, 1]
        g[UX - 1, 0] += rc[k, h, 2]
        g[UX - 1, UY - 1] += rc[k, h, 3]

    def edge(h, k, x, ey, j):
        return grid[k % 2, h, x - x // NP, ey * 3 + j]

    def initial(h, x, ey, j):
        return st[h, x, ey * NP + j]

    def first(h, x, ey, j):
        y = ey * NP + j
        value = st[h, x, y] - (STEP * inv_mass[x, y]) * edge(h, 0, x, ey, j)
        fld[h, x, y] = value
        return value

    def second(h, x, ey, j):
        y = ey * NP + j
        value = 0.75 * st[h, x, y] + 0.25 * fld[h, x, y] - (0.25 * STEP * inv_mass[x, y]) * edge(h, 1, x, ey, j)
        fld[h, x, y] = value
        return value

    def third(h, x, ey, j):
        y = ey * NP + j
        value = (1.0 / 3.0) * st[h, x, y] + (2.0 / 3.0) * fld[h, x, y]
        return value - (2.0 / 3.0 * STEP * inv_mass[x, y]) * edge(h, 2, x, ey, j)

    def final(h, lines):
        def body(ey, carry):
            for X in lines:
                for j in range(3):
                    row = (X * EY + ey) * 3 + j
                    fin[h, pl.ds(pl.multiple_of(row * 8, 8), 8), :] = third(h, X + X // 3, ey, j)
            return carry

        lax.fori_loop(0, EY, body, 0, unroll=4 if len(lines) == 1 else 1)

    def go(h, k):
        moves = halo(h, k)
        for move in moves:
            move.start()
        return moves

    def repack(s, carry):
        for g in range(ngy):
            a2s[s, g * 8:(g + 1) * 8, :] = a1[g, pl.ds(pl.multiple_of(s * 8, 8), 8), :]
        return carry

    def gather(h, slots):
        source = two_parts(jnp.concatenate(slots, axis=1))
        many = sum(jnp.dot(picks[h][SKIP:], part, preferred_element_type=F32) for part in source)
        few = sum(jnp.dot(late_picks[h], part, preferred_element_type=F32) for part in source)
        for j in range(4):
            rows = slice((4 * h + j) * 128, (4 * h + j + 1) * 128)
            bt[rows, :] = many[:, j * 128:(j + 1) * 128].T
            bp[rows, :] = few[:, j * 128:(j + 1) * 128].T

    level = lax.rem(lax.broadcasted_iota(jnp.int32, (128, 128), 0), 64)
    target = lax.broadcasted_iota(jnp.int32, (128, 128), 1) // 32
    for load in loads[:2] + loads[7:]:
        load.wait()
    winds = []
    for raw_w in (raw_wx, raw_wy):
        w = raw_w[...].reshape(NX * NY, 64)
        high = w.astype(BF16).astype(F32)
        winds.append(jnp.concatenate([high, w - high], axis=1).astype(BF16))

    def spread_winds(h):
        for parts, wide_w in zip(winds, (wxe, wye)):
            for i in range(8):
                spreader = (level == target + 4 * (8 * h + i)).astype(BF16)
                value = jnp.dot(parts, spreader, preferred_element_type=F32)
                wide_w[h, pl.ds(i, NX * NY, stride=8), :] = value

    def turn(h):
        loads[2 + h].wait()

        def body(n, carry):
            x, y8 = n // (NY // 8), lax.rem(n, NY // 8)
            block = raw[x, pl.ds(pl.multiple_of(y8 * 8, 8), 8), 1024 * h:1024 * (h + 1)]
            st[h, x, pl.ds(y8 * 8, 8)] = block.reshape(8, 8, 128)
            return carry

        lax.fori_loop(0, NX * NY // 8, body, 0, unroll=2)

    for h in range(2):
        fin[h, SKIP * 8:LINE * 8, :] = jnp.zeros(((LINE - SKIP) * 8, 128), F32)
        fin[h, COLS * 8:, :] = jnp.zeros(((LINE * 9 + 1 - COLS) * 8, 128), F32)
    spread_winds(0)
    turn(0)
    weighted(0, 0, initial)
    pl.semaphore_wait(barrier, ngy - 1 + ngx - 1 + 4)
    go(0, 0)
    loads[4].wait()

    def pack(s, carry):
        upper_half = lax.broadcasted_iota(jnp.int32, (8, 128), 0) < 4
        for four in range(ngy // 4):
            rows = pl.ds(pl.multiple_of(s * (2 * ngy) + four * 8, 8), 8)
            block = raw_inv[rows, :].reshape(8, 8, 128)
            for q in range(4):
                one, two = block[2 * q], block[2 * q + 1]
                a0[four * 4 + q, pl.ds(pl.multiple_of(s * 8, 8), 8), :] = jnp.where(upper_half, one, pltpu.roll(two, 4, 0))
                b0[s, four * 4 + q] = jnp.where(upper_half, pltpu.roll(one, 4, 0), two)
        return carry

    lax.fori_loop(0, ngx, pack, 0)
    for d in range(1, ngx // 2):
        b_first(d).start()
    b1[gx] = b0[gx]
    spread_winds(1)
    turn(1)
    weighted(1, 0, initial)
    go(1, 0)
    for d in range(ngx // 2, ngx):
        b_first(d).start()
    across = (((1,), (1,)), ((), ()))
    loads[5].wait()
    slot = lax.broadcasted_iota(jnp.int32, (3, 2 * devices), 1)
    rows = jnp.concatenate(
        [jnp.where(lax.rem(slot, 2) == r, raw_coup[...], 0.0) for r in range(2)] + [jnp.zeros((122, 2 * devices), F32)], axis=0)
    owner = lax.broadcasted_iota(jnp.int32, (devices, 2 * devices), 0)
    slot = lax.broadcasted_iota(jnp.int32, (devices, 2 * devices), 1)
    chooser = (slot // 2 == owner).astype(BF16)
    both = sum(lax.dot_general(chooser, part, across, preferred_element_type=F32) for part in two_parts(rows))
    both = both.reshape(ngx, ngy, 128)
    for s in range(ngy):
        a0[s, ngx * 8:, :] = both[:, s, :]

    for d in range(1, ngy):
        a_first(d).start()
    a1[gy] = a0[gy]
    loads[6].wait()
    earlier = (lax.broadcasted_iota(jnp.int32, (COLS, COLS), 1) < lax.broadcasted_iota(jnp.int32, (COLS, COLS), 0)).astype(BF16)
    itself = (lax.broadcasted_iota(jnp.int32, (COLS, COLS), 1) == lax.broadcasted_iota(jnp.int32, (COLS, COLS), 0)).astype(BF16)
    span = lax.broadcasted_iota(jnp.int32, (devices, COLS), 0)
    late = lax.rem(lax.broadcasted_iota(jnp.int32, (128, COLS), 0), 32)
    late = jnp.where(late < LINE, late, (late - LINE + 1) * LINE)
    late = (late == lax.broadcasted_iota(jnp.int32, (128, COLS), 1)).astype(BF16)
    picks, late_picks = [], []
    for order in (span, lax.rem(span, ngx) * ngy + span // ngx):
        named = (raw_span[...] == order).astype(BF16)
        chosen = lax.dot_general(itself, named, across, preferred_element_type=F32)
        count = lax.dot_general(earlier, named, across, preferred_element_type=F32)
        picks.append(jnp.concatenate(
            [jnp.where(count < 0.5, chosen, 0.0), jnp.where(count < 0.5, 0.0, chosen)], axis=1).astype(BF16))
        late_picks.append(jnp.dot(late, picks[-1], preferred_element_type=F32).astype(BF16))

    arrive(0, 0)
    weighted(0, 1, first)
    go(0, 1)
    arrive(1, 0)
    weighted(1, 1, first)
    go(1, 1)
    for d in range(1, ngx):
        b_first(d).wait_recv()
    for d in range(1, ngy):
        b_second(d).start()
    b2r[gy] = b1[:, gy]
    for d in range(1, ngy):
        a_first(d).wait_recv()
    lax.fori_loop(0, ngx, repack, 0)
    row = a1[0, ngx * 8:, :]
    for g in range(1, ngy):
        row = row + pltpu.roll(a1[g, ngx * 8:, :], 16 * g, 1)
    for s in range(ngx):
        a2s[s, ngy * 8:ngy * 8 + 1, :] = row[s:s + 1]
    a2r[gx, :ngy * 8 + 1, :] = a2s[gx, :ngy * 8 + 1, :]
    for d in range(1, ngx):
        a_second(d).start()
    arrive(0, 1)
    weighted(0, 2, second)
    last_low = go(0, 2)
    arrive(1, 1)
    weighted(1, 2, second)
    last_high = go(1, 2)
    last = [last_low, last_high]
    def solve(h, count, blocks, values, solved):
        def body(n, carry):
            blk, four = 2 * h + n // 4, lax.rem(n, 4)
            rows = blocks[pl.ds(pl.multiple_of(blk * 256 + four * 64, 8), 64), :]
            for tt in range(count):
                v = [values[pl.ds(pl.multiple_of(((blk * 16 + b) * count + tt) * 8, 8), 8), :] for b in range(16)]
                for a in range(4):
                    total = None
                    for b in range(16):
                        term = rows[a * 16 + b:a * 16 + b + 1, :] * v[b]
                        total = term if total is None else total + term
                    solved[pl.ds(pl.multiple_of(((blk * 16 + four * 4 + a) * count + tt) * 8, 8), 8), :] = total
            return carry

        lax.fori_loop(0, 8, body, 0, unroll=8 // count if count < 4 else 1)

    def sweep(tt, count, blocks, strengths, solved):
        def level(blk, a):
            return pl.ds(pl.multiple_of(((blk * 16 + a) * count + tt) * 8, 8), 8)

        def entry(blk, a, b):
            return blocks[blk * 256 + a * 16 + b:blk * 256 + a * 16 + b + 1, :]

        head = [solved[level(b, 0), :] for b in range(NB)]
        tail = [solved[level(b, 15), :] for b in range(NB)]
        strength = [strengths[b:b + 1, :] for b in range(NB - 1)]
        now_head, now_tail = head, tail
        for n in range(SWEEPS):
            upper = [strength[b] * now_head[b + 1] for b in range(NB - 1)] + [None]
            lower = [None] + [strength[b] * now_tail[b] for b in range(NB - 1)]
            if n < SWEEPS - 1:
                now_head, now_tail = list(head), list(tail)
                for b in range(NB):
                    for a, now in ((0, now_head), (15, now_tail)):
                        if upper[b] is not None:
                            now[b] = now[b] + entry(b, a, 15) * upper[b]
                        if lower[b] is not None:
                            now[b] = now[b] + entry(b, a, 0) * lower[b]
        for b in range(NB):
            for a in range(16):
                value = solved[level(b, a), :]
                if upper[b] is not None:
                    value = value + entry(b, a, 15) * upper[b]
                if lower[b] is not None:
                    value = value + entry(b, a, 0) * lower[b]
                solved[level(b, a), :] = value

    quarter = lax.broadcasted_iota(jnp.int32, (8, 128), 1) // 32

    def lay_many(h):
        for s in range(8):
            vt[(8 * h + s) * 128:(8 * h + s + 1) * 128, :] = fin[h, pl.ds(SKIP * 8 + s, 128, stride=8), :].T

    def lay_few(h):
        for s in range(8):
            four = jnp.concatenate([fin[h, pl.ds(s, LINE, stride=8), :], fin[h, pl.ds(LINE * 8 + s, 8, stride=LINE * 8), :]] * 4, axis=0).T
            for g in range(4):
                value = four[g * 32:g * 32 + 8]
                for q in range(1, 4):
                    value = jnp.where(quarter == q, four[g * 32 + q * 8:g * 32 + q * 8 + 8], value)
                vp[((8 * h + s) * 4 + g) * 8:((8 * h + s) * 4 + g + 1) * 8, :] = value

    def take_many(s):
        turned = xt[s * 128:(s + 1) * 128, :].T
        out[LINE:, s * 128:(s + 1) * 128] = turned[LINE - SKIP:]

    eighth = lax.rem(lax.broadcasted_iota(jnp.int32, (32, 128), 1) // 8, 4)

    def take_few(s):
        turned = jnp.concatenate([xp[(s * 4 + g) * 8:(s * 4 + g + 1) * 8, :] for g in range(4) for q in range(4)], axis=0).T
        value = turned[:32]
        for q in range(1, 4):
            value = jnp.where(eighth == q, turned[q * 32:q * 32 + 32], value)
        out[:LINE, s * 128:(s + 1) * 128] = value[:LINE]
        for n in range(1, UX - 1):
            out[n * LINE:n * LINE + 1, s * 128:(s + 1) * 128] = value[LINE + n - 1:LINE + n]

    def sweep_many(tt, carry):
        sweep(tt, 4, bt, kt, xt)
        return carry

    for d in range(1, ngy):
        b_second(d).wait_recv()
    gather(1, [
        jnp.concatenate([b2r[g, pl.ds(0, ngx), r * 4 + j, :] for r in range(2) for g in range(ngy)], axis=0)
        for j in range(4)])
    for h in range(2):
        final(h, range(1, UX - 1))
        lay_many(h)
    solve(1, 4, bt, vt, xt)
    for d in range(1, ngx):
        a_second(d).wait_recv()
    gather(0, [
        jnp.concatenate([a2r[g, pl.ds(r * 4 + j, ngy, stride=8), :] for r in range(2) for g in range(ngx)], axis=0)
        for j in range(4)])

    row = a2r[:, ngy * 8, :]
    links = two_parts(jnp.concatenate(
        [pltpu.roll(row, (128 - 16 * g - 3 * r) % 128, 1) for r in range(2) for g in range(ngy)], axis=0))
    kt[...] = sum(jnp.dot(picks[1][SKIP:], part, preferred_element_type=F32) for part in links).T
    kp[...] = sum(jnp.dot(late_picks[1], part, preferred_element_type=F32) for part in links).T

    solve(0, 4, bt, vt, xt)
    lax.fori_loop(0, 4, sweep_many, 0)
    for s in range(16):
        take_many(s)
    for d in range(1, ngy):
        a_first(d).wait_send()
        b_second(d).wait_send()
    for d in range(1, ngx):
        a_second(d).wait_send()
        b_first(d).wait_send()
    for k in range(2):
        for h in range(2):
            for move in halo(h, k):
                move.wait_send()
    for h in range(2):
        for move in last[h][:2]:
            move.wait_recv()
        grid[0, h, 0:UX - 1, 0] += ry[2, h, 0, 0:UX - 1]
        grid[0, h, 0, 0] += rc[2, h, 0]
        for X in range(1, UX - 1):
            fin[h, X * LINE * 8:X * LINE * 8 + 8, :] = third(h, X + X // 3, 0, 0)
    for h in range(2):
        last[h][2].wait_recv()
        grid[0, h, 0, 0:UY - 1] += rx[2, h, 0, 0:UY - 1]
        final(h, range(1))
        lay_few(h)
        solve(h, 1, bp, vp, xp)
    sweep(0, 1, bp, kp, xp)
    for s in range(16):
        take_few(s)

    for moves in last:
        for move in moves:
            move.wait_send()


def on_device(ngx, ngy, state, wind_x, wind_y, mass, inv_mass, span_of, block_inverse, coupling):
    width = state.shape[2]
    any_ = pl.BlockSpec(memory_space=pl.ANY)
    nodes = (2, NX, NY, 8, 128)
    vmem = pltpu.VMEM
    dma = pltpu.SemaphoreType.DMA
    span_of, coupling = span_of.T, coupling.T
    return pl.pallas_call(
        functools.partial(kernel, ngx, ngy),
        out_shape=pltpu.VMEM((COLS, width), F32),
        in_specs=[any_] * 8,
        out_specs=pl.BlockSpec(memory_space=pltpu.VMEM),
        scratch_shapes=[
            pltpu.SMEM(mass.shape, F32), pltpu.SMEM(inv_mass.shape, F32),
            vmem(state.shape, F32), vmem(wind_x.shape, F32), vmem(wind_y.shape, F32), vmem(span_of.shape, jnp.int32),
            vmem(block_inverse.shape, F32), vmem(coupling.shape, F32),
            vmem(nodes, F32), vmem(nodes, F32),
            vmem((2, (NX * NY + 1) * 8, 128), F32), vmem((2, (NX * NY + 1) * 8, 128), F32),
            vmem((2, 2, UX, UY, 8, 128), F32),
            vmem((3, 2, 2, UY, 8, 128), F32), vmem((3, 2, 2, UX, 8, 128), F32),
            vmem((3, 2, 2, UY, 8, 128), F32), vmem((3, 2, 2, UX, 8, 128), F32), vmem((3, 2, 4, 8, 128), F32),
            vmem((2, (LINE * 9 + 1) * 8, 128), F32),
            vmem((ngy, ngx * 9, 128), F32), vmem((ngy, ngx * 9, 128), F32),
            vmem((ngx, ngy * 9, 128), F32), vmem((ngx, ngy * 9, 128), F32),
            vmem((ngx, ngy, 8, 128), F32), vmem((ngx, ngy, 8, 128), F32), vmem((ngy, ngx, 8, 128), F32),
            vmem((128, 128), F32), vmem((1024, 128), F32), vmem((2048, 128), F32), vmem((2048, 128), F32),
            vmem((128, 128), F32), vmem((1024, 128), F32), vmem((512, 128), F32), vmem((512, 128), F32),
            dma((9,)), dma((3, 2, 8)), dma((3, 2, 8)),
            dma((ngy,)), dma((ngy,)), dma((ngx,)), dma((ngx,)),
            dma((ngx,)), dma((ngx,)), dma((ngy,)), dma((ngy,)),
        ],
        compiler_params=pltpu.CompilerParams(
            collective_id=0, has_side_effects=True, vmem_limit_bytes=60 * 2**20),
    )(state, wind_x, wind_y, mass, inv_mass, span_of, block_inverse, coupling)


def solution(mesh):
    placed = (
        P("gx", "gy", None),
        P("gx", "gy", None),
        P("gx", "gy", None),
        P("gx", "gy"),
        P("gx", "gy"),
        P(("gx", "gy"), None),
        P(("gx", "gy"), None),
        P(("gx", "gy"), None),
    )
    return jax.shard_map(
        functools.partial(on_device, mesh.shape["gx"], mesh.shape["gy"]),
        mesh=mesh, in_specs=placed, out_specs=P(("gx", "gy"), None), check_vma=False,
    )
```
